32 devices in a mesh: fsdp: 8 (over z, y), ctx: 2 (over x), tp: 2 (over core).
Axes of the slice: x: 2, y: 2, z: 4, core: 2. Of those that a mesh axis runs over, the one named last changes fastest.
Arguments:
- inputs: bfloat16 [32, 580, 1024], P('fsdp', 'ctx'), may hold values from -6 to 6
- cotangent: bfloat16 [32, 580, 1024], P('fsdp', 'ctx'), may hold values from -9 to 9
- key_mask: int32 [32, 580], P('fsdp', 'ctx'), may hold values from 0 to 1, as said below
- image_mask: int32 [32], P('fsdp'), may hold values 0 or 1
- qkv_weight: float32 [1024, 3, 1024], P('fsdp', None, 'tp'), may hold values from -0.1875 to 0.1875
- out_weight: float32 [1024, 1024], P('tp', 'fsdp'), may hold values from -2.5 to 2.5
- up_weight: float32 [1024, 4096], P('fsdp', 'tp'), may hold values from -0.1875 to 0.1875
- down_weight: float32 [4096, 1024], P('tp', 'fsdp'), may hold values from -1 to 1
- vectors: float32 [12, 1024], replicated, may hold values from -2 to 2
- row_qkv: float32 [1024], P('fsdp'), may hold values from 4640 to 18560
- col_qkv: float32 [3, 1024], P(None, 'tp'), may hold values from 4640 to 18560
- row_out: float32 [1024], P('tp'), may hold values from 257 to 1030
- col_out: float32 [1024], P('fsdp'), may hold values from 257 to 1030
- row_up: float32 [1024], P('fsdp'), may hold values from 3093 to 12373
- col_up: float32 [4096], P('tp'), may hold values from 3093 to 12373
- row_down: float32 [4096], P('tp'), may hold values from 12992 to 55680
- col_down: float32 [1024], P('fsdp'), may hold values from 12992 to 55680
- vector_moments: float32 [12, 1024], replicated, may hold values from 3712 to 37120
Outputs:
- output: bfloat16 [32, 580, 1024], P('fsdp', 'ctx')
- input_grad: bfloat16 [32, 580, 1024], P('fsdp', 'ctx')
- qkv_grad: float32 [1024, 3, 1024], P('fsdp', None, 'tp')
- out_grad: float32 [1024, 1024], P('tp', 'fsdp')
- up_grad: float32 [1024, 4096], P('fsdp', 'tp')
- down_grad: float32 [4096, 1024], P('tp', 'fsdp')
- vector_grad: float32 [12, 1024], replicated
- qkv_new: float32 [1024, 3, 1024], P('fsdp', None, 'tp')
- out_new: float32 [1024, 1024], P('tp', 'fsdp')
- up_new: float32 [1024, 4096], P('fsdp', 'tp')
- down_new: float32 [4096, 1024], P('tp', 'fsdp')
- vector_new: float32 [12, 1024], replicated
- qkv_copy: bfloat16 [1024, 3, 1024], P('fsdp', None, 'tp')
- out_copy: bfloat16 [1024, 1024], P('tp', 'fsdp')
- up_copy: bfloat16 [1024, 4096], P('fsdp', 'tp')
- down_copy: bfloat16 [4096, 1024], P('tp', 'fsdp')
- qkv_rows: float32 [1024], P('fsdp')
- qkv_cols: float32 [3, 1024], P(None, 'tp')
- out_rows: float32 [1024], P('tp')
- out_cols: float32 [1024], P('fsdp')
- up_rows: float32 [1024], P('fsdp')
- up_cols: float32 [4096], P('tp')
- down_rows: float32 [4096], P('tp')
- down_cols: float32 [1024], P('fsdp')
- vector_moment: float32 [12, 1024], replicated
The draws below stay inside these ranges and needn't reach their ends.
Inputs may be any that keep to these rules, and one draw needn't show every extreme that they name: `key_mask`: each image's real slots are its first ones, at least 577 of them.
All inputs are finite; a program needn't handle non-finite values. No bound on the sum of `image_mask` on one device may be relied on, other than what follows from the above.
Results may differ from the reference program's by a relative error of at most 0.017.
Values may be sent and summed in bfloat16 or wider, within the bound.
A program may use at most 256 MiB of HBM per device.

```python
import math
import jax
import jax.numpy as jnp
from jax import lax

D = 1024
H = 16
HD = 64
FF = 4096
SEQ = 580
IMG_DEV = 4
IMAGES = 32
VROWS = 12


def rising(length, ratio):
    return jnp.exp(jnp.linspace(0.0, 1.0, length) * jnp.log(ratio))


def draw_cotangent(key, part):
    key = jax.random.fold_in(key, 3)
    base_draw = jnp.clip(jax.random.normal(key, (IMAGES, SEQ, D)), -5.0, 5.0)
    rise_row = rising(D, 3.0 ** 0.5)
    return (base_draw * rise_row).astype(jnp.bfloat16)


def draw_vectors(key, part):
    key = jax.random.fold_in(key, 5)
    key_one, key_two = jax.random.split(key)
    row_count = 8 + FF // D
    base_draw = 0.4 * jnp.clip(jax.random.normal(key_one, (row_count, D)), -5.0, 5.0)
    rise_row = rising(D, 3.0 ** 0.5)
    gain_rows = 0.7 * rise_row * jax.random.uniform(key_two, (2, D), minval=0.8, maxval=1.25)
    base_draw = base_draw.at[0].set(gain_rows[0]).at[5].set(gain_rows[1])
    return base_draw.astype(jnp.float32)


def draw_out_weight(key, part):
    key = jax.random.fold_in(key, 7)
    base_draw = jnp.clip(jax.random.normal(key, (D, D)), -5.0, 5.0)
    return (base_draw * (8.0 / D) ** 0.5 * rising(D, 3.0 ** 0.5)[:, None]).astype(jnp.float32)


def draw_down_weight(key, part):
    key = jax.random.fold_in(key, 8)
    base_draw = jnp.clip(jax.random.normal(key, (FF, D)), -5.0, 5.0)
    return (base_draw * FF ** (-0.5) * rising(FF, 3.0 ** 0.5)[:, None]).astype(jnp.float32)


def draw_key_mask(key, part):
    key = jax.random.fold_in(key, 9)
    lengths = SEQ - jax.random.randint(key, (IMAGES, 1), 0, 4)
    return (jnp.arange(SEQ, dtype=jnp.int32)[None, :] < lengths).astype(jnp.int32)


def touch_ends(values, own_key, smallest, high):
    spot = [jax.random.randint(jax.random.fold_in(own_key, axis), (), 0, length) for axis, length in enumerate(values.shape)]
    longest = values.shape.index(max(values.shape))
    beside = spot[:longest] + [(spot[longest] + 1) % values.shape[longest]] + spot[longest + 1:]
    return values.at[tuple(spot)].set(smallest).at[tuple(beside)].set(high)


def shard_levels(stream_key, shape, cuts, low, largest):
    factor_of = 1.0
    for dim, parts in cuts:
        steps = jax.random.uniform(jax.random.fold_in(jax.random.fold_in(stream_key, 6), dim), (parts,), jnp.float32, low / len(cuts), largest / len(cuts))
        factor_of = factor_of * jnp.repeat(jnp.exp(steps), shape[dim] // parts).reshape((-1,) + (1,) * (len(shape) - 1 - dim))
    return factor_of


def scatter_about(stream_key, extent, spread, reach, cuts=(), held_as=jnp.bfloat16):
    drawn = spread * jax.random.normal(stream_key, extent, jnp.float32)
    if cuts:
        drawn = drawn * shard_levels(stream_key, extent, cuts, -0.22, 0.18)
    return jnp.clip(drawn, -reach, reach).astype(held_as)


def setup_inputs(seed: int = 0) -> dict:
    seeds = jax.random.split(jax.random.key(seed), 19)
    return {
        "inputs": scatter_about(seeds[0], (IMAGES, SEQ, D), 1.0, 6.0, ((0, 8), (1, 2))),
        "cotangent": draw_cotangent(jax.random.fold_in(seeds[18], 71), 0),
        "key_mask": draw_key_mask(jax.random.fold_in(seeds[18], 71), 0),
        "image_mask": touch_ends((jax.random.randint(seeds[3], (IMAGES,), 0, 8) < 7).astype(jnp.int32), jax.random.fold_in(seeds[3], 1), 0, 1),
        "qkv_weight": scatter_about(seeds[4], (D, 3, D), D ** -0.5, 0.1875, ((0, 8), (2, 2)), jnp.float32),
        "out_weight": draw_out_weight(jax.random.fold_in(seeds[18], 71), 0),
        "up_weight": scatter_about(seeds[6], (D, FF), D ** -0.5, 0.1875, ((0, 8), (1, 2)), jnp.float32),
        "down_weight": draw_down_weight(jax.random.fold_in(seeds[18], 71), 0),
        "vectors": draw_vectors(jax.random.fold_in(seeds[18], 71), 0),
        "row_qkv": jnp.clip(jnp.exp(math.log(18560.0) - 1.3862944 * jax.random.uniform(seeds[9], (D,), jnp.float32) ** shard_levels(seeds[9], (D,), ((0, 8),), -0.2, 0.2)), 4640.0, 18560.0),
        "col_qkv": jnp.clip(jnp.exp(math.log(18560.0) - 1.3862944 * jax.random.uniform(seeds[10], (3, D), jnp.float32) ** shard_levels(seeds[10], (3, D), ((1, 2),), -0.2, 0.2)), 4640.0, 18560.0),
        "row_out": jnp.clip(jnp.exp(math.log(1030.0) - 1.388238 * jax.random.uniform(seeds[11], (D,), jnp.float32) ** shard_levels(seeds[11], (D,), ((0, 2),), -0.2, 0.2)), 257.0, 1030.0),
        "col_out": jnp.clip(jnp.exp(math.log(1030.0) - 1.388238 * jax.random.uniform(seeds[12], (D,), jnp.float32) ** shard_levels(seeds[12], (D,), ((0, 8),), -0.2, 0.2)), 257.0, 1030.0),
        "row_up": jnp.clip(jnp.exp(math.log(12373.0) - 1.3863752 * jax.random.uniform(seeds[13], (D,), jnp.float32) ** shard_levels(seeds[13], (D,), ((0, 8),), -0.2, 0.2)), 3093.0, 12373.0),
        "col_up": jnp.clip(jnp.exp(math.log(12373.0) - 1.3863752 * jax.random.uniform(seeds[14], (FF,), jnp.float32) ** shard_levels(seeds[14], (FF,), ((0, 2),), -0.2, 0.2)), 3093.0, 12373.0),
        "row_down": jnp.clip(jnp.exp(math.log(55680.0) - 1.4552872 * jax.random.uniform(seeds[15], (FF,), jnp.float32) ** shard_levels(seeds[15], (FF,), ((0, 2),), -0.2, 0.2)), 12992.0, 55680.0),
        "col_down": jnp.clip(jnp.exp(math.log(55680.0) - 1.4552872 * jax.random.uniform(seeds[16], (D,), jnp.float32) ** shard_levels(seeds[16], (D,), ((0, 8),), -0.2, 0.2)), 12992.0, 55680.0),
        "vector_moments": jnp.clip(jnp.exp(jax.random.uniform(seeds[17], (VROWS, D), jnp.float32, math.log(3712.0), math.log(37120.0))), 3712.0, 37120.0),
    }


@jax.custom_vjp
def low(v):
    return lax.optimization_barrier(v.astype(jnp.bfloat16)).astype(jnp.float32)

@jax.custom_vjp
def low_back(v):
    return v

def low_keep(v):
    return (low(v), None)

def low_pass(kept, grad):
    return (grad,)

def back_keep(v):
    return (v, None)

def back_low(kept, grad):
    return (low(grad),)
low.defvjp(low_keep, low_pass)
low_back.defvjp(back_keep, back_low)
eps_norm = 1e-06
decay_rate = 0.5
clip_level = 0.1
step_rate = 5.0
highest = lax.Precision.HIGHEST

def norm_rows(rows, scale_row, offset):
    row_mean = lax.optimization_barrier(jnp.mean(rows, -1, keepdims=True))
    centered = rows - row_mean
    inverse = lax.rsqrt(lax.optimization_barrier(jnp.mean(centered * centered, -1, keepdims=True)) + eps_norm)
    return centered * inverse * scale_row + offset

def gelu_erf(argument):
    return 0.5 * argument * (1.0 + lax.erf(argument * 0.7071067811865476))

def attend_one(pieces):
    queries, key_rows, value_rows, valid_keys = pieces
    scores = jnp.einsum('qhe,khe->hqk', queries, key_rows, precision=highest) * HD ** (-0.5)
    scores = low_back(scores)
    scores = jnp.where(valid_keys[None, None, :] > 0, scores, -1000000000.0)
    attention = low(jax.nn.softmax(scores, axis=-1))
    return jnp.einsum('hqk,khe->qhe', attention, value_rows, precision=highest)

def layer_forward(rows_in, mix_weight, out_weight, up_weight, down_weight, vectors, valid_keys):
    images = rows_in.shape[0]
    flat_rows = rows_in.reshape(images * SEQ, D)
    mix_low = low(mix_weight)
    out_low = low(out_weight)
    up_low = low(up_weight)
    down_low = low(down_weight)
    normed = low(norm_rows(flat_rows, vectors[0], vectors[1]))
    projected = jnp.einsum('td,dcn->tcn', normed, mix_low, precision=highest)
    projected = projected + jnp.stack([vectors[2], jnp.zeros_like(vectors[2]), vectors[3]])[None]
    queries = low_back(low(projected[:, 0])).reshape(images, SEQ, H, HD)
    key_rows = low_back(low(projected[:, 1])).reshape(images, SEQ, H, HD)
    value_rows = low_back(low(projected[:, 2])).reshape(images, SEQ, H, HD)
    attended = lax.map(jax.checkpoint(attend_one), (queries, key_rows, value_rows, valid_keys))
    heads_low = low_back(low(attended.reshape(images * SEQ, D)))
    branch = jnp.dot(heads_low, out_low, precision=highest) + vectors[4]
    hidden = flat_rows + low_back(branch)
    second = low(norm_rows(hidden, vectors[5], vectors[6]))
    pre_active = jnp.dot(second, up_low, precision=highest) + vectors[8:].reshape(FF)
    active = low(gelu_erf(low_back(pre_active)))
    output = hidden + jnp.dot(active, down_low, precision=highest) + vectors[7]
    return output.reshape(images, SEQ, D)

def factor_step(grad, rows_old, cols_old):
    flat_grad = grad.reshape(grad.shape[0], -1)
    square = flat_grad * flat_grad
    rows_new = decay_rate * rows_old + (1.0 - decay_rate) * lax.optimization_barrier(jnp.mean(square, 1))
    cols_new = decay_rate * cols_old.reshape(-1) + (1.0 - decay_rate) * lax.optimization_barrier(jnp.mean(square, 0))
    estimate = rows_new[:, None] * cols_new[None, :] / jnp.mean(rows_new)
    update = flat_grad * lax.rsqrt(estimate)
    return (rows_new, cols_new.reshape(cols_old.shape), update.reshape(grad.shape))

def reference(inputs, cotangent, key_mask, image_mask, qkv_weight, out_weight, up_weight, down_weight, vectors, row_qkv, col_qkv, row_out, col_out, row_up, col_up, row_down, col_down, vector_moments):
    groups = IMAGES // IMG_DEV

    def grouped(array):
        return array.reshape((groups, IMG_DEV) + array.shape[1:])
    params = (qkv_weight, out_weight, up_weight, down_weight, vectors)

    def group_step(totals, pieces):
        rows_in, back_in, valid_keys, valid_images = pieces
        weight_rows = valid_keys.astype(jnp.float32) * valid_images.astype(jnp.float32)[:, None]
        back = back_in.astype(jnp.float32) * weight_rows[:, :, None]

        def run_layer(rows_f, mix_w, out_w, up_w, down_w, vector_w):
            return layer_forward(rows_f, mix_w, out_w, up_w, down_w, vector_w, valid_keys)
        result, pullback = jax.vjp(run_layer, rows_in.astype(jnp.float32), qkv_weight, out_weight, up_weight, down_weight, vectors)
        gradients = pullback(back)
        totals = tuple((total_one + grad_one for total_one, grad_one in zip(totals, gradients[1:])))
        return (totals, (result.astype(jnp.bfloat16), gradients[0].astype(jnp.bfloat16)))
    zeros_init = tuple((jnp.zeros_like(param) for param in params))
    sums, (results, input_grads) = lax.scan(group_step, zeros_init, (grouped(inputs), grouped(cotangent), grouped(key_mask), grouped(image_mask)))
    qkv_grad, out_grad, up_grad, down_grad, vector_grad = sums
    output = results.reshape(IMAGES, SEQ, D)
    input_grad = input_grads.reshape(IMAGES, SEQ, D)
    qkv_rows, qkv_cols, qkv_step = factor_step(qkv_grad, row_qkv, col_qkv)
    out_rows, out_cols, out_step = factor_step(out_grad, row_out, col_out)
    up_rows, up_cols, up_step = factor_step(up_grad, row_up, col_up)
    down_rows, down_cols, down_step = factor_step(down_grad, row_down, col_down)
    vector_moment = decay_rate * vector_moments + (1.0 - decay_rate) * vector_grad * vector_grad
    vector_step = vector_grad * lax.rsqrt(vector_moment)
    steps = (qkv_step, out_step, up_step, down_step, vector_step)
    total_square = jnp.float32(0.0)
    param_count = 0
    for step_one in steps:
        total_square = total_square + jnp.sum(step_one * step_one)
        param_count = param_count + step_one.size
    shrink = 1.0 / jnp.maximum(1.0, jnp.sqrt(total_square / param_count) / clip_level)
    news = tuple((param - step_rate * jnp.sqrt(jnp.mean(param * param)) * step_one * shrink for param, step_one in zip(params, steps)))
    qkv_new, out_new, up_new, down_new, vector_new = news
    return (output, input_grad, qkv_grad, out_grad, up_grad, down_grad, vector_grad, qkv_new, out_new, up_new, down_new, vector_new, qkv_new.astype(jnp.bfloat16), out_new.astype(jnp.bfloat16), up_new.astype(jnp.bfloat16), down_new.astype(jnp.bfloat16), qkv_rows, qkv_cols, out_rows, out_cols, up_rows, up_cols, down_rows, down_cols, vector_moment)
```

```python
import jax
import jax.numpy as jnp
from jax import lax
from jax.experimental import pallas as pl
from jax.experimental.pallas import tpu as pltpu
from jax.sharding import PartitionSpec as P

HD = 64
FF = 4096


eps_norm = 1e-06
decay_rate = 0.5
clip_level = 0.1
step_rate = 5.0


def norm_rows(rows, scale_row, offset):
    row_mean = jnp.mean(rows, -1, keepdims=True)
    centered = rows - row_mean
    inverse = lax.rsqrt(jnp.mean(centered * centered, -1, keepdims=True) + eps_norm)
    normal = centered * inverse
    return (normal * scale_row + offset, normal, inverse)


def norm_back(grad_rows, normal, inverse, scale_row):
    scaled = grad_rows * scale_row
    first_term = jnp.mean(scaled, -1, keepdims=True)
    second_term = jnp.mean(scaled * normal, -1, keepdims=True)
    return inverse * (scaled - first_term - normal * second_term)


def gelu_erf(argument):
    return 0.5 * argument * (1.0 + lax.erf(argument * 0.7071067811865476))


def gelu_slope(argument):
    return (
        0.5 * (1.0 + lax.erf(argument * 0.7071067811865476))
        + argument * jnp.exp(-0.5 * argument * argument) * 0.3989422804014327
    )


def masked_scores(queries, key_rows, valid_keys):
    scale_qk = queries.shape[-1] ** (-0.5)
    scores = (
        jnp.einsum("gqhe,gkhe->ghqk", queries, key_rows, preferred_element_type=jnp.float32)
        * scale_qk
    )
    return jnp.where(valid_keys[:, None, None, :] > 0, scores, -1000000000.0)


def attend_forward(pieces):
    queries, key_rows, value_rows, valid_keys = pieces
    scores = masked_scores(queries, key_rows, valid_keys)
    row_max = jnp.max(scores, -1, keepdims=True)
    exponent = jnp.exp(scores - row_max)
    totals = jnp.sum(exponent, -1, keepdims=True)
    attention = (exponent / totals).astype(jnp.bfloat16)
    attended = jnp.einsum(
        "ghqk,gkhe->gqhe", attention, value_rows, preferred_element_type=jnp.float32
    )
    return (attended.astype(jnp.bfloat16), (row_max + jnp.log(totals))[..., 0])


def attend_back(pieces):
    queries, key_rows, value_rows, valid_keys, logsum, grad_heads = pieces
    scale_qk = queries.shape[-1] ** (-0.5)
    scores = masked_scores(queries, key_rows, valid_keys)
    attention = jnp.exp(scores - logsum[..., None])
    grad_attention = jnp.einsum(
        "gqhe,gkhe->ghqk", grad_heads, value_rows, preferred_element_type=jnp.float32
    )
    inner = jnp.sum(attention * grad_attention, -1, keepdims=True)
    grad_scores = (attention * (grad_attention - inner)).astype(jnp.bfloat16)
    grad_queries = (
        jnp.einsum("ghqk,gkhe->gqhe", grad_scores, key_rows, preferred_element_type=jnp.float32)
        * scale_qk
    ).astype(jnp.bfloat16)
    grad_keys = (
        jnp.einsum("ghqk,gqhe->gkhe", grad_scores, queries, preferred_element_type=jnp.float32)
        * scale_qk
    )
    grad_values = jnp.einsum(
        "ghqk,gqhe->gkhe",
        attention.astype(jnp.bfloat16),
        grad_heads,
        preferred_element_type=jnp.float32,
    )
    return (grad_queries, grad_keys, grad_values)


def place_at(piece, full_shape, start, axis):
    return lax.dynamic_update_slice_in_dim(jnp.zeros(full_shape, jnp.float32), piece, start, axis)


def factor_local(
    grad_local, rows_old, cols_old, rows_full, rows_here, cols_here, row_total, col_total, old_total
):
    rows_new = decay_rate * rows_old + (1.0 - decay_rate) * rows_here / col_total
    cols_new = decay_rate * cols_old + (1.0 - decay_rate) * cols_here / row_total
    rows_avg = decay_rate * old_total / row_total + (1.0 - decay_rate) * jnp.sum(rows_full) / (
        row_total * col_total
    )
    update = grad_local * lax.rsqrt(rows_new[:, None] * cols_new[None, :] / rows_avg)
    return (rows_new, cols_new, update)


def body(
    inputs,
    cotangent,
    key_mask,
    image_mask,
    qkv_weight,
    out_weight,
    up_weight,
    down_weight,
    vectors,
    row_qkv,
    col_qkv,
    row_out,
    col_out,
    row_up,
    col_up,
    row_down,
    col_down,
    vector_moments,
):
    images, local_tokens, model_width = inputs.shape
    rows_here = images * local_tokens
    width_piece = qkv_weight.shape[0]
    half_width = qkv_weight.shape[2]
    half_hidden = up_weight.shape[1]
    head_size = HD
    heads_here = half_width // head_size
    tp_index = lax.axis_index("tp")
    fsdp_index = lax.axis_index("fsdp")
    tp_first = (tp_index == 0).astype(jnp.float32)
    ctx_first = (lax.axis_index("ctx") == 0).astype(jnp.float32)
    fsdp_first = (fsdp_index == 0).astype(jnp.float32)
    mix_w, out_w, up_w, down_w = (
        lax.all_gather(qkv_weight.astype(jnp.bfloat16), "fsdp", axis=0, tiled=True),
        lax.all_gather(out_weight.astype(jnp.bfloat16), "fsdp", axis=1, tiled=True),
        lax.all_gather(up_weight.astype(jnp.bfloat16), "fsdp", axis=0, tiled=True),
        lax.all_gather(down_weight.astype(jnp.bfloat16), "fsdp", axis=1, tiled=True),
    )
    query_bias = lax.dynamic_slice_in_dim(vectors[2], tp_index * half_width, half_width)
    value_bias = lax.dynamic_slice_in_dim(vectors[3], tp_index * half_width, half_width)
    up_bias = lax.dynamic_slice_in_dim(vectors[8:].reshape(-1), tp_index * half_hidden, half_hidden)
    flat_rows = inputs.astype(jnp.float32).reshape(rows_here, model_width)
    normed, normal_one, inverse_one = norm_rows(flat_rows, vectors[0], vectors[1])
    normed_low = normed.astype(jnp.bfloat16)
    projected = jnp.einsum("td,dcn->tcn", normed_low, mix_w, preferred_element_type=jnp.float32)
    queries = (projected[:, 0] + query_bias).astype(jnp.bfloat16)
    key_low = projected[:, 1].astype(jnp.bfloat16).reshape(images, local_tokens, half_width)
    value_low = (
        (projected[:, 2] + value_bias)
        .astype(jnp.bfloat16)
        .reshape(images, local_tokens, half_width)
    )
    all_keys, all_values, all_valid = (
        lax.all_gather(key_low, "ctx", axis=1, tiled=True),
        lax.all_gather(value_low, "ctx", axis=1, tiled=True),
        lax.all_gather(key_mask.astype(jnp.bfloat16), "ctx", axis=1, tiled=True),
    )
    seq_all = all_keys.shape[1]
    group_size = min(2, images)
    groups = images // group_size

    def grouped(array):
        return array.reshape((groups, group_size) + array.shape[1:])

    query_heads = grouped(queries.reshape(images, local_tokens, heads_here, head_size))
    key_heads = grouped(all_keys.reshape(images, seq_all, heads_here, head_size))
    value_heads = grouped(all_values.reshape(images, seq_all, heads_here, head_size))
    valid_groups = grouped(all_valid)
    attended, logsum = lax.map(attend_forward, (query_heads, key_heads, value_heads, valid_groups))
    heads_low = attended.reshape(rows_here, half_width)
    branch = (
        lax.psum(
            jnp.dot(heads_low, out_w, preferred_element_type=jnp.float32).astype(jnp.bfloat16), "tp"
        ).astype(jnp.float32)
        + vectors[4]
    )
    hidden = flat_rows + branch
    second, normal_two, inverse_two = norm_rows(hidden, vectors[5], vectors[6])
    second_low = second.astype(jnp.bfloat16)
    pre_active = jnp.dot(second_low, up_w, preferred_element_type=jnp.float32) + up_bias
    active_low = gelu_erf(pre_active).astype(jnp.bfloat16)
    mlp_sum = lax.psum(
        jnp.dot(active_low, down_w, preferred_element_type=jnp.float32).astype(jnp.bfloat16), "tp"
    ).astype(jnp.float32)
    output = (
        (hidden + mlp_sum + vectors[7])
        .astype(jnp.bfloat16)
        .reshape(images, local_tokens, model_width)
    )
    weight_rows = key_mask.astype(jnp.float32) * image_mask.astype(jnp.float32)[:, None]
    back = (cotangent.astype(jnp.float32) * weight_rows[:, :, None]).reshape(rows_here, model_width)
    back_low = back.astype(jnp.bfloat16)
    grad_active = jnp.einsum("td,fd->tf", back_low, down_w, preferred_element_type=jnp.float32)
    grad_pre = (grad_active * gelu_slope(pre_active)).astype(jnp.bfloat16)
    grad_down = jnp.einsum("tf,td->fd", active_low, back_low, preferred_element_type=jnp.float32)
    grad_up = jnp.einsum("td,tf->df", second_low, grad_pre, preferred_element_type=jnp.float32)
    grad_up_bias = jnp.sum(grad_pre.astype(jnp.float32), 0)
    grad_second = lax.psum(
        jnp.einsum("tf,df->td", grad_pre, up_w, preferred_element_type=jnp.float32).astype(
            jnp.bfloat16
        ),
        "tp",
    ).astype(jnp.float32)
    grad_hidden = back + norm_back(grad_second, normal_two, inverse_two, vectors[5])
    grad_branch = grad_hidden.astype(jnp.bfloat16)
    grad_out = jnp.einsum("tn,td->nd", heads_low, grad_branch, preferred_element_type=jnp.float32)
    grad_heads = jnp.einsum(
        "td,nd->tn", grad_branch, out_w, preferred_element_type=jnp.float32
    ).astype(jnp.bfloat16)
    grad_head_groups = grouped(grad_heads.reshape(images, local_tokens, heads_here, head_size))
    grad_queries, grad_keys, grad_values = lax.map(
        attend_back, (query_heads, key_heads, value_heads, valid_groups, logsum, grad_head_groups)
    )
    key_grads, value_grads = (
        lax.psum_scatter(
            grad_keys.reshape(images, seq_all, half_width).astype(jnp.bfloat16),
            "ctx",
            scatter_dimension=1,
            tiled=True,
        ).astype(jnp.float32),
        lax.psum_scatter(
            grad_values.reshape(images, seq_all, half_width).astype(jnp.bfloat16),
            "ctx",
            scatter_dimension=1,
            tiled=True,
        ).astype(jnp.float32),
    )
    grad_projected = jnp.stack(
        [
            grad_queries.reshape(rows_here, half_width),
            key_grads.reshape(rows_here, half_width).astype(jnp.bfloat16),
            value_grads.reshape(rows_here, half_width).astype(jnp.bfloat16),
        ],
        1,
    )
    grad_mix = jnp.einsum(
        "td,tcn->dcn", normed_low, grad_projected, preferred_element_type=jnp.float32
    )
    grad_normed = lax.psum(
        jnp.einsum("tcn,dcn->td", grad_projected, mix_w, preferred_element_type=jnp.float32).astype(
            jnp.bfloat16
        ),
        "tp",
    ).astype(jnp.float32)
    input_grad = (
        (grad_hidden + norm_back(grad_normed, normal_one, inverse_one, vectors[0]))
        .astype(jnp.bfloat16)
        .reshape(images, local_tokens, model_width)
    )
    projected_sums = jnp.sum(grad_projected.astype(jnp.float32), 0)
    vector_part = jnp.concatenate(
        [
            jnp.stack(
                [
                    jnp.sum(grad_normed * normal_one, 0) * tp_first,
                    jnp.sum(grad_normed, 0) * tp_first,
                    place_at(projected_sums[0], (model_width,), tp_index * half_width, 0),
                    place_at(projected_sums[2], (model_width,), tp_index * half_width, 0),
                    jnp.sum(grad_branch.astype(jnp.float32), 0) * tp_first,
                    jnp.sum(grad_second * normal_two, 0) * tp_first,
                    jnp.sum(grad_second, 0) * tp_first,
                    jnp.sum(back, 0) * tp_first,
                ]
            ),
            place_at(grad_up_bias, (FF,), tp_index * half_hidden, 0).reshape(-1, model_width),
        ],
        0,
    )
    shards = (
        lax.psum_scatter(grad_mix, "fsdp", scatter_dimension=0, tiled=True),
        lax.psum_scatter(grad_out, "fsdp", scatter_dimension=1, tiled=True),
        lax.psum_scatter(grad_up, "fsdp", scatter_dimension=0, tiled=True),
        lax.psum_scatter(grad_down, "fsdp", scatter_dimension=1, tiled=True),
    )
    sum_mix, sum_out, sum_up, sum_down = (
        lax.psum(shards[0].astype(jnp.bfloat16), "ctx").astype(jnp.float32),
        lax.psum(shards[1].astype(jnp.bfloat16), "ctx").astype(jnp.float32),
        lax.psum(shards[2].astype(jnp.bfloat16), "ctx").astype(jnp.float32),
        lax.psum(shards[3].astype(jnp.bfloat16), "ctx").astype(jnp.float32),
    )
    fsdp_start = fsdp_index * width_piece
    tp_width = tp_index * half_width
    tp_hidden = tp_index * half_hidden
    mix_square = sum_mix * sum_mix
    out_square = sum_out * sum_out
    up_square = sum_up * sum_up
    down_square = sum_down * sum_down
    scalar_part = (
        jnp.stack(
            [
                jnp.sum(qkv_weight * qkv_weight),
                jnp.sum(out_weight * out_weight),
                jnp.sum(up_weight * up_weight),
                jnp.sum(down_weight * down_weight),
                jnp.sum(row_qkv) * tp_first,
                jnp.sum(row_out) * fsdp_first,
                jnp.sum(row_up) * tp_first,
                jnp.sum(row_down) * fsdp_first,
            ]
        )
        * ctx_first
    )
    (
        vector_grad,
        rows_mix,
        cols_mix,
        rows_out,
        cols_out,
        rows_up,
        cols_up,
        rows_down,
        cols_down,
        scalar_sums,
    ) = lax.psum(
        (
            vector_part,
            place_at(jnp.sum(mix_square, (1, 2)), (model_width,), fsdp_start, 0) * ctx_first,
            place_at(jnp.sum(mix_square, 0), (3, model_width), tp_width, 1) * ctx_first,
            place_at(jnp.sum(out_square, 1), (model_width,), tp_width, 0) * ctx_first,
            place_at(jnp.sum(out_square, 0), (model_width,), fsdp_start, 0) * ctx_first,
            place_at(jnp.sum(up_square, 1), (model_width,), fsdp_start, 0) * ctx_first,
            place_at(jnp.sum(up_square, 0), (FF,), tp_hidden, 0) * ctx_first,
            place_at(jnp.sum(down_square, 1), (FF,), tp_hidden, 0) * ctx_first,
            place_at(jnp.sum(down_square, 0), (model_width,), fsdp_start, 0) * ctx_first,
            scalar_part,
        ),
        ("fsdp", "ctx", "tp"),
    )
    qkv_rows, qkv_cols_flat, mix_update = factor_local(
        sum_mix.reshape(width_piece, -1),
        row_qkv,
        col_qkv.reshape(-1),
        rows_mix,
        lax.dynamic_slice_in_dim(rows_mix, fsdp_start, width_piece),
        lax.dynamic_slice_in_dim(cols_mix, tp_width, half_width, 1).reshape(-1),
        model_width,
        3 * model_width,
        scalar_sums[4],
    )
    out_rows, out_cols, out_update = factor_local(
        sum_out,
        row_out,
        col_out,
        rows_out,
        lax.dynamic_slice_in_dim(rows_out, tp_width, half_width),
        lax.dynamic_slice_in_dim(cols_out, fsdp_start, width_piece),
        model_width,
        model_width,
        scalar_sums[5],
    )
    up_rows, up_cols, up_update = factor_local(
        sum_up,
        row_up,
        col_up,
        rows_up,
        lax.dynamic_slice_in_dim(rows_up, fsdp_start, width_piece),
        lax.dynamic_slice_in_dim(cols_up, tp_hidden, half_hidden),
        model_width,
        FF,
        scalar_sums[6],
    )
    down_rows, down_cols, down_update = factor_local(
        sum_down,
        row_down,
        col_down,
        rows_down,
        lax.dynamic_slice_in_dim(rows_down, tp_hidden, half_hidden),
        lax.dynamic_slice_in_dim(cols_down, fsdp_start, width_piece),
        FF,
        model_width,
        scalar_sums[7],
    )
    vector_moment = decay_rate * vector_moments + (1.0 - decay_rate) * vector_grad * vector_grad
    vector_step = vector_grad * lax.rsqrt(vector_moment)
    local_square = (
        jnp.sum(mix_update * mix_update)
        + jnp.sum(out_update * out_update)
        + jnp.sum(up_update * up_update)
        + jnp.sum(down_update * down_update)
    )
    global_square = lax.psum(local_square, ("fsdp", "tp")) + jnp.sum(vector_step * vector_step)
    param_count = 4 * model_width * model_width + 2 * model_width * FF + vectors.size
    shrink = 1.0 / jnp.maximum(1.0, jnp.sqrt(global_square / param_count) / clip_level)
    qkv_new = (
        qkv_weight
        - step_rate
        * jnp.sqrt(scalar_sums[0] / (3 * model_width * model_width))
        * mix_update.reshape(qkv_weight.shape)
        * shrink
    )
    out_new = (
        out_weight
        - step_rate * jnp.sqrt(scalar_sums[1] / (model_width * model_width)) * out_update * shrink
    )
    up_new = (
        up_weight - step_rate * jnp.sqrt(scalar_sums[2] / (model_width * FF)) * up_update * shrink
    )
    down_new = (
        down_weight
        - step_rate * jnp.sqrt(scalar_sums[3] / (model_width * FF)) * down_update * shrink
    )
    vector_new = vectors - step_rate * jnp.sqrt(jnp.mean(vectors * vectors)) * vector_step * shrink
    return (
        output,
        input_grad,
        sum_mix,
        sum_out,
        sum_up,
        sum_down,
        vector_grad,
        qkv_new,
        out_new,
        up_new,
        down_new,
        vector_new,
        qkv_new.astype(jnp.bfloat16),
        out_new.astype(jnp.bfloat16),
        up_new.astype(jnp.bfloat16),
        down_new.astype(jnp.bfloat16),
        qkv_rows,
        qkv_cols_flat.reshape(3, half_width),
        out_rows,
        out_cols,
        up_rows,
        up_cols,
        down_rows,
        down_cols,
        vector_moment,
    )


MESH = pl.DeviceIdType.MESH
LANES = 128
SLOTS = 320
ROWS = 2 * SLOTS
WIDE = 512
CHUNKS = 12
PAIRS = 8
MIB = 1024 * 1024


def place():
    shard = lax.axis_index("fsdp")
    return (lax.div(shard, 2), lax.rem(shard, 2), lax.axis_index("ctx"), lax.axis_index("tp"))


def peers_of(z, y, x, c):
    line = [(lax.rem(z + step, 4) * 2 + y, x, c) for step in (1, 2, 3)]
    return (line, (z * 2 + 1 - y, x, c), (z * 2 + y, 1 - x, c), (z * 2 + y, x, 1 - c))


def greet(peers):
    barrier = pltpu.get_barrier_semaphore()
    for peer in peers:
        pl.semaphore_signal(barrier, inc=1, device_id=peer, device_id_type=MESH)
    pl.semaphore_wait(barrier, len(peers))


def remote(src, dst, send, recv, peer):
    return pltpu.make_async_remote_copy(
        src_ref=src, dst_ref=dst, send_sem=send, recv_sem=recv, device_id=peer, device_id_type=MESH
    )


def nn(left, right):
    return lax.dot_general(left, right, (((1,), (0,)), ((), ())), preferred_element_type=jnp.float32)


def nt(left, right):
    return lax.dot_general(left, right, (((1,), (1,)), ((), ())), preferred_element_type=jnp.float32)


def aligned(start, size, unit):
    if isinstance(start, int):
        return pl.ds(start, size)
    return pl.ds(pl.multiple_of(start, unit), size)


def columns(start, size):
    return aligned(start, size, LANES)


def slots_valid(counts, axis):
    shape = (1, ROWS) if axis else (ROWS, 1)
    slot = lax.broadcasted_iota(jnp.int32, shape, axis)
    first = counts[0, 0:1, 0:1].astype(jnp.int32)
    second = counts[1, 0:1, 0:1].astype(jnp.int32)
    return ((slot < SLOTS) & (slot < first)) | ((slot >= SLOTS) & (slot - SLOTS < second))


def square_sum(ref):
    flat = ref if len(ref.shape) == 2 else ref.reshape(ref.shape[0] * ref.shape[1], ref.shape[2])
    step = flat.shape[0] // 8

    def add(at, total):
        values = flat[pl.ds(pl.multiple_of(at * step, step), step), :]
        return total + jnp.sum(values * values, 0, keepdims=True)

    total = lax.fori_loop(0, 8, add, jnp.zeros((1, flat.shape[1]), jnp.float32))
    return jnp.sum(total, 1, keepdims=True)


def front_body(
    x_in, b_in, n_in, mix_w, out_w, up_w, down_w, vectors,
    kept, b_out, x_out, n_out, qkv, heads, hidden, second, squares,
    normed, w, wo,
    local, in_s, in_r, zs, zr, ys, yr, xs, xr, cs, cr, ws,
):
    z, y, x, c = place()
    line, y_peer, x_peer, c_peer = peers_of(z, y, x, c)
    own = []
    mine, theirs = 2 * x + c, 2 * (1 - x) + c
    pairs = ((x_in, x_out), (n_in, n_out), (b_in, b_out))
    for at, (src, dst) in enumerate(pairs):
        own.append(pltpu.make_async_copy(src.at[mine], dst.at[x], local.at[at]))
    for copy in own:
        copy.start()
    low = jnp.bfloat16
    for k in range(4):
        lanes = pl.ds(k * LANES, LANES)
        for part in range(3):
            w[k, c, z, y, :, pl.ds(part * LANES, LANES)] = mix_w[part, :, lanes].astype(low)
        w[k, c, z, y, :, pl.ds(3 * LANES, LANES)] = out_w[lanes, :].T.astype(low)
        w[4 + 2 * k, c, z, y] = up_w[:, pl.ds(k * WIDE, WIDE)].astype(low)
        for part in range(4):
            rows = pl.ds(k * WIDE + part * LANES, LANES)
            w[5 + 2 * k, c, z, y, :, pl.ds(part * LANES, LANES)] = down_w[rows, :].T.astype(low)
    greet(line + [y_peer, x_peer, c_peer])
    swaps = [
        remote(src.at[theirs], dst.at[x], in_s.at[at], in_r.at[at], x_peer)
        for at, (src, dst) in enumerate(pairs)
    ]

    def share(odd):
        size = 80 if odd else 96
        return aligned(x * (128 - size), size, 16), aligned(x * size, 128 - size, 16)

    def z_copies(k, odd):
        block = w.at[k, c, z, y, share(odd)[0]]
        return [remote(block, block, zs.at[k, at], zr.at[k, at], peer) for at, peer in enumerate(line)]

    def y_copies(k, odd):
        rows = share(odd)[0]
        blocks = [w.at[k, c, pl.ds(2 * at, 2), y, rows] for at in range(2)]
        return [remote(block, block, ys.at[k, at], yr.at[k, at], y_peer) for at, block in enumerate(blocks)]

    def x_copies(k, odd):
        rows = share(odd)[1]
        blocks = [w.at[k, c, at, :, rows] for at in range(4)]
        return [remote(block, block, xs.at[k, at], xr.at[k, at], x_peer) for at, block in enumerate(blocks)]

    def c_copies(k):
        blocks = [w.at[k, c, at] for at in range(4)]
        return [remote(block, block, cs.at[k, at], cr.at[k, at], c_peer) for at, block in enumerate(blocks)]

    def keep(k):
        return pltpu.make_async_copy(w.at[k], kept.at[k], ws.at[k])

    def start(copies):
        for copy in copies:
            copy.start()

    def arrive(copies):
        for copy in copies:
            copy.wait_recv()

    ahead = 2

    def within(k):
        return not isinstance(k, int) or 0 <= k < CHUNKS

    def link_step(t, odd):
        if within(t):
            arrive(z_copies(t, odd))
            start(y_copies(t, odd))
        if isinstance(t, int):
            if within(t + ahead):
                start(z_copies(t + ahead, odd))
        else:

            @pl.when(t + ahead < CHUNKS)
            def _():
                start(z_copies(t + ahead, odd))

        if within(t - 2):
            arrive(y_copies(t - 2, odd))
            start(x_copies(t - 2, odd))
        if within(t - 4):
            arrive(x_copies(t - 4, odd))
            start(c_copies(t - 4))
        if within(t - 6):
            arrive(c_copies(t - 6))
            keep(t - 6).start()

    swaps[0].start()
    swaps[1].start()
    for t in range(ahead):
        start(z_copies(t, t % 2 == 1))
    swaps[2].start()
    own[0].wait()
    own[1].wait()

    def norm_first(half):
        @pl.loop(0, SLOTS // 64)
        def _(at):
            rows = pl.ds(pl.multiple_of(at * 64, 64), 64)
            result, _, _ = norm_rows(
                x_out[half, rows, :].astype(jnp.float32), vectors[0:1, :], vectors[1:2, :]
            )
            normed[half, rows, :] = result.astype(jnp.bfloat16)

    norm_first(x)
    for m, ref in enumerate((mix_w, out_w, up_w, down_w)):
        squares[pl.ds(m, 1), :] = jnp.broadcast_to(square_sum(ref), (1, LANES))
    link_step(0, False)
    swaps[0].wait_recv()
    swaps[1].wait_recv()
    norm_first(1 - x)
    for t in range(1, 7):
        link_step(t, t % 2 == 1)
    valid = slots_valid(n_out, 1)
    lane = lax.broadcasted_iota(jnp.int32, (1, LANES), 1)

    def pair_task(side, k):
        pair = side * 4 + k
        weights = w[k, side].reshape(1024, WIDE)
        wo[:, columns(pair * LANES, LANES)] = weights[:, 3 * LANES :]
        weights = weights[:, : 3 * LANES]
        q_bias = vectors[2:3, columns(pair * LANES, LANES)]
        v_bias = vectors[3:4, columns(pair * LANES, LANES)]
        bias = jnp.concatenate([q_bias, jnp.zeros_like(q_bias), v_bias], 1)
        for half in range(2):
            qkv[pair, pl.ds(half * SLOTS, SLOTS), :] = (nn(normed[half], weights) + bias).astype(
                jnp.bfloat16
            )

        @pl.loop(0, 2)
        def _(half):
            rows = pl.ds(pl.multiple_of(half * SLOTS, SLOTS), SLOTS)
            queries = qkv[pair, rows, pl.ds(0, LANES)] * jnp.bfloat16(0.125)
            keys = qkv[pair, :, pl.ds(LANES, LANES)]
            values = qkv[pair, :, pl.ds(2 * LANES, LANES)]
            results = []
            for at in range(2):
                here = (lane < HD) if at == 0 else (lane >= HD)
                scores = nt(jnp.where(here, queries, jnp.zeros_like(queries)), keys)
                scores = jnp.where(valid, scores, -1000000000.0)
                top = jnp.max(scores, 1, keepdims=True)
                exponent = jnp.exp(scores - top)
                attention = exponent * (1.0 / jnp.sum(exponent, 1, keepdims=True))
                results.append(nn(attention.astype(jnp.bfloat16), values))
            heads[rows, columns(pair * LANES, LANES)] = jnp.where(
                lane < HD, results[0], results[1]
            ).astype(jnp.bfloat16)

    for k in range(4):
        pair_task(0, k)
        link_step(2 * k + 7, True)
        pair_task(1, k)
        link_step(2 * k + 8, False)

    for tile in range(4):
        for half in range(2):
            rows = pl.ds(half * SLOTS, SLOTS)
            cols = pl.ds(tile * 256, 256)
            branch = nt(heads[rows, :], wo[cols, :])
            hidden[rows, cols] = x_out[half, :, cols].astype(jnp.float32) + (branch + vectors[4:5, cols])
        if tile < 3:
            link_step(15 + tile, tile != 1)

    @pl.loop(0, ROWS // 64)
    def _(at):
        rows = pl.ds(pl.multiple_of(at * 64, 64), 64)
        result, _, _ = norm_rows(hidden[rows, :], vectors[5:6, :], vectors[6:7, :])
        second[rows, :] = result.astype(jnp.bfloat16)

    own[2].wait()
    for k in range(CHUNKS):
        keep(k).wait()
    swaps[2].wait_recv()
    for swap in swaps:
        swap.wait_send()

    @pl.loop(0, CHUNKS // 2)
    def _(at):
        for odd in (False, True):
            k = 2 * at + int(odd)
            for copy in z_copies(k, odd) + y_copies(k, odd) + x_copies(k, odd) + c_copies(k):
                copy.wait_send()


def front_all(x_in, b_in, n_in, weights, vectors):
    dma = pltpu.SemaphoreType.DMA
    low, full = jnp.bfloat16, jnp.float32
    anywhere = pl.BlockSpec(memory_space=pl.ANY)
    in_vmem = pl.BlockSpec(memory_space=pltpu.VMEM)
    shape = jax.ShapeDtypeStruct
    width = x_in.shape[2]
    return pl.pallas_call(
        front_body,
        out_shape=(
            shape((CHUNKS, 2, 4, 2, 128, WIDE), low),
            shape((2, SLOTS, width), low),
            shape((2, SLOTS, width), low),
            shape((2, 8, LANES), full),
            shape((PAIRS, ROWS, 3 * LANES), low),
            shape((ROWS, width), low),
            shape((ROWS, width), full),
            shape((ROWS, width), low),
            shape((8, LANES), full),
        ),
        in_specs=[anywhere] * 3 + [in_vmem] * 5,
        out_specs=(anywhere, anywhere) + (in_vmem,) * 7,
        scratch_shapes=[
            pltpu.VMEM((2, SLOTS, width), low),
            pltpu.VMEM((CHUNKS, 2, 4, 2, 128, WIDE), low),
            pltpu.VMEM((1024, 1024), low),
            dma((3,)), dma((3,)), dma((3,)), dma((CHUNKS, 3)), dma((CHUNKS, 3)),
            dma((CHUNKS, 2)), dma((CHUNKS, 2)), dma((CHUNKS, 4)), dma((CHUNKS, 4)), dma((CHUNKS, 4)), dma((CHUNKS, 4)),
            dma((CHUNKS,)),
        ],
        compiler_params=pltpu.CompilerParams(
            collective_id=0, has_side_effects=True, vmem_limit_bytes=58 * MIB
        ),
    )(x_in, b_in, n_in, *weights, vectors)


def add_into(held, index, arrived, from_index):
    held[index] = (
        held[index].astype(jnp.float32) + arrived[from_index].astype(jnp.float32)
    ).astype(jnp.bfloat16)


class Scatter:
    def __init__(self, crosswise, refs):
        self.crosswise = crosswise
        self.where = place()
        self.line, self.y_peer, self.x_peer, self.c_peer = peers_of(*self.where)
        x = self.where[2]
        self.near = aligned(x * 64, 64, 64)
        self.far = aligned((1 - x) * 64, 64, 64)
        self.slot = [sum(k == crosswise[at] for k in crosswise[:at]) for at in range(len(crosswise))]
        (
            self.g, self.cb, self.xa, self.ya, self.za, self.fa, self.yb, self.zb, self.xb, self.stage,
            self.cs, self.cr, self.s1s, self.s1r, self.s2s, self.s2r, self.s3s, self.s3r, self.s4s, self.s4r,
            self.out_sem, self.free,
        ) = refs[:22]
        self.totals = refs[22:]
        self.waited = set()

    def hops(self, stage, q):
        z, y, x, c = self.where
        at, own = self.slot[q], self.g.at[q % 8]
        if stage == 0:
            return [
                remote(self.g.at[8 + q % 4], self.cb.at[q % 4], self.cs.at[q], self.cr.at[q], self.c_peer)
            ]
        first, third = (self.s1s.at[q], self.s1r.at[q]), (self.s4s.at[q], self.s4r.at[q])
        second, last = (self.s2s.at[q], self.s2r.at[q]), (self.s3s.at[q], self.s3r.at[q])
        ahead = [lax.rem(z + d + 1, 4) for d in range(3)]
        if self.crosswise[q]:
            near = self.near
            if stage == 1:
                return [remote(own.at[:, :, self.far], self.xa.at[at], *first, self.x_peer)]
            if stage == 2:
                return [
                    remote(own.at[:, 1 - y, near], self.ya.at[at], second[0].at[0], second[1].at[0], self.y_peer)
                ]
            if stage == 3:
                return [
                    remote(own.at[to, y, near], self.za.at[at, d], last[0].at[d], last[1].at[d], peer)
                    for d, (to, peer) in enumerate(zip(ahead, self.line))
                ]
            return [remote(own.at[z, y, near], self.fa.at[at], *third, self.x_peer)]
        if stage == 1:
            return [remote(own.at[:, 1 - y], self.yb.at[at], *first, self.y_peer)]
        if stage == 2:
            return [
                remote(own.at[to, y], self.zb.at[at, d], second[0].at[d], second[1].at[d], peer)
                for d, (to, peer) in enumerate(zip(ahead, self.line))
            ]
        if stage == 3:
            return [remote(own.at[z, y], self.xb.at[at], last[0].at[0], last[1].at[0], self.x_peer)]
        return []

    def start(self, stage, q):
        for copy in self.hops(stage, q):
            copy.start()

    def arrive(self, stage, q):
        for copy in self.hops(stage, q):
            copy.wait_recv()

    def sent(self, q, stages):
        for stage in stages:
            self.waited.add((stage, q))
            for copy in self.hops(stage, q):
                copy.wait_send()

    def begin(self, q):
        if q >= 4:
            pl.semaphore_wait(self.free.at[q % 4], 1)
        self.start(0, q)

    def one(self, q):
        self.arrive(0, q)

        @pl.loop(0, 8)
        def _(block):
            zi, yi = lax.div(block, 2), lax.rem(block, 2)
            add_into(self.g, (q % 8, zi, yi), self.cb, (q % 4, zi, yi))

        if q < 8:
            pl.semaphore_signal(
                self.free.at[q % 4], inc=1, device_id=self.c_peer, device_id_type=MESH
            )

        self.start(1, q)

    def two(self, q):
        y, at = self.where[1], self.slot[q]
        self.arrive(1, q)
        if self.crosswise[q]:

            @pl.loop(0, 8)
            def _(block):
                zi, yi = lax.div(block, 2), lax.rem(block, 2)
                add_into(self.g, (q % 8, zi, yi, self.near), self.xa, (at, zi, yi))

        else:

            @pl.loop(0, 4)
            def _(zi):
                add_into(self.g, (q % 8, zi, y), self.yb, (at, zi))

        self.start(2, q)

    def sum_line(self, q, rows, buffer):
        z, y = self.where[:2]
        value = self.g[(q % 8, z, y) + rows].astype(jnp.float32)
        for d in range(3):
            value += buffer[self.slot[q], d].astype(jnp.float32)
        self.g[(q % 8, z, y) + rows] = value.astype(jnp.bfloat16)

    def three(self, q):
        y, at = self.where[1], self.slot[q]
        self.arrive(2, q)
        if self.crosswise[q]:

            @pl.loop(0, 4)
            def _(zi):
                add_into(self.g, (q % 8, zi, y, self.near), self.ya, (at, zi))

        else:
            self.sum_line(q, (), self.zb)
        self.start(3, q)

    def export(self, q):
        target = self.totals[0].at[q] if q < 8 else self.totals[1].at[q - 8]
        return pltpu.make_async_copy(self.stage.at[q % 4], target, self.out_sem.at[q])

    def four(self, q):
        z, y = self.where[:2]
        at = self.slot[q]
        self.arrive(3, q)
        if self.crosswise[q]:
            self.sum_line(q, (self.near,), self.za)
            self.start(4, q)
        else:
            if q >= 4:
                self.export(q - 4).wait()
            self.stage[q % 4] = self.g[q % 8, z, y].astype(jnp.float32) + self.xb[at].astype(jnp.float32)
            self.export(q).start()

    def five(self, q):
        z, y = self.where[:2]
        if self.crosswise[q]:
            self.arrive(4, q)
            if q >= 4:
                self.export(q - 4).wait()
            self.stage[q % 4, self.near] = self.g[q % 8, z, y, self.near].astype(jnp.float32)
            self.stage[q % 4, self.far] = self.fa[self.slot[q]].astype(jnp.float32)
            self.export(q).start()

    def run(self, calls):
        for name, q in calls:
            getattr(self, name)(q)

    def finish(self):
        count = len(self.crosswise)
        for q in range(count - 4, count):
            self.export(q).wait()
        for stage in range(5):
            for q in range(count):
                if (stage, q) not in self.waited:
                    self.sent(q, (stage,))

    @staticmethod
    def scratch(crosswise):
        dma, vmem, low = pltpu.SemaphoreType.DMA, pltpu.VMEM, jnp.bfloat16
        n, across = len(crosswise), sum(crosswise)
        along = n - across
        return [
            vmem((12, 4, 2, 128, WIDE), low),
            vmem((4, 4, 2, 128, WIDE), low),
            vmem((across, 4, 2, 64, WIDE), low),
            vmem((across, 4, 64, WIDE), low),
            vmem((across, 3, 64, WIDE), low),
            vmem((across, 64, WIDE), low),
            vmem((along, 4, 128, WIDE), low),
            vmem((along, 3, 128, WIDE), low),
            vmem((along, 128, WIDE), low),
            vmem((4, 128, WIDE), jnp.float32),
            dma((n,)), dma((n,)), dma((n,)), dma((n,)), dma((n, 3)), dma((n, 3)),
            dma((n, 3)), dma((n, 3)), dma((n,)), dma((n,)), dma((n,)), pltpu.SemaphoreType.REGULAR((4,)),
        ]


class Spread:
    def __init__(self, src, dst, sems):
        z, y, x, c = place()
        _, _, x_peer, c_peer = peers_of(z, y, x, c)
        mine, theirs = 2 * x + c, 2 * (1 - x) + c
        self.cross = remote(src.at[1 - x], dst.at[mine], sems.at[0], sems.at[1], x_peer)
        self.near = remote(src.at[x], dst.at[mine], sems.at[2], sems.at[3], c_peer)
        self.local = pltpu.make_async_copy(src.at[x], dst.at[mine], sems.at[4])
        self.onward = remote(dst.at[theirs], dst.at[theirs], sems.at[5], sems.at[6], c_peer)

    def start(self):
        self.near.start()
        self.local.start()

    def forward(self):
        self.cross.wait_recv()
        self.onward.start()

    def finish(self):
        self.cross.wait_send()
        self.near.wait()
        self.local.wait()
        self.onward.wait()


def transpose_into(target, source):
    for at in range(source.shape[1] // LANES):
        target[pl.ds(at * LANES, LANES), :] = source[:, pl.ds(at * LANES, LANES)].T


KINDS = (True, False) * 4 + (True, False, False, False)


def both(name, tile):
    return ((name, 2 * tile), (name, 2 * tile + 1))


MLP_PLAN = {
    0: both("begin", 0),
    1: both("one", 0),
    2: both("begin", 1),
    3: both("one", 1) + both("two", 0),
    4: both("begin", 2),
    5: both("one", 2),
    6: both("begin", 3) + both("two", 1) + both("three", 0),
    7: both("one", 3) + both("four", 0),
}
OUTPUT_PLAN = both("five", 0) + both("two", 2)
NORM_PLAN = both("three", 1)
PAIR_PLAN = {
    0: (("begin", 8),) + both("four", 1) + both("two", 3),
    1: (("one", 8),) + both("three", 2) + both("five", 1),
    2: (("begin", 9),) + both("four", 2) + both("three", 3),
    3: (("one", 9), ("two", 8)) + both("five", 2),
    4: (("begin", 10),) + both("four", 3),
    5: (("one", 10), ("two", 9), ("three", 8)) + both("five", 3),
    6: (("begin", 11), ("three", 9), ("four", 8)),
    7: (("one", 11), ("two", 10), ("four", 9)),
}
DRAIN_PLAN = (("five", 8), ("three", 10), ("two", 11), ("four", 10), ("three", 11), ("four", 11))


def back_body(
    w, second_in, back_in, x_in, hidden_in, counts, qkv_in, heads_in, vectors,
    total_m, total_q, out_spread, grad_spread, bias_grad, vec_out, qv_out,
    tall, tall_t, back, back_t, halves, hidden, total_acc, grad_second, out_low, in_low, wv,
    grad_part, parts, query_part, qkv_v, heads_v, vec_acc, *rest,
):
    ws, qs, hs, in_sems, out_sems, grad_sems = rest[:6]
    z, y, x, c = place()
    rs = Scatter(KINDS, rest[6:] + (total_m, total_q))
    greet(rs.line + [rs.y_peer, rs.x_peer, rs.c_peer])
    low, full = jnp.bfloat16, jnp.float32

    def turn(s):
        return (s % 2, s // 2) if isinstance(s, int) else (lax.rem(s, 2), lax.div(s, 2))

    def side_of(s):
        return lax.rem(1 - c + s, 2)

    def tile_load(s):
        slot, j = turn(s)
        return pltpu.make_async_copy(w.at[pl.ds(4 + 2 * j, 2), side_of(s)], wv.at[slot], ws.at[slot])

    def pair_loads(s):
        slot, k = turn(s)
        pair = side_of(s) * 4 + k
        return [
            pltpu.make_async_copy(w.at[k, side_of(s)], wv.at[slot, 0], ws.at[slot]),
            pltpu.make_async_copy(qkv_in.at[pair], qkv_v.at[slot], qs.at[slot]),
            pltpu.make_async_copy(
                heads_in.at[:, columns(pair * LANES, LANES)], heads_v.at[slot], hs.at[slot]
            ),
        ]

    def start(copies):
        for copy in copies:
            copy.start()

    loads = [
        pltpu.make_async_copy(src, dst, in_sems.at[at])
        for at, (src, dst) in enumerate(
            ((second_in, tall), (back_in, back), (hidden_in, hidden), (x_in, in_low))
        )
    ]
    start(loads[:3])
    tile_load(0).start()
    tile_load(1).start()
    loads[3].start()
    grad_second[...] = jnp.zeros_like(grad_second)
    loads[0].wait()
    transpose_into(tall_t, tall)
    loads[1].wait()
    transpose_into(back_t, back)
    loads[2].wait()
    total_acc[...] = hidden[...] + vectors[7:8, :]

    @pl.loop(0, 8)
    def _(s):
        slot, j = turn(s)
        side = side_of(s)
        tile_load(s).wait()
        tile = side * 4 + j
        bias = vectors[pl.ds(8 + side * 2 + lax.div(j, 2), 1), columns(lax.rem(j, 2) * WIDE, WIDE)]
        up = wv[slot, 0].reshape(1024, WIDE)
        down = wv[slot, 1].reshape(1024, WIDE)
        sums = jnp.zeros((1, WIDE), full)
        for half in range(2):
            rows = pl.ds(half * SLOTS, SLOTS)
            pre = nn(tall[rows, :], up) + bias
            grad_active = nn(back[rows, :], down)
            share = 0.5 * (1.0 + lax.erf(pre * 0.7071067811865476))
            slope = share + pre * jnp.exp(-0.5 * pre * pre) * 0.3989422804014327
            act = (pre * share).astype(low)
            grad_pre = (grad_active * slope).astype(low)
            halves[0, rows, :] = act
            halves[1, rows, :] = grad_pre
            sums += jnp.sum(grad_pre.astype(full), 0, keepdims=True)
            total_acc[rows, :] += nt(act, down)
            grad_second[rows, :] += nt(grad_pre, up)
        bias_grad[pl.ds(tile, 1), :] = sums
        for again in (4, 6):

            @pl.when(s == again)
            def _():
                rs.sent(again - 4, (0,))
                rs.sent(again - 3, (0,))

        first = jnp.where(slot == 0, 8 + lax.rem(2 * j, 4), 2 * j)
        for zi in range(4):
            rows = pl.ds(zi * 256, 256)
            rs.g[first, zi] = nn(tall_t[rows, :], halves[1]).astype(low).reshape(2, 128, WIDE)
            rs.g[first + 1, zi] = nn(back_t[rows, :], halves[0]).astype(low).reshape(2, 128, WIDE)

        @pl.when(s < 6)
        def _():
            tile_load(s + 2).start()

        for done, calls in MLP_PLAN.items():

            @pl.when(s == done)
            def _():
                rs.run(calls)

    start(pair_loads(0))
    start(pair_loads(1))
    sent_out = Spread(out_low, out_spread, out_sems)
    for first in (True, False):
        half = 1 - x if first else x
        out_low[half] = total_acc[aligned(half * SLOTS, SLOTS, SLOTS), :].astype(low)
        if first:
            sent_out.cross.start()
    sent_out.start()
    rs.run(OUTPUT_PLAN)
    vec_acc[...] = jnp.zeros_like(vec_acc)

    def fold(row, value):
        vec_acc[row] += jnp.sum(value.reshape(-1, 8, value.shape[1]), 0)

    step = 64
    loads[3].wait()

    @pl.loop(0, ROWS // step)
    def _(at):
        rows = pl.ds(pl.multiple_of(at * step, step), step)
        half_rows = pl.ds(pl.multiple_of(lax.rem(at, 5) * step, step), step)
        ones = vectors[5:6, :]
        _, normal, inverse = norm_rows(hidden[rows, :], ones, vectors[6:7, :])
        grad = grad_second[rows, :]
        behind = back[rows, :].astype(full)
        result = behind + norm_back(grad, normal, inverse, ones)
        hidden[rows, :] = result
        branch = result.astype(low)
        back[rows, :] = branch
        fold(2, branch.astype(full))
        fold(3, grad * normal)
        fold(4, grad)
        fold(5, behind)
        first, _, _ = norm_rows(
            in_low[lax.div(at, 5), half_rows, :].astype(full), vectors[0:1, :], vectors[1:2, :]
        )
        tall[rows, :] = first.astype(low)

    transpose_into(back_t, back)
    transpose_into(tall_t, tall)
    total_acc[...] = jnp.zeros_like(total_acc)
    rs.run(NORM_PLAN)
    sent_out.forward()
    valid = slots_valid(counts, 0)
    lane = lax.broadcasted_iota(jnp.int32, (1, LANES), 1)
    line = lax.broadcasted_iota(jnp.int32, (LANES, 1), 0)

    @pl.loop(0, 8)
    def _(s):
        slot, k = turn(s)
        pair = side_of(s) * 4 + k
        for copy in pair_loads(s):
            copy.wait()
        grad_heads = nn(back[...], wv[slot, 0, :, :, :, pl.ds(3 * LANES, LANES)].reshape(1024, LANES))
        grad_heads = grad_heads.astype(low)
        queries = qkv_v[slot, :, pl.ds(0, LANES)]
        keys = qkv_v[slot, :, pl.ds(LANES, LANES)]
        values = qkv_v[slot, :, pl.ds(2 * LANES, LANES)]
        keys_t = keys.T
        parts[...] = jnp.zeros_like(parts)
        query_part[...] = jnp.zeros_like(query_part)

        @pl.loop(0, 2)
        def _(at):
            here = (lane >= at * HD) & (lane < at * HD + HD)
            own_keys = jnp.where(here, keys * jnp.bfloat16(0.125), jnp.zeros_like(keys))
            own_values = jnp.where(here, values, jnp.zeros_like(values))
            scores = jnp.where(valid, nt(own_keys, queries), -1000000000.0)
            top = jnp.max(scores, 0, keepdims=True)
            exponent = jnp.exp(scores - top)
            attention = exponent * (1.0 / jnp.sum(exponent, 0, keepdims=True))
            grad_attention = nt(own_values, grad_heads)
            inner = jnp.sum(attention * grad_attention, 0, keepdims=True)
            grad_scores = (attention * (grad_attention - inner)).astype(low)
            own_line = (line >= at * HD) & (line < at * HD + HD)
            query_part[...] += jnp.where(own_line, nn(keys_t, grad_scores), 0.0)
            parts[0] += jnp.where(here, nn(grad_scores, queries), 0.0)
            parts[1] += jnp.where(here, nn(attention.astype(low), grad_heads), 0.0)

        grad_q = (query_part[...] * 0.125).T.astype(low)
        grad_k = (parts[0] * 0.125).astype(low)
        grad_v = parts[1].astype(low)
        grad_part[:, pl.ds(0, LANES)] = grad_q
        grad_part[:, pl.ds(LANES, LANES)] = grad_k
        grad_part[:, pl.ds(2 * LANES, LANES)] = grad_v
        qv_out[pl.ds(pair, 1), :] = jnp.sum(grad_q.astype(full), 0, keepdims=True)
        qv_out[pl.ds(8 + pair, 1), :] = jnp.sum(grad_v.astype(full), 0, keepdims=True)
        for half in range(2):
            rows = pl.ds(half * SLOTS, SLOTS)
            total_acc[rows, :] += nt(
                grad_part[rows, :], wv[slot, 0, :, :, :, pl.ds(0, 3 * LANES)].reshape(1024, 3 * LANES)
            )
        for again in range(4):

            @pl.when(s == 2 * again)
            def _():
                rs.sent(4 + again, (0,))

            @pl.when(s == 2 * again + 1)
            def _():
                rs.sent(again, (1, 2, 3, 4))

        target = jnp.where(slot == 0, 8 + k, k)
        for zi in range(4):
            rows = pl.ds(zi * 256, 256)
            rs.g[target, zi, :, :, pl.ds(0, 3 * LANES)] = (
                nn(tall_t[rows, :], grad_part[...]).astype(low).reshape(2, 128, 3 * LANES)
            )
            rs.g[target, zi, :, :, pl.ds(3 * LANES, LANES)] = (
                nn(back_t[rows, :], heads_v[slot]).astype(low).reshape(2, 128, LANES)
            )

        @pl.when(s < 6)
        def _():
            start(pair_loads(s + 2))

        for done, calls in PAIR_PLAN.items():

            @pl.when(s == done)
            def _():
                rs.run(calls)

    sent_grad = Spread(in_low, grad_spread, grad_sems)
    for first in (True, False):
        half = 1 - x if first else x

        @pl.loop(0, SLOTS // step)
        def _(at):
            half_rows = pl.ds(pl.multiple_of(at * step, step), step)
            rows = aligned(half * SLOTS + at * step, step, step)
            ones = vectors[0:1, :]
            _, normal, inverse = norm_rows(in_low[half, half_rows, :].astype(full), ones, vectors[1:2, :])
            grad = total_acc[rows, :]
            fold(0, grad * normal)
            fold(1, grad)
            result = hidden[rows, :] + norm_back(grad, normal, inverse, ones)
            in_low[half, half_rows, :] = result.astype(low)

        if first:
            sent_grad.cross.start()
    sent_grad.start()
    for row in range(6):
        vec_out[pl.ds(row, 1), :] = jnp.sum(vec_acc[row], 0, keepdims=True)
    rs.run(DRAIN_PLAN)
    sent_grad.forward()
    sent_out.finish()
    sent_grad.finish()
    rs.finish()


def back_all(w, second, back, x_all, hidden, counts, qkv, heads, vectors):
    dma, vmem = pltpu.SemaphoreType.DMA, pltpu.VMEM
    low, full = jnp.bfloat16, jnp.float32
    anywhere = pl.BlockSpec(memory_space=pl.ANY)
    in_vmem = pl.BlockSpec(memory_space=pltpu.VMEM)
    shape = jax.ShapeDtypeStruct
    width = second.shape[1]
    return pl.pallas_call(
        back_body,
        out_shape=(
            shape((8, 128, WIDE), full),
            shape((4, 128, WIDE), full),
            shape((4, SLOTS, width), low),
            shape((4, SLOTS, width), low),
            shape((8, WIDE), full),
            shape((8, width), full),
            shape((16, LANES), full),
        ),
        in_specs=[anywhere] * 5 + [in_vmem] + [anywhere] * 2 + [in_vmem],
        out_specs=(anywhere,) * 4 + (in_vmem,) * 3,
        scratch_shapes=[
            vmem((ROWS, width), low),
            vmem((width, ROWS), low),
            vmem((ROWS, width), low),
            vmem((width, ROWS), low),
            vmem((2, ROWS, WIDE), low),
            vmem((ROWS, width), full),
            vmem((ROWS, width), full),
            vmem((ROWS, width), full),
            vmem((2, SLOTS, width), low),
            vmem((2, SLOTS, width), low),
            vmem((2, 2, 4, 2, 128, WIDE), low),
            vmem((ROWS, 3 * LANES), low),
            vmem((2, ROWS, LANES), full),
            vmem((LANES, ROWS), full),
            vmem((2, ROWS, 3 * LANES), low),
            vmem((2, ROWS, LANES), low),
            vmem((6, 8, width), full),
            dma((2,)), dma((2,)), dma((2,)), dma((4,)), dma((7,)), dma((7,)),
        ] + Scatter.scratch(KINDS),
        compiler_params=pltpu.CompilerParams(
            collective_id=1, has_side_effects=True, vmem_limit_bytes=62 * MIB
        ),
    )(w, second, back, x_all, hidden, counts, qkv, heads, vectors)


TILES = (
    [t for t in range(16) if t % 4 < 3],
    [3, 7, 11, 15],
    [t for t in range(16, 48) if t // 4 % 2 == 0],
    [t for t in range(16, 48) if t // 4 % 2 == 1],
)
SIZES = (3072.0 * 1024.0, 1024.0 * 1024.0, 4096.0 * 1024.0, 4096.0 * 1024.0)
VECS = 12
MISC = 12
SUMS = 14


def col_of(refs, t):
    chunk, part = t // 4, t % 4
    if chunk < 4:
        if part < 3:
            return refs[0].at[pl.ds(part, 1), pl.ds(chunk * LANES, LANES)]
        return refs[1].at[pl.ds(chunk, 1), :]
    return refs[2 + chunk % 2].at[pl.ds((chunk - 4) // 2 * 4 + part, 1), :]


def factor_body(
    total_q, total_m, squares, vec_sums, qv_sums, bias_grad, vecs, moments,
    row_mix, col_out, row_up, col_down, col_mix, row_out, col_up, row_down,
    row_new, row_flat, new_mix, new_out, new_up, new_down, vec_grad, vec_moment, vec_new, scale,
    core_s, core_r, pack_s, pack_r, ctx_r, line_s, line_r, y_r, last_s, last_r,
    c_ss, c_rs, x_ss, x_rs, z_ss, z_rs, y_ss, y_rs, l_ss, l_rs,
):
    z, y, x, c = place()
    line, y_peer, x_peer, c_peer = peers_of(z, y, x, c)
    square_peers = []
    for step in range(1, 16):
        spot = lax.rem((z * 2 + y) * 2 + c + step, 16)
        square_peers.append((lax.div(spot, 2), x, lax.rem(spot, 2)))
    greet(square_peers + [x_peer])

    def tile_of(t):
        cols = pl.ds(t % 4 * LANES, LANES)
        return total_q[t // 4, :, cols] if t < 16 else total_m[t // 4 - 4, :, cols]

    def lanes(at):
        return pl.ds(at % 8 * LANES, LANES)

    lane = lax.broadcasted_iota(jnp.int32, (128, 128), 1)
    core_s[pl.ds(0, 2), :] = vec_sums[pl.ds(0, 2), :]
    for at in range(8):
        core_s[pl.ds(2, 1), lanes(at)] = qv_sums[pl.ds(at, 1), :]
        core_s[pl.ds(3, 1), lanes(at)] = qv_sums[pl.ds(8 + at, 1), :]
        core_s[pl.ds(8 + at // 2, 1), pl.ds(at % 2 * WIDE, WIDE)] = bias_grad[pl.ds(at, 1), :]
    core_s[pl.ds(4, 4), :] = vec_sums[pl.ds(2, 4), :]
    packed = jnp.zeros((128, 128), jnp.float32)
    sums, olds = [], []
    old_cols = (col_mix, row_out, col_up, row_down)
    for m in range(4):
        block = jnp.zeros((128, 128), jnp.float32)
        old = jnp.zeros((1, LANES), jnp.float32)
        for t in TILES[m]:
            tile = tile_of(t)
            tile = tile * tile
            line_s[pl.ds(SUMS + t // 8, 1), lanes(t)] = jnp.sum(tile, 0, keepdims=True)
            block += tile
            old += col_of(old_cols, t)[...]
        per_row = jnp.sum(block, 1, keepdims=True)
        packed = jnp.where((lane >= 32 * m) & (lane < 32 * m + 32), per_row, packed)
        sums.append(jnp.sum(per_row, 0, keepdims=True))
        if m % 2 == 0:
            olds.append(jnp.sum((row_mix, None, row_up)[m][...], 1, keepdims=True) * 0.5)
        else:
            olds.append(jnp.sum(old, 1, keepdims=True) * 0.125)
    pack_s[...] = packed
    misc = sums + [squares[pl.ds(m, 1), 0:1] for m in range(4)] + olds + [jnp.zeros((1, 1), jnp.float32)] * 4
    for at, value in enumerate(misc):
        core_s[pl.ds(MISC + at // 8, 1), lanes(at)] = jnp.broadcast_to(value, (1, LANES))
    core_s[pl.ds(14, 2), :] = jnp.zeros((2, 1024), jnp.float32)
    hops = [
        remote(core_s, core_r, c_ss.at[0], c_rs.at[0], c_peer),
        remote(pack_s, pack_r, c_ss.at[1], c_rs.at[1], c_peer),
    ]
    for hop in hops:
        hop.start()
    for hop in hops:
        hop.wait()
    core_r[...] = core_r[...] + core_s[...]
    hop = remote(core_r, ctx_r, x_ss.at[0], x_rs.at[0], x_peer)
    hop.start()
    hop.wait()
    line_s[pl.ds(0, VECS), :] = core_r[pl.ds(0, VECS), :] + ctx_r[pl.ds(0, VECS), :]
    line_s[pl.ds(VECS, 2), :] = core_r[pl.ds(VECS, 2), :]
    line_s[pl.ds(20, 4), :] = jnp.zeros((4, 1024), jnp.float32)
    hops = [
        remote(line_s, line_r.at[z], z_ss.at[at], z_rs.at[at], peer) for at, peer in enumerate(line)
    ]
    for hop in hops:
        hop.start()
    line_r[pl.ds(z, 1)] = line_s[...][None]
    for hop in hops:
        hop.wait()
    line_s[...] = (line_r[0] + line_r[1]) + (line_r[2] + line_r[3])
    hop = remote(line_s, y_r, y_ss.at[0], y_rs.at[0], y_peer)
    hop.start()
    hop.wait()
    line_s[...] = line_s[...] + y_r[...]
    grads = line_s[pl.ds(0, VECS), :]
    vec_grad[...] = grads
    moment = decay_rate * moments[...] + (1.0 - decay_rate) * grads * grads
    vec_moment[...] = moment
    vec_step = grads * lax.rsqrt(moment)
    new_cols = (new_mix, new_out, new_up, new_down)
    for t in range(48):
        col_of(new_cols, t)[...] = decay_rate * col_of(old_cols, t)[...] + (1.0 - decay_rate) * (
            line_s[pl.ds(SUMS + t // 8, 1), lanes(t)] * (1.0 / 1024.0)
        )
    row_sum = pack_r[...] + pack_s[...]
    row_count = jnp.where(lane < 32, 1.0 / 3072.0, jnp.where(lane < 64, 1.0 / 1024.0, 1.0 / 4096.0))
    row_old = jnp.concatenate(
        [jnp.broadcast_to(one[...], (32, LANES)) for one in (row_mix, col_out, row_up, col_down)], 0
    ).T
    row_all = decay_rate * row_old + (1.0 - decay_rate) * row_sum * row_count
    row_new[...] = row_all
    row_flat[...] = row_all.T
    row_inverse = lax.rsqrt(row_all)
    row_lengths = (1024.0, 1024.0, 1024.0, 4096.0)
    square = jnp.zeros((1, 1), jnp.float32)
    factors = []
    for m in range(4):
        all_square, all_weight, all_old = (
            line_s[pl.ds(MISC + at // 8, 1), pl.ds(at % 8 * LANES, 1)] for at in (m, 4 + m, 8 + m)
        )
        average = decay_rate * all_old / row_lengths[m] + (1.0 - decay_rate) * all_square / SIZES[m]
        block = jnp.zeros((128, 128), jnp.float32)
        for t in TILES[m]:
            update = tile_of(t) * lax.rsqrt(col_of(new_cols, t)[...])
            block += update * update
        by_row = row_inverse[:, 32 * m : 32 * m + 1]
        per_row = jnp.sum(block, 1, keepdims=True) * by_row * by_row
        square += jnp.sum(per_row, 0, keepdims=True) * average
        factors.append((jnp.sqrt(average), jnp.sqrt(all_weight / SIZES[m])))
    spot = (z * 2 + y) * 2 + c
    last_s[...] = jnp.broadcast_to(square, (8, LANES))
    last_r[pl.ds(spot, 1)] = last_s[...][None]
    hops = [
        remote(last_s, last_r.at[spot], l_ss.at[at], l_rs.at[at], peer)
        for at, peer in enumerate(square_peers)
    ]
    for hop in hops:
        hop.start()
    for hop in hops:
        hop.wait()
    square = jnp.zeros((1, 1), jnp.float32)
    for at in range(16):
        square += last_r[at, 0:1, 0:1]
    vec_square = jnp.sum(jnp.sum(vec_step * vec_step, 1, keepdims=True), 0, keepdims=True)
    old_vecs = vecs[...]
    vec_size = VECS * 1024.0
    vec_mean = jnp.sum(jnp.sum(old_vecs * old_vecs, 1, keepdims=True), 0, keepdims=True) / vec_size
    count = sum(SIZES) + vec_size
    shrink = 1.0 / jnp.maximum(1.0, jnp.sqrt((square + vec_square) / count) / clip_level)
    vec_new[...] = old_vecs - step_rate * jnp.sqrt(vec_mean) * vec_step * shrink
    for m in range(4):
        scale[pl.ds(m, 1), :] = jnp.broadcast_to(
            step_rate * factors[m][0] * factors[m][1] * shrink, (1, LANES)
        )
    scale[pl.ds(4, 4), :] = jnp.zeros((4, LANES), jnp.float32)


def factor_all(*arrays):
    dma = pltpu.SemaphoreType.DMA
    full = jnp.float32
    in_vmem = pl.BlockSpec(memory_space=pltpu.VMEM)
    shape = jax.ShapeDtypeStruct
    shapes = [(128, 128), (128, 128), (3, WIDE), (4, LANES), (16, LANES), (16, LANES)]
    shapes += [(VECS, 1024)] * 3 + [(8, LANES)]
    return pl.pallas_call(
        factor_body,
        out_shape=tuple(shape(one, full) for one in shapes),
        in_specs=[in_vmem] * len(arrays),
        out_specs=(in_vmem,) * len(shapes),
        scratch_shapes=[
            pltpu.VMEM((16, 1024), full),
            pltpu.VMEM((16, 1024), full),
            pltpu.VMEM((128, 128), full),
            pltpu.VMEM((128, 128), full),
            pltpu.VMEM((16, 1024), full),
            pltpu.VMEM((24, 1024), full),
            pltpu.VMEM((4, 24, 1024), full),
            pltpu.VMEM((24, 1024), full),
            pltpu.VMEM((8, LANES), full),
            pltpu.VMEM((16, 8, LANES), full),
            dma((2,)), dma((2,)), dma((1,)), dma((1,)), dma((3,)), dma((3,)), dma((1,)), dma((1,)),
            dma((15,)), dma((15,)),
        ],
        compiler_params=pltpu.CompilerParams(
            collective_id=3, has_side_effects=True, vmem_limit_bytes=40 * MIB
        ),
    )(*arrays)


def finish_body(
    total_q, total_m, mix_w, out_w, up_w, down_w, row_new, row_flat, new_mix, new_out, new_up, new_down,
    vec_grad, vec_moment, vec_new, scale, *outs,
):
    grads, news, copies, smalls = outs[:4], outs[4:8], outs[8:12], outs[12:]
    at = pl.program_id(0)

    def by_row(m):
        return lax.rsqrt(row_new[:, 32 * m : 32 * m + 1])

    def by_col(row, m):
        return lax.rsqrt(row) * scale[pl.ds(m, 1), :]

    def put(m, index, grad, old, update):
        new = old - grad * update
        grads[m][index] = grad
        news[m][index] = new
        copies[m][index] = new.astype(jnp.bfloat16)

    everything = slice(None)
    for part in range(3):
        cols = new_mix[pl.ds(part, 1), columns(at * LANES, LANES)]
        grad = total_q[0, :, pl.ds(part * LANES, LANES)]
        put(0, (part, everything, everything), grad, mix_w[part], by_row(0) * by_col(cols, 0))
    turned_out = lax.rsqrt(row_flat[pl.ds(32, 1), :])
    turned_down = lax.rsqrt(row_flat[pl.ds(96, 1), :])
    cols = jnp.broadcast_to(by_col(new_out[pl.ds(at, 1), :], 1), (LANES, LANES)).T
    grad = total_q[0, :, pl.ds(3 * LANES, LANES)].T
    put(1, (everything, everything), grad, out_w[...], cols * turned_out)
    for part in range(4):
        here = pl.ds(part * LANES, LANES)
        row = pl.ds(at * 4 + part, 1)
        put(
            2, (everything, here), total_m[0, :, here], up_w[:, here],
            by_row(2) * by_col(new_up[row, :], 2),
        )
        cols = jnp.broadcast_to(by_col(new_down[row, :], 3), (LANES, LANES)).T
        put(3, (here, everything), total_m[1, :, here].T, down_w[here, :], cols * turned_down)
    for target, source in zip(smalls[:7], (vec_grad, vec_moment, vec_new, new_mix, new_out, new_up, new_down)):
        target[...] = source[...]
    for m, target in enumerate(smalls[7:]):
        target[...] = row_flat[pl.ds(32 * m, 1), :]


def finish_all(total_q, total_m, weights, factors):
    low, full = jnp.bfloat16, jnp.float32
    shape = jax.ShapeDtypeStruct
    blocks = [
        pl.BlockSpec((3, 128, LANES), lambda at: (0, 0, at)),
        pl.BlockSpec((LANES, 128), lambda at: (at, 0)),
        pl.BlockSpec((128, WIDE), lambda at: (0, at)),
        pl.BlockSpec((WIDE, 128), lambda at: (at, 0)),
    ]

    def whole(array_shape):
        return pl.BlockSpec(array_shape, lambda at: (0,) * len(array_shape))

    smalls = [(VECS, 1024)] * 3 + [(3, WIDE), (4, LANES), (16, LANES), (16, LANES)] + [(1, LANES)] * 4
    shapes = [shape(one.shape, kind) for kind in (full, full, low) for one in weights]
    shapes += [shape(one, full) for one in smalls]
    return pl.pallas_call(
        finish_body,
        grid=(4,),
        out_shape=tuple(shapes),
        in_specs=[
            pl.BlockSpec((1, 128, WIDE), lambda at: (at, 0, 0)),
            pl.BlockSpec((2, 128, WIDE), lambda at: (at, 0, 0)),
        ] + blocks + [whole(one.shape) for one in factors],
        out_specs=tuple(blocks * 3 + [whole(one) for one in smalls]),
        compiler_params=pltpu.CompilerParams(vmem_limit_bytes=40 * MIB),
    )(total_q, total_m, *weights, *factors)


def fast_body(
    inputs, cotangent, key_mask, image_mask, qkv_weight, out_weight, up_weight, down_weight,
    vectors, row_qkv, col_qkv, row_out, col_out, row_up, col_up, row_down, col_down, vector_moments,
):
    images, tokens, width = inputs.shape
    pad = ((0, 0), (0, SLOTS - tokens), (0, 0))
    weight_rows = (key_mask * image_mask[:, None]).astype(jnp.bfloat16)
    x_in = jnp.pad(inputs, pad)
    b_in = jnp.pad(cotangent * weight_rows[:, :, None], pad)
    counts = jnp.sum(key_mask, 1).astype(jnp.float32)
    n_in = jnp.broadcast_to(counts[:, None, None], (images, 8, LANES))
    weights = (qkv_weight.transpose(1, 0, 2), out_weight, up_weight, down_weight)
    w, b_all, x_all, n_all, qkv, heads, hidden, second, squares = front_all(
        x_in, b_in, n_in, weights, vectors
    )
    total_m, total_q, out_spread, grad_spread, bias_grad, vec_sums, qv_sums = back_all(
        w, second, b_all.reshape(ROWS, width), x_all, hidden, n_all, qkv, heads, vectors
    )
    factors = factor_all(
        total_q, total_m, squares, vec_sums, qv_sums, bias_grad, vectors, vector_moments,
        row_qkv.reshape(1, LANES), col_out.reshape(1, LANES), row_up.reshape(1, LANES),
        col_down.reshape(1, LANES), col_qkv, row_out.reshape(4, LANES), col_up.reshape(16, LANES),
        row_down.reshape(16, LANES),
    )
    done = finish_all(total_q, total_m, weights, factors)

    def natural(four):
        return (four[0].transpose(1, 0, 2),) + tuple(four[1:])

    vector_grad, vector_moment, vector_new, new_mix, new_out, new_up, new_down = done[12:19]
    rows = [one.reshape(-1) for one in done[19:]]
    return (
        (out_spread[:, :tokens], grad_spread[:, :tokens])
        + natural(done[:4])
        + (vector_grad,)
        + natural(done[4:8])
        + (vector_new,)
        + natural(done[8:12])
        + (
            rows[0], new_mix, new_out.reshape(-1), rows[1], rows[2], new_up.reshape(-1),
            new_down.reshape(-1), rows[3], vector_moment,
        )
    )


def pick_body(*arrays):
    sizes = tuple(lax.axis_size(name) for name in ("fsdp", "ctx", "tp"))
    if sizes == (8, 2, 2) and arrays[0].shape == (4, 290, 1024) and arrays[6].shape == (128, 2048):
        return fast_body(*arrays)
    return body(*arrays)


def solution(mesh):
    placed = (
        P("fsdp", "ctx", None),
        P("fsdp", "ctx", None),
        P("fsdp", "ctx"),
        P("fsdp"),
        P("fsdp", None, "tp"),
        P("tp", "fsdp"),
        P("fsdp", "tp"),
        P("tp", "fsdp"),
        P(),
        P("fsdp"),
        P(None, "tp"),
        P("tp"),
        P("fsdp"),
        P("fsdp"),
        P("tp"),
        P("tp"),
        P("fsdp"),
        P(),
    )
    return jax.shard_map(
        pick_body,
        mesh=mesh,
        in_specs=placed,
        out_specs=(
            P("fsdp", "ctx", None),
            P("fsdp", "ctx", None),
            P("fsdp", None, "tp"),
            P("tp", "fsdp"),
            P("fsdp", "tp"),
            P("tp", "fsdp"),
            P(),
            P("fsdp", None, "tp"),
            P("tp", "fsdp"),
            P("fsdp", "tp"),
            P("tp", "fsdp"),
            P(),
            P("fsdp", None, "tp"),
            P("tp", "fsdp"),
            P("fsdp", "tp"),
            P("tp", "fsdp"),
            P("fsdp"),
            P(None, "tp"),
            P("tp"),
            P("fsdp"),
            P("fsdp"),
            P("tp"),
            P("tp"),
            P("fsdp"),
            P(),
        ),
        check_vma=False,
    )
```

```python
import jax
import jax.numpy as jnp
from jax import lax
from jax.experimental import pallas as pl
from jax.experimental.pallas import tpu as pltpu
from jax.sharding import PartitionSpec as P

HD = 64
FF = 4096


eps_norm = 1e-06
decay_rate = 0.5
clip_level = 0.1
step_rate = 5.0


def norm_rows(rows, scale_row, offset):
    row_mean = jnp.mean(rows, -1, keepdims=True)
    centered = rows - row_mean
    inverse = lax.rsqrt(jnp.mean(centered * centered, -1, keepdims=True) + eps_norm)
    normal = centered * inverse
    return (normal * scale_row + offset, normal, inverse)


def norm_back(grad_rows, normal, inverse, scale_row):
    scaled = grad_rows * scale_row
    first_term = jnp.mean(scaled, -1, keepdims=True)
    second_term = jnp.mean(scaled * normal, -1, keepdims=True)
    return inverse * (scaled - first_term - normal * second_term)


def gelu_erf(argument):
    return 0.5 * argument * (1.0 + lax.erf(argument * 0.7071067811865476))


def gelu_slope(argument):
    return (
        0.5 * (1.0 + lax.erf(argument * 0.7071067811865476))
        + argument * jnp.exp(-0.5 * argument * argument) * 0.3989422804014327
    )


def masked_scores(queries, key_rows, valid_keys):
    scale_qk = queries.shape[-1] ** (-0.5)
    scores = (
        jnp.einsum("gqhe,gkhe->ghqk", queries, key_rows, preferred_element_type=jnp.float32)
        * scale_qk
    )
    return jnp.where(valid_keys[:, None, None, :] > 0, scores, -1000000000.0)


def attend_forward(pieces):
    queries, key_rows, value_rows, valid_keys = pieces
    scores = masked_scores(queries, key_rows, valid_keys)
    row_max = jnp.max(scores, -1, keepdims=True)
    exponent = jnp.exp(scores - row_max)
    totals = jnp.sum(exponent, -1, keepdims=True)
    attention = (exponent / totals).astype(jnp.bfloat16)
    attended = jnp.einsum(
        "ghqk,gkhe->gqhe", attention, value_rows, preferred_element_type=jnp.float32
    )
    return (attended.astype(jnp.bfloat16), (row_max + jnp.log(totals))[..., 0])


def attend_back(pieces):
    queries, key_rows, value_rows, valid_keys, logsum, grad_heads = pieces
    scale_qk = queries.shape[-1] ** (-0.5)
    scores = masked_scores(queries, key_rows, valid_keys)
    attention = jnp.exp(scores - logsum[..., None])
    grad_attention = jnp.einsum(
        "gqhe,gkhe->ghqk", grad_heads, value_rows, preferred_element_type=jnp.float32
    )
    inner = jnp.sum(attention * grad_attention, -1, keepdims=True)
    grad_scores = (attention * (grad_attention - inner)).astype(jnp.bfloat16)
    grad_queries = (
        jnp.einsum("ghqk,gkhe->gqhe", grad_scores, key_rows, preferred_element_type=jnp.float32)
        * scale_qk
    ).astype(jnp.bfloat16)
    grad_keys = (
        jnp.einsum("ghqk,gqhe->gkhe", grad_scores, queries, preferred_element_type=jnp.float32)
        * scale_qk
    )
    grad_values = jnp.einsum(
        "ghqk,gqhe->gkhe",
        attention.astype(jnp.bfloat16),
        grad_heads,
        preferred_element_type=jnp.float32,
    )
    return (grad_queries, grad_keys, grad_values)


def place_at(piece, full_shape, start, axis):
    return lax.dynamic_update_slice_in_dim(jnp.zeros(full_shape, jnp.float32), piece, start, axis)


def factor_local(
    grad_local, rows_old, cols_old, rows_full, rows_here, cols_here, row_total, col_total, old_total
):
    rows_new = decay_rate * rows_old + (1.0 - decay_rate) * rows_here / col_total
    cols_new = decay_rate * cols_old + (1.0 - decay_rate) * cols_here / row_total
    rows_avg = decay_rate * old_total / row_total + (1.0 - decay_rate) * jnp.sum(rows_full) / (
        row_total * col_total
    )
    update = grad_local * lax.rsqrt(rows_new[:, None] * cols_new[None, :] / rows_avg)
    return (rows_new, cols_new, update)


def body(
    inputs,
    cotangent,
    key_mask,
    image_mask,
    qkv_weight,
    out_weight,
    up_weight,
    down_weight,
    vectors,
    row_qkv,
    col_qkv,
    row_out,
    col_out,
    row_up,
    col_up,
    row_down,
    col_down,
    vector_moments,
):
    images, local_tokens, model_width = inputs.shape
    rows_here = images * local_tokens
    width_piece = qkv_weight.shape[0]
    half_width = qkv_weight.shape[2]
    half_hidden = up_weight.shape[1]
    head_size = HD
    heads_here = half_width // head_size
    tp_index = lax.axis_index("tp")
    fsdp_index = lax.axis_index("fsdp")
    tp_first = (tp_index == 0).astype(jnp.float32)
    ctx_first = (lax.axis_index("ctx") == 0).astype(jnp.float32)
    fsdp_first = (fsdp_index == 0).astype(jnp.float32)
    mix_w, out_w, up_w, down_w = (
        lax.all_gather(qkv_weight.astype(jnp.bfloat16), "fsdp", axis=0, tiled=True),
        lax.all_gather(out_weight.astype(jnp.bfloat16), "fsdp", axis=1, tiled=True),
        lax.all_gather(up_weight.astype(jnp.bfloat16), "fsdp", axis=0, tiled=True),
        lax.all_gather(down_weight.astype(jnp.bfloat16), "fsdp", axis=1, tiled=True),
    )
    query_bias = lax.dynamic_slice_in_dim(vectors[2], tp_index * half_width, half_width)
    value_bias = lax.dynamic_slice_in_dim(vectors[3], tp_index * half_width, half_width)
    up_bias = lax.dynamic_slice_in_dim(vectors[8:].reshape(-1), tp_index * half_hidden, half_hidden)
    flat_rows = inputs.astype(jnp.float32).reshape(rows_here, model_width)
    normed, normal_one, inverse_one = norm_rows(flat_rows, vectors[0], vectors[1])
    normed_low = normed.astype(jnp.bfloat16)
    projected = jnp.einsum("td,dcn->tcn", normed_low, mix_w, preferred_element_type=jnp.float32)
    queries = (projected[:, 0] + query_bias).astype(jnp.bfloat16)
    key_low = projected[:, 1].astype(jnp.bfloat16).reshape(images, local_tokens, half_width)
    value_low = (
        (projected[:, 2] + value_bias)
        .astype(jnp.bfloat16)
        .reshape(images, local_tokens, half_width)
    )
    all_keys, all_values, all_valid = (
        lax.all_gather(key_low, "ctx", axis=1, tiled=True),
        lax.all_gather(value_low, "ctx", axis=1, tiled=True),
        lax.all_gather(key_mask.astype(jnp.bfloat16), "ctx", axis=1, tiled=True),
    )
    seq_all = all_keys.shape[1]
    group_size = min(2, images)
    groups = images // group_size

    def grouped(array):
        return array.reshape((groups, group_size) + array.shape[1:])

    query_heads = grouped(queries.reshape(images, local_tokens, heads_here, head_size))
    key_heads = grouped(all_keys.reshape(images, seq_all, heads_here, head_size))
    value_heads = grouped(all_values.reshape(images, seq_all, heads_here, head_size))
    valid_groups = grouped(all_valid)
    attended, logsum = lax.map(attend_forward, (query_heads, key_heads, value_heads, valid_groups))
    heads_low = attended.reshape(rows_here, half_width)
    branch = (
        lax.psum(
            jnp.dot(heads_low, out_w, preferred_element_type=jnp.float32).astype(jnp.bfloat16), "tp"
        ).astype(jnp.float32)
        + vectors[4]
    )
    hidden = flat_rows + branch
    second, normal_two, inverse_two = norm_rows(hidden, vectors[5], vectors[6])
    second_low = second.astype(jnp.bfloat16)
    pre_active = jnp.dot(second_low, up_w, preferred_element_type=jnp.float32) + up_bias
    active_low = gelu_erf(pre_active).astype(jnp.bfloat16)
    mlp_sum = lax.psum(
        jnp.dot(active_low, down_w, preferred_element_type=jnp.float32).astype(jnp.bfloat16), "tp"
    ).astype(jnp.float32)
    output = (
        (hidden + mlp_sum + vectors[7])
        .astype(jnp.bfloat16)
        .reshape(images, local_tokens, model_width)
    )
    weight_rows = key_mask.astype(jnp.float32) * image_mask.astype(jnp.float32)[:, None]
    back = (cotangent.astype(jnp.float32) * weight_rows[:, :, None]).reshape(rows_here, model_width)
    back_low = back.astype(jnp.bfloat16)
    grad_active = jnp.einsum("td,fd->tf", back_low, down_w, preferred_element_type=jnp.float32)
    grad_pre = (grad_active * gelu_slope(pre_active)).astype(jnp.bfloat16)
    grad_down = jnp.einsum("tf,td->fd", active_low, back_low, preferred_element_type=jnp.float32)
    grad_up = jnp.einsum("td,tf->df", second_low, grad_pre, preferred_element_type=jnp.float32)
    grad_up_bias = jnp.sum(grad_pre.astype(jnp.float32), 0)
    grad_second = lax.psum(
        jnp.einsum("tf,df->td", grad_pre, up_w, preferred_element_type=jnp.float32).astype(
            jnp.bfloat16
        ),
        "tp",
    ).astype(jnp.float32)
    grad_hidden = back + norm_back(grad_second, normal_two, inverse_two, vectors[5])
    grad_branch = grad_hidden.astype(jnp.bfloat16)
    grad_out = jnp.einsum("tn,td->nd", heads_low, grad_branch, preferred_element_type=jnp.float32)
    grad_heads = jnp.einsum(
        "td,nd->tn", grad_branch, out_w, preferred_element_type=jnp.float32
    ).astype(jnp.bfloat16)
    grad_head_groups = grouped(grad_heads.reshape(images, local_tokens, heads_here, head_size))
    grad_queries, grad_keys, grad_values = lax.map(
        attend_back, (query_heads, key_heads, value_heads, valid_groups, logsum, grad_head_groups)
    )
    key_grads, value_grads = (
        lax.psum_scatter(
            grad_keys.reshape(images, seq_all, half_width).astype(jnp.bfloat16),
            "ctx",
            scatter_dimension=1,
            tiled=True,
        ).astype(jnp.float32),
        lax.psum_scatter(
            grad_values.reshape(images, seq_all, half_width).astype(jnp.bfloat16),
            "ctx",
            scatter_dimension=1,
            tiled=True,
        ).astype(jnp.float32),
    )
    grad_projected = jnp.stack(
        [
            grad_queries.reshape(rows_here, half_width),
            key_grads.reshape(rows_here, half_width).astype(jnp.bfloat16),
            value_grads.reshape(rows_here, half_width).astype(jnp.bfloat16),
        ],
        1,
    )
    grad_mix = jnp.einsum(
        "td,tcn->dcn", normed_low, grad_projected, preferred_element_type=jnp.float32
    )
    grad_normed = lax.psum(
        jnp.einsum("tcn,dcn->td", grad_projected, mix_w, preferred_element_type=jnp.float32).astype(
            jnp.bfloat16
        ),
        "tp",
    ).astype(jnp.float32)
    input_grad = (
        (grad_hidden + norm_back(grad_normed, normal_one, inverse_one, vectors[0]))
        .astype(jnp.bfloat16)
        .reshape(images, local_tokens, model_width)
    )
    projected_sums = jnp.sum(grad_projected.astype(jnp.float32), 0)
    vector_part = jnp.concatenate(
        [
            jnp.stack(
                [
                    jnp.sum(grad_normed * normal_one, 0) * tp_first,
                    jnp.sum(grad_normed, 0) * tp_first,
                    place_at(projected_sums[0], (model_width,), tp_index * half_width, 0),
                    place_at(projected_sums[2], (model_width,), tp_index * half_width, 0),
                    jnp.sum(grad_branch.astype(jnp.float32), 0) * tp_first,
                    jnp.sum(grad_second * normal_two, 0) * tp_first,
                    jnp.sum(grad_second, 0) * tp_first,
                    jnp.sum(back, 0) * tp_first,
                ]
            ),
            place_at(grad_up_bias, (FF,), tp_index * half_hidden, 0).reshape(-1, model_width),
        ],
        0,
    )
    shards = (
        lax.psum_scatter(grad_mix, "fsdp", scatter_dimension=0, tiled=True),
        lax.psum_scatter(grad_out, "fsdp", scatter_dimension=1, tiled=True),
        lax.psum_scatter(grad_up, "fsdp", scatter_dimension=0, tiled=True),
        lax.psum_scatter(grad_down, "fsdp", scatter_dimension=1, tiled=True),
    )
    sum_mix, sum_out, sum_up, sum_down = (
        lax.psum(shards[0].astype(jnp.bfloat16), "ctx").astype(jnp.float32),
        lax.psum(shards[1].astype(jnp.bfloat16), "ctx").astype(jnp.float32),
        lax.psum(shards[2].astype(jnp.bfloat16), "ctx").astype(jnp.float32),
        lax.psum(shards[3].astype(jnp.bfloat16), "ctx").astype(jnp.float32),
    )
    fsdp_start = fsdp_index * width_piece
    tp_width = tp_index * half_width
    tp_hidden = tp_index * half_hidden
    mix_square = sum_mix * sum_mix
    out_square = sum_out * sum_out
    up_square = sum_up * sum_up
    down_square = sum_down * sum_down
    scalar_part = (
        jnp.stack(
            [
                jnp.sum(qkv_weight * qkv_weight),
                jnp.sum(out_weight * out_weight),
                jnp.sum(up_weight * up_weight),
                jnp.sum(down_weight * down_weight),
                jnp.sum(row_qkv) * tp_first,
                jnp.sum(row_out) * fsdp_first,
                jnp.sum(row_up) * tp_first,
                jnp.sum(row_down) * fsdp_first,
            ]
        )
        * ctx_first
    )
    (
        vector_grad,
        rows_mix,
        cols_mix,
        rows_out,
        cols_out,
        rows_up,
        cols_up,
        rows_down,
        cols_down,
        scalar_sums,
    ) = lax.psum(
        (
            vector_part,
            place_at(jnp.sum(mix_square, (1, 2)), (model_width,), fsdp_start, 0) * ctx_first,
            place_at(jnp.sum(mix_square, 0), (3, model_width), tp_width, 1) * ctx_first,
            place_at(jnp.sum(out_square, 1), (model_width,), tp_width, 0) * ctx_first,
            place_at(jnp.sum(out_square, 0), (model_width,), fsdp_start, 0) * ctx_first,
            place_at(jnp.sum(up_square, 1), (model_width,), fsdp_start, 0) * ctx_first,
            place_at(jnp.sum(up_square, 0), (FF,), tp_hidden, 0) * ctx_first,
            place_at(jnp.sum(down_square, 1), (FF,), tp_hidden, 0) * ctx_first,
            place_at(jnp.sum(down_square, 0), (model_width,), fsdp_start, 0) * ctx_first,
            scalar_part,
        ),
        ("fsdp", "ctx", "tp"),
    )
    qkv_rows, qkv_cols_flat, mix_update = factor_local(
        sum_mix.reshape(width_piece, -1),
        row_qkv,
        col_qkv.reshape(-1),
        rows_mix,
        lax.dynamic_slice_in_dim(rows_mix, fsdp_start, width_piece),
        lax.dynamic_slice_in_dim(cols_mix, tp_width, half_width, 1).reshape(-1),
        model_width,
        3 * model_width,
        scalar_sums[4],
    )
    out_rows, out_cols, out_update = factor_local(
        sum_out,
        row_out,
        col_out,
        rows_out,
        lax.dynamic_slice_in_dim(rows_out, tp_width, half_width),
        lax.dynamic_slice_in_dim(cols_out, fsdp_start, width_piece),
        model_width,
        model_width,
        scalar_sums[5],
    )
    up_rows, up_cols, up_update = factor_local(
        sum_up,
        row_up,
        col_up,
        rows_up,
        lax.dynamic_slice_in_dim(rows_up, fsdp_start, width_piece),
        lax.dynamic_slice_in_dim(cols_up, tp_hidden, half_hidden),
        model_width,
        FF,
        scalar_sums[6],
    )
    down_rows, down_cols, down_update = factor_local(
        sum_down,
        row_down,
        col_down,
        rows_down,
        lax.dynamic_slice_in_dim(rows_down, tp_hidden, half_hidden),
        lax.dynamic_slice_in_dim(cols_down, fsdp_start, width_piece),
        FF,
        model_width,
        scalar_sums[7],
    )
    vector_moment = decay_rate * vector_moments + (1.0 - decay_rate) * vector_grad * vector_grad
    vector_step = vector_grad * lax.rsqrt(vector_moment)
    local_square = (
        jnp.sum(mix_update * mix_update)
        + jnp.sum(out_update * out_update)
        + jnp.sum(up_update * up_update)
        + jnp.sum(down_update * down_update)
    )
    global_square = lax.psum(local_square, ("fsdp", "tp")) + jnp.sum(vector_step * vector_step)
    param_count = 4 * model_width * model_width + 2 * model_width * FF + vectors.size
    shrink = 1.0 / jnp.maximum(1.0, jnp.sqrt(global_square / param_count) / clip_level)
    qkv_new = (
        qkv_weight
        - step_rate
        * jnp.sqrt(scalar_sums[0] / (3 * model_width * model_width))
        * mix_update.reshape(qkv_weight.shape)
        * shrink
    )
    out_new = (
        out_weight
        - step_rate * jnp.sqrt(scalar_sums[1] / (model_width * model_width)) * out_update * shrink
    )
    up_new = (
        up_weight - step_rate * jnp.sqrt(scalar_sums[2] / (model_width * FF)) * up_update * shrink
    )
    down_new = (
        down_weight
        - step_rate * jnp.sqrt(scalar_sums[3] / (model_width * FF)) * down_update * shrink
    )
    vector_new = vectors - step_rate * jnp.sqrt(jnp.mean(vectors * vectors)) * vector_step * shrink
    return (
        output,
        input_grad,
        sum_mix,
        sum_out,
        sum_up,
        sum_down,
        vector_grad,
        qkv_new,
        out_new,
        up_new,
        down_new,
        vector_new,
        qkv_new.astype(jnp.bfloat16),
        out_new.astype(jnp.bfloat16),
        up_new.astype(jnp.bfloat16),
        down_new.astype(jnp.bfloat16),
        qkv_rows,
        qkv_cols_flat.reshape(3, half_width),
        out_rows,
        out_cols,
        up_rows,
        up_cols,
        down_rows,
        down_cols,
        vector_moment,
    )


MESH = pl.DeviceIdType.MESH
LANES = 128
SLOTS = 320
ROWS = 2 * SLOTS
WIDE = 512
CHUNKS = 12
PAIRS = 8
MIB = 1024 * 1024


def place():
    shard = lax.axis_index("fsdp")
    return (lax.div(shard, 2), lax.rem(shard, 2), lax.axis_index("ctx"), lax.axis_index("tp"))


def peers_of(z, y, x, c):
    line = [(lax.rem(z + step, 4) * 2 + y, x, c) for step in (1, 2, 3)]
    return (line, (z * 2 + 1 - y, x, c), (z * 2 + y, 1 - x, c), (z * 2 + y, x, 1 - c))


def greet(peers):
    barrier = pltpu.get_barrier_semaphore()
    for peer in peers:
        pl.semaphore_signal(barrier, inc=1, device_id=peer, device_id_type=MESH)
    pl.semaphore_wait(barrier, len(peers))


def remote(src, dst, send, recv, peer):
    return pltpu.make_async_remote_copy(
        src_ref=src, dst_ref=dst, send_sem=send, recv_sem=recv, device_id=peer, device_id_type=MESH
    )


def nn(left, right):
    return lax.dot_general(left, right, (((1,), (0,)), ((), ())), preferred_element_type=jnp.float32)


def nt(left, right):
    return lax.dot_general(left, right, (((1,), (1,)), ((), ())), preferred_element_type=jnp.float32)


def aligned(start, size, unit):
    if isinstance(start, int):
        return pl.ds(start, size)
    return pl.ds(pl.multiple_of(start, unit), size)


def columns(start, size):
    return aligned(start, size, LANES)


def slots_valid(counts, axis):
    shape = (1, ROWS) if axis else (ROWS, 1)
    slot = lax.broadcasted_iota(jnp.int32, shape, axis)
    first = counts[0, 0:1, 0:1].astype(jnp.int32)
    second = counts[1, 0:1, 0:1].astype(jnp.int32)
    return ((slot < SLOTS) & (slot < first)) | ((slot >= SLOTS) & (slot - SLOTS < second))


def square_sum(ref):
    flat = ref if len(ref.shape) == 2 else ref.reshape(ref.shape[0] * ref.shape[1], ref.shape[2])
    step = flat.shape[0] // 8

    def add(at, total):
        values = flat[pl.ds(pl.multiple_of(at * step, step), step), :]
        return total + jnp.sum(values * values, 0, keepdims=True)

    total = lax.fori_loop(0, 8, add, jnp.zeros((1, flat.shape[1]), jnp.float32))
    return jnp.sum(total, 1, keepdims=True)


def arrival_time(event):
    kind, k = event
    return k + kind * (1.1 if k < 2 else 2.1)


ARRIVALS = sorted(((kind, k) for k in range(CHUNKS) for kind in range(4)), key=arrival_time)


def transpose_into(target, source):
    for at in range(source.shape[1] // LANES):
        target[pl.ds(at * LANES, LANES), :] = source[:, pl.ds(at * LANES, LANES)].T


def front_body(
    x_in, b_in, n_in, mix_w, out_w, up_w, down_w, vectors,
    kept, g_out, b_out, x_out, n_out, qkv, heads, hidden, squares, grad_second, image_out, bias_grad,
    normed, w, wo, normed_t, back_t, halves, total_acc, staged,
    local, in_s, in_r, zs, zr, ys, yr, xs, xr, cs, cr, ws, gs,
):
    z, y, x, c = place()
    line, y_peer, x_peer, c_peer = peers_of(z, y, x, c)
    own = []
    mine, theirs = 2 * x + c, 2 * (1 - x) + c
    pairs = ((x_in, x_out), (n_in, n_out), (b_in, b_out))
    for at, (src, dst) in enumerate(pairs):
        own.append(pltpu.make_async_copy(src.at[mine], dst.at[x], local.at[at]))
    for copy in own:
        copy.start()
    low = jnp.bfloat16
    for k in range(4):
        lanes = pl.ds(k * LANES, LANES)
        for part in range(3):
            w[k, c, z, y, :, pl.ds(part * LANES, LANES)] = mix_w[part, :, lanes].astype(low)
        w[k, c, z, y, :, pl.ds(3 * LANES, LANES)] = out_w[lanes, :].T.astype(low)
        w[4 + 2 * k, c, z, y] = up_w[:, pl.ds(k * WIDE, WIDE)].astype(low)
        for part in range(4):
            rows = pl.ds(k * WIDE + part * LANES, LANES)
            w[5 + 2 * k, c, z, y, :, pl.ds(part * LANES, LANES)] = down_w[rows, :].T.astype(low)
    greet(line + [y_peer, x_peer, c_peer])
    swaps = [
        remote(src.at[theirs], dst.at[x], in_s.at[at], in_r.at[at], x_peer)
        for at, (src, dst) in enumerate(pairs)
    ]

    def share(odd):
        size = 96
        return aligned(x * (128 - size), size, 16), aligned(x * size, 128 - size, 16)

    def z_copies(k, odd):
        block = w.at[k, c, z, y, share(odd)[0]]
        return [remote(block, block, zs.at[k, at], zr.at[k, at], peer) for at, peer in enumerate(line)]

    def y_copies(k, odd):
        rows = share(odd)[0]
        blocks = [w.at[k, c, pl.ds(2 * at, 2), y, rows] for at in range(2)]
        return [remote(block, block, ys.at[k, at], yr.at[k, at], y_peer) for at, block in enumerate(blocks)]

    def x_copies(k, odd):
        rows = share(odd)[1]
        blocks = [w.at[k, c, at, :, rows] for at in range(4)]
        return [remote(block, block, xs.at[k, at], xr.at[k, at], x_peer) for at, block in enumerate(blocks)]

    def c_copies(k):
        blocks = [w.at[k, c, at] for at in range(4)]
        return [remote(block, block, cs.at[k, at], cr.at[k, at], c_peer) for at, block in enumerate(blocks)]

    def keep(k):
        return pltpu.make_async_copy(w.at[k], kept.at[k], ws.at[k])

    def start(copies):
        for copy in copies:
            copy.start()

    def arrive(copies):
        for copy in copies:
            copy.wait_recv()

    ahead = 2

    def serve(kind, k):
        odd = k % 2 == 1
        if kind == 0:
            arrive(z_copies(k, odd))
            start(y_copies(k, odd))
            if k + ahead < CHUNKS:
                start(z_copies(k + ahead, odd))
        elif kind == 1:
            arrive(y_copies(k, odd))
            start(x_copies(k, odd))
        elif kind == 2:
            arrive(x_copies(k, odd))
            start(c_copies(k))
        else:
            arrive(c_copies(k))
            if k < 4:
                keep(k).start()

    events = list(ARRIVALS)

    def serve_some(count):
        for _ in range(min(count, len(events))):
            serve(*events.pop(0))

    def serve_until(k):
        while (3, k) in events:
            serve(*events.pop(0))

    swaps[0].start()
    swaps[1].start()
    for t in range(ahead):
        start(z_copies(t, t % 2 == 1))
    own[0].wait()
    own[1].wait()

    def norm_first(half):
        @pl.loop(0, SLOTS // 64)
        def _(at):
            rows = pl.ds(pl.multiple_of(at * 64, 64), 64)
            result, _, _ = norm_rows(
                x_out[half, rows, :].astype(jnp.float32), vectors[0:1, :], vectors[1:2, :]
            )
            normed[aligned(half * SLOTS + at * 64, 64, 64), :] = result.astype(jnp.bfloat16)

    norm_first(x)
    for m, ref in enumerate((mix_w, out_w, up_w, down_w)):
        squares[pl.ds(m, 1), :] = jnp.broadcast_to(square_sum(ref), (1, LANES))
    serve_some(1)
    swaps[0].wait_recv()
    swaps[1].wait_recv()
    norm_first(1 - x)
    serve_until(0)
    swaps[2].start()
    valid = slots_valid(n_out, 1)
    lane = lax.broadcasted_iota(jnp.int32, (1, LANES), 1)

    def pair_task(side, k):
        pair = side * 4 + k
        weights = w[k, side].reshape(1024, WIDE)
        wo[:, columns(pair * LANES, LANES)] = weights[:, 3 * LANES :]
        weights = weights[:, : 3 * LANES]
        q_bias = vectors[2:3, columns(pair * LANES, LANES)]
        v_bias = vectors[3:4, columns(pair * LANES, LANES)]
        bias = jnp.concatenate([q_bias, jnp.zeros_like(q_bias), v_bias], 1)
        for half in range(2):
            qkv[pair, pl.ds(half * SLOTS, SLOTS), :] = (
                nn(normed[pl.ds(half * SLOTS, SLOTS), :], weights) + bias
            ).astype(
                jnp.bfloat16
            )

        @pl.loop(0, 2)
        def _(half):
            rows = pl.ds(pl.multiple_of(half * SLOTS, SLOTS), SLOTS)
            queries = qkv[pair, rows, pl.ds(0, LANES)] * jnp.bfloat16(0.125)
            keys = qkv[pair, :, pl.ds(LANES, LANES)]
            values = qkv[pair, :, pl.ds(2 * LANES, LANES)]
            results = []
            for at in range(2):
                here = (lane < HD) if at == 0 else (lane >= HD)
                scores = nt(jnp.where(here, queries, jnp.zeros_like(queries)), keys)
                scores = jnp.where(valid, scores, -1000000000.0)
                top = jnp.max(scores, 1, keepdims=True)
                exponent = jnp.exp(scores - top)
                attention = exponent * (1.0 / jnp.sum(exponent, 1, keepdims=True))
                results.append(nn(attention.astype(jnp.bfloat16), values))
            heads[rows, columns(pair * LANES, LANES)] = jnp.where(
                lane < HD, results[0], results[1]
            ).astype(jnp.bfloat16)

    for k in range(4):
        serve_until(k)
        pair_task(0, k)
        serve_some(3)
        pair_task(1, k)
        serve_some(3)

    for tile in range(4):
        for half in range(2):
            rows = pl.ds(half * SLOTS, SLOTS)
            cols = pl.ds(tile * 256, 256)
            branch = nt(heads[rows, :], wo[cols, :])
            hidden[rows, cols] = x_out[half, :, cols].astype(jnp.float32) + (branch + vectors[4:5, cols])
        serve_some(1)

    @pl.loop(0, ROWS // 64)
    def _(at):
        rows = pl.ds(pl.multiple_of(at * 64, 64), 64)
        result, _, _ = norm_rows(hidden[rows, :], vectors[5:6, :], vectors[6:7, :])
        normed[rows, :] = result.astype(jnp.bfloat16)
        total_acc[rows, :] = hidden[rows, :] + vectors[7:8, :]

    own[2].wait()
    swaps[2].wait_recv()
    transpose_into(normed_t, normed)
    for half in range(2):
        for at in range(1024 // LANES):
            lanes = pl.ds(at * LANES, LANES)
            back_t[lanes, pl.ds(half * SLOTS, SLOTS)] = b_out[half, :, lanes].T
    grad_second[...] = jnp.zeros_like(grad_second)

    def send_tile(s):
        j, side = (s // 2, s % 2) if isinstance(s, int) else (lax.div(s, 2), lax.rem(s, 2))
        return pltpu.make_async_copy(staged, g_out.at[pl.ds(2 * j, 2), side], gs.at[0])

    serve_until(5)
    shares = {}
    for s in range(7):
        mark = len(events)
        goal = [event for event in events if event[0] == 3 and event[1] <= 5 + 2 * ((s + 1) // 2)]
        taken = max([events.index(event) + 1 for event in goal] + [0])
        taken = max(taken, min(3, mark))
        shares[s] = events[:taken]
        del events[:taken]

    @pl.loop(0, 8)
    def _(s):
        j, side = lax.div(s, 2), lax.rem(s, 2)
        tile = side * 4 + j
        bias = vectors[pl.ds(8 + side * 2 + lax.div(j, 2), 1), columns(lax.rem(j, 2) * WIDE, WIDE)]
        up = w[4 + 2 * j, side].reshape(1024, WIDE)
        down = w[5 + 2 * j, side].reshape(1024, WIDE)
        sums = jnp.zeros((1, WIDE), jnp.float32)
        for half in range(2):
            rows = pl.ds(half * SLOTS, SLOTS)
            pre = nn(normed[rows, :], up) + bias
            grad_active = nn(b_out[half], down)
            share = 0.5 * (1.0 + lax.erf(pre * 0.7071067811865476))
            slope = share + pre * jnp.exp(-0.5 * pre * pre) * 0.3989422804014327
            act = (pre * share).astype(low)
            grad_pre = (grad_active * slope).astype(low)
            halves[0, rows, :] = act
            halves[1, rows, :] = grad_pre
            sums += jnp.sum(grad_pre.astype(jnp.float32), 0, keepdims=True)
            total_acc[rows, :] += nt(act, down)
            grad_second[rows, :] += nt(grad_pre, up)
        bias_grad[pl.ds(tile, 1), :] = sums

        @pl.when(s > 0)
        def _():
            send_tile(s).wait()

        for zi in range(2):
            rows = pl.ds(zi * 512, 512)
            staged[0, pl.ds(2 * zi, 2)] = nn(normed_t[rows, :], halves[1]).astype(low).reshape(2, 2, 128, WIDE)
            staged[1, pl.ds(2 * zi, 2)] = nn(back_t[rows, :], halves[0]).astype(low).reshape(2, 2, 128, WIDE)
        send_tile(s).start()
        for done, calls in shares.items():
            if calls:

                @pl.when(s == done)
                def _():
                    for call in calls:
                        serve(*call)

    for half in range(2):
        image_out[half] = total_acc[pl.ds(half * SLOTS, SLOTS), :].astype(low)
    send_tile(7).wait()
    for k in range(4):
        keep(k).wait()
    for swap in swaps:
        swap.wait_send()

    @pl.loop(0, CHUNKS // 2)
    def _(at):
        for odd in (False, True):
            k = 2 * at + int(odd)
            for copy in z_copies(k, odd) + y_copies(k, odd) + x_copies(k, odd) + c_copies(k):
                copy.wait_send()


def front_all(x_in, b_in, n_in, weights, vectors):
    dma = pltpu.SemaphoreType.DMA
    low, full = jnp.bfloat16, jnp.float32
    anywhere = pl.BlockSpec(memory_space=pl.ANY)
    in_vmem = pl.BlockSpec(memory_space=pltpu.VMEM)
    shape = jax.ShapeDtypeStruct
    width = x_in.shape[2]
    return pl.pallas_call(
        front_body,
        out_shape=(
            shape((4, 2, 4, 2, 128, WIDE), low),
            shape((8, 2, 4, 2, 128, WIDE), low),
            shape((2, SLOTS, width), low),
            shape((2, SLOTS, width), low),
            shape((2, 8, LANES), full),
            shape((PAIRS, ROWS, 3 * LANES), low),
            shape((ROWS, width), low),
            shape((ROWS, width), full),
            shape((8, LANES), full),
            shape((ROWS, width), full),
            shape((2, SLOTS, width), low),
            shape((8, WIDE), full),
        ),
        in_specs=[anywhere] * 3 + [in_vmem] * 5,
        out_specs=(anywhere, anywhere) + (in_vmem,) * 10,
        scratch_shapes=[
            pltpu.VMEM((ROWS, width), low),
            pltpu.VMEM((CHUNKS, 2, 4, 2, 128, WIDE), low),
            pltpu.VMEM((1024, 1024), low),
            pltpu.VMEM((width, ROWS), low),
            pltpu.VMEM((width, ROWS), low),
            pltpu.VMEM((2, ROWS, WIDE), low),
            pltpu.VMEM((ROWS, width), full),
            pltpu.VMEM((2, 4, 2, 128, WIDE), low),
            dma((3,)), dma((3,)), dma((3,)), dma((CHUNKS, 3)), dma((CHUNKS, 3)),
            dma((CHUNKS, 2)), dma((CHUNKS, 2)), dma((CHUNKS, 4)), dma((CHUNKS, 4)), dma((CHUNKS, 4)), dma((CHUNKS, 4)),
            dma((4,)), dma((1,)),
        ],
        compiler_params=pltpu.CompilerParams(
            collective_id=0, has_side_effects=True, vmem_limit_bytes=62 * MIB
        ),
    )(x_in, b_in, n_in, *weights, vectors)


def add_into(held, index, arrived, from_index):
    held[index] = (
        held[index].astype(jnp.float32) + arrived[from_index].astype(jnp.float32)
    ).astype(jnp.bfloat16)


class Scatter:
    def __init__(self, crosswise, refs):
        self.crosswise = crosswise
        self.where = place()
        self.line, self.y_peer, self.x_peer, self.c_peer = peers_of(*self.where)
        x = self.where[2]
        self.near = aligned(x * 64, 64, 64)
        self.far = aligned((1 - x) * 64, 64, 64)
        self.slot = [sum(k == crosswise[at] for k in crosswise[:at]) for at in range(len(crosswise))]
        (
            self.g, self.cb, self.xa, self.ya, self.za, self.fa, self.yb, self.zb, self.xb, self.stage,
            self.cs, self.cr, self.s1s, self.s1r, self.s2s, self.s2r, self.s3s, self.s3r, self.s4s, self.s4r,
            self.out_sem, self.free, self.in_sem, self.made,
        ) = refs[:24]
        self.totals = refs[24:]
        self.waited = set()

    def hops(self, stage, q):
        z, y, x, c = self.where
        at, own = self.slot[q], self.g.at[q]
        if stage == 0:
            c = self.where[3]
            source = self.made.at[q, 1 - c] if q < 8 else self.g.at[12 + q % 2]
            return [
                remote(source, self.cb.at[q % 4], self.cs.at[q], self.cr.at[q], self.c_peer)
            ]
        first, third = (self.s1s.at[q], self.s1r.at[q]), (self.s4s.at[q], self.s4r.at[q])
        second, last = (self.s2s.at[q], self.s2r.at[q]), (self.s3s.at[q], self.s3r.at[q])
        ahead = [lax.rem(z + d + 1, 4) for d in range(3)]
        if self.crosswise[q]:
            near = self.near
            if stage == 1:
                return [remote(own.at[:, :, self.far], self.xa.at[at], *first, self.x_peer)]
            if stage == 2:
                return [
                    remote(own.at[:, 1 - y, near], self.ya.at[at], second[0].at[0], second[1].at[0], self.y_peer)
                ]
            if stage == 3:
                return [
                    remote(own.at[to, y, near], self.za.at[at, d], last[0].at[d], last[1].at[d], peer)
                    for d, (to, peer) in enumerate(zip(ahead, self.line))
                ]
            return [remote(own.at[z, y, near], self.fa.at[at], *third, self.x_peer)]
        if stage == 1:
            return [remote(own.at[:, 1 - y], self.yb.at[at], *first, self.y_peer)]
        if stage == 2:
            return [
                remote(own.at[to, y], self.zb.at[at, d], second[0].at[d], second[1].at[d], peer)
                for d, (to, peer) in enumerate(zip(ahead, self.line))
            ]
        if stage == 3:
            return [remote(own.at[z, y], self.xb.at[at], last[0].at[0], last[1].at[0], self.x_peer)]
        return []

    def start(self, stage, q):
        for copy in self.hops(stage, q):
            copy.start()

    def arrive(self, stage, q):
        for copy in self.hops(stage, q):
            copy.wait_recv()

    def sent(self, q, stages):
        for stage in stages:
            self.waited.add((stage, q))
            for copy in self.hops(stage, q):
                copy.wait_send()

    def begin(self, q):
        if q < 8:
            self.load(q).start()
        if q >= 4:
            pl.semaphore_wait(self.free.at[q % 4], 1)
        self.start(0, q)

    def load(self, q):
        return pltpu.make_async_copy(self.made.at[q, self.where[3]], self.g.at[q], self.in_sem.at[q])

    def one(self, q):
        if q < 8:
            self.load(q).wait()
        self.arrive(0, q)

        @pl.loop(0, 8)
        def _(block):
            zi, yi = lax.div(block, 2), lax.rem(block, 2)
            add_into(self.g, (q, zi, yi), self.cb, (q % 4, zi, yi))

        if q < 8:
            pl.semaphore_signal(
                self.free.at[q % 4], inc=1, device_id=self.c_peer, device_id_type=MESH
            )

        self.start(1, q)

    def two(self, q):
        y, at = self.where[1], self.slot[q]
        self.arrive(1, q)
        if self.crosswise[q]:

            @pl.loop(0, 8)
            def _(block):
                zi, yi = lax.div(block, 2), lax.rem(block, 2)
                add_into(self.g, (q, zi, yi, self.near), self.xa, (at, zi, yi))

        else:

            @pl.loop(0, 4)
            def _(zi):
                add_into(self.g, (q, zi, y), self.yb, (at, zi))

        self.start(2, q)

    def sum_line(self, q, rows, buffer):
        z, y = self.where[:2]
        value = self.g[(q, z, y) + rows].astype(jnp.float32)
        for d in range(3):
            value += buffer[self.slot[q], d].astype(jnp.float32)
        self.g[(q, z, y) + rows] = value.astype(jnp.bfloat16)

    def three(self, q):
        y, at = self.where[1], self.slot[q]
        self.arrive(2, q)
        if self.crosswise[q]:

            @pl.loop(0, 4)
            def _(zi):
                add_into(self.g, (q, zi, y, self.near), self.ya, (at, zi))

        else:
            self.sum_line(q, (), self.zb)
        self.start(3, q)

    def export(self, q):
        target = self.totals[0].at[q] if q < 8 else self.totals[1].at[q - 8]
        return pltpu.make_async_copy(self.stage.at[q % 4], target, self.out_sem.at[q])

    def four(self, q):
        z, y = self.where[:2]
        at = self.slot[q]
        self.arrive(3, q)
        if self.crosswise[q]:
            self.sum_line(q, (self.near,), self.za)
            self.start(4, q)
        else:
            if q >= 4:
                self.export(q - 4).wait()
            self.stage[q % 4] = self.g[q, z, y].astype(jnp.float32) + self.xb[at].astype(jnp.float32)
            self.export(q).start()

    def five(self, q):
        z, y = self.where[:2]
        if self.crosswise[q]:
            self.arrive(4, q)
            if q >= 4:
                self.export(q - 4).wait()
            self.stage[q % 4, self.near] = self.g[q, z, y, self.near].astype(jnp.float32)
            self.stage[q % 4, self.far] = self.fa[self.slot[q]].astype(jnp.float32)
            self.export(q).start()

    def run(self, calls):
        for name, q in calls:
            getattr(self, name)(q)

    def finish(self):
        count = len(self.crosswise)
        for q in range(count - 4, count):
            self.export(q).wait()
        for stage in range(5):
            for q in range(count):
                if (stage, q) not in self.waited:
                    self.sent(q, (stage,))

    @staticmethod
    def scratch(crosswise):
        dma, vmem, low = pltpu.SemaphoreType.DMA, pltpu.VMEM, jnp.bfloat16
        n, across = len(crosswise), sum(crosswise)
        along = n - across
        return [
            vmem((14, 4, 2, 128, WIDE), low),
            vmem((4, 4, 2, 128, WIDE), low),
            vmem((across, 4, 2, 64, WIDE), low),
            vmem((across, 4, 64, WIDE), low),
            vmem((across, 3, 64, WIDE), low),
            vmem((across, 64, WIDE), low),
            vmem((along, 4, 128, WIDE), low),
            vmem((along, 3, 128, WIDE), low),
            vmem((along, 128, WIDE), low),
            vmem((4, 128, WIDE), jnp.float32),
            dma((n,)), dma((n,)), dma((n,)), dma((n,)), dma((n, 3)), dma((n, 3)),
            dma((n, 3)), dma((n, 3)), dma((n,)), dma((n,)), dma((n,)), pltpu.SemaphoreType.REGULAR((4,)), dma((8,)),
        ]


class Spread:
    def __init__(self, src, dst, sems):
        z, y, x, c = place()
        _, _, x_peer, c_peer = peers_of(z, y, x, c)
        mine, theirs = 2 * x + c, 2 * (1 - x) + c
        self.cross = remote(src.at[1 - x], dst.at[mine], sems.at[0], sems.at[1], x_peer)
        self.near = remote(src.at[x], dst.at[mine], sems.at[2], sems.at[3], c_peer)
        self.local = pltpu.make_async_copy(src.at[x], dst.at[mine], sems.at[4])
        self.onward = remote(dst.at[theirs], dst.at[theirs], sems.at[5], sems.at[6], c_peer)

    def start(self):
        self.near.start()
        self.local.start()

    def forward(self):
        self.cross.wait_recv()
        self.onward.start()

    def finish(self):
        self.cross.wait_send()
        self.near.wait()
        self.local.wait()
        self.onward.wait()


KINDS = (False, False, False, True, True, True, True, True, False, True, False, False)
PLAN = (
    (("begin", 2), ("begin", 0), ("begin", 1), ("begin", 3),),
    (),
    (),
    (("one", 2),),
    (("begin", 6),),
    (("one", 0),),
    (("begin", 4),),
    (("one", 1),),
    (("begin", 5), ("one", 3),),
    (("two", 2), ("begin", 7), ("one", 6),),
    (("one", 4),),
    (("two", 0), ("one", 5), ("two", 3), ("one", 7), ("begin", 8),),
    (("three", 2),),
    (("two", 1), ("two", 6), ("one", 8),),
    (("begin", 9),),
    (("three", 0), ("three", 3),),
    (("one", 9), ("three", 6), ("two", 4),),
    (("three", 1),),
    (("begin", 10),),
    (("four", 3), ("two", 5), ("two", 8),),
    (("four", 6), ("one", 10), ("three", 4),),
    (("three", 5), ("two", 7),),
    (("four", 2), ("begin", 11), ("four", 0), ("three", 8),),
    (("two", 10), ("four", 4),),
    (("one", 11),),
    (("four", 5), ("two", 9), ("four", 1), ("three", 7),),
    (("five", 3), ("five", 6),),
    (("five", 4), ("four", 8), ("two", 11), ("three", 10), ("three", 9), ("four", 7), ("five", 5), ("four", 10), ("three", 11), ("five", 7), ("four", 11), ("four", 9), ("five", 9),),
)


def back_body(
    w, made, image_in, back_in, x_in, hidden_in, second_in, counts, qkv_in, heads_in, vectors,
    total_m, total_q, out_spread, grad_spread, vec_out, qv_out,
    tall, tall_t, back, back_t, hidden, total_acc, grad_second, out_low, in_low, wv,
    grad_part, parts, query_part, qkv_v, heads_v, vec_acc, *rest,
):
    ws, qs, hs, in_sems, out_sems, grad_sems = rest[:6]
    z, y, x, c = place()
    rs = Scatter(KINDS, rest[6:] + (made, total_m, total_q))
    greet(rs.line + [rs.y_peer, rs.x_peer, rs.c_peer])
    low, full = jnp.bfloat16, jnp.float32

    def turn(s):
        return (s % 2, s // 2) if isinstance(s, int) else (lax.rem(s, 2), lax.div(s, 2))

    def side_of(s):
        return lax.rem(1 - c + s, 2)

    def pair_loads(s):
        slot, k = turn(s)
        pair = side_of(s) * 4 + k
        return [
            pltpu.make_async_copy(w.at[k, side_of(s)], wv.at[slot], ws.at[slot]),
            pltpu.make_async_copy(qkv_in.at[pair], qkv_v.at[slot], qs.at[slot]),
            pltpu.make_async_copy(
                heads_in.at[:, columns(pair * LANES, LANES)], heads_v.at[slot], hs.at[slot]
            ),
        ]

    def start(copies):
        for copy in copies:
            copy.start()

    loads = [
        pltpu.make_async_copy(src, dst, in_sems.at[at])
        for at, (src, dst) in enumerate(
            ((image_in, out_low), (second_in, grad_second), (hidden_in, hidden), (back_in, back), (x_in, in_low))
        )
    ]
    rs.run(PLAN[0])
    start(loads)
    start(pair_loads(0))
    start(pair_loads(1))
    sent_out = Spread(out_low, out_spread, out_sems)
    loads[0].wait()
    sent_out.cross.start()
    sent_out.start()
    rs.run(PLAN[1])
    vec_acc[...] = jnp.zeros_like(vec_acc)

    def fold(row, value):
        vec_acc[row] += jnp.sum(value.reshape(-1, 8, value.shape[1]), 0)

    step = 64
    for load in loads[1:]:
        load.wait()

    @pl.loop(0, ROWS // step)
    def _(at):
        rows = pl.ds(pl.multiple_of(at * step, step), step)
        half_rows = pl.ds(pl.multiple_of(lax.rem(at, 5) * step, step), step)
        ones = vectors[5:6, :]
        _, normal, inverse = norm_rows(hidden[rows, :], ones, vectors[6:7, :])
        grad = grad_second[rows, :]
        behind = back[rows, :].astype(full)
        result = behind + norm_back(grad, normal, inverse, ones)
        hidden[rows, :] = result
        branch = result.astype(low)
        back[rows, :] = branch
        fold(2, branch.astype(full))
        fold(3, grad * normal)
        fold(4, grad)
        fold(5, behind)
        first, _, _ = norm_rows(
            in_low[lax.div(at, 5), half_rows, :].astype(full), vectors[0:1, :], vectors[1:2, :]
        )
        tall[rows, :] = first.astype(low)
        for turn_at in range(5):
            if PLAN[2 + turn_at]:

                @pl.when(at == 2 * turn_at + 1)
                def _():
                    rs.run(PLAN[2 + turn_at])

    transpose_into(back_t, back)
    rs.run(PLAN[7])
    transpose_into(tall_t, tall)
    total_acc[...] = jnp.zeros_like(total_acc)
    rs.run(PLAN[8])
    sent_out.forward()
    valid = slots_valid(counts, 0)
    lane = lax.broadcasted_iota(jnp.int32, (1, LANES), 1)
    line = lax.broadcasted_iota(jnp.int32, (LANES, 1), 0)

    @pl.loop(0, 8)
    def _(s):
        slot, k = turn(s)
        pair = side_of(s) * 4 + k
        for copy in pair_loads(s):
            copy.wait()
        grad_heads = nn(back[...], wv[slot, :, :, :, pl.ds(3 * LANES, LANES)].reshape(1024, LANES))
        grad_heads = grad_heads.astype(low)
        queries = qkv_v[slot, :, pl.ds(0, LANES)]
        keys = qkv_v[slot, :, pl.ds(LANES, LANES)]
        values = qkv_v[slot, :, pl.ds(2 * LANES, LANES)]
        keys_t = keys.T
        parts[...] = jnp.zeros_like(parts)
        query_part[...] = jnp.zeros_like(query_part)

        @pl.loop(0, 2)
        def _(at):
            here = (lane >= at * HD) & (lane < at * HD + HD)
            own_keys = jnp.where(here, keys * jnp.bfloat16(0.125), jnp.zeros_like(keys))
            own_values = jnp.where(here, values, jnp.zeros_like(values))
            scores = jnp.where(valid, nt(own_keys, queries), -1000000000.0)
            top = jnp.max(scores, 0, keepdims=True)
            exponent = jnp.exp(scores - top)
            attention = exponent * (1.0 / jnp.sum(exponent, 0, keepdims=True))
            grad_attention = nt(own_values, grad_heads)
            inner = jnp.sum(attention * grad_attention, 0, keepdims=True)
            grad_scores = (attention * (grad_attention - inner)).astype(low)
            own_line = (line >= at * HD) & (line < at * HD + HD)
            query_part[...] += jnp.where(own_line, nn(keys_t, grad_scores), 0.0)
            parts[0] += jnp.where(here, nn(grad_scores, queries), 0.0)
            parts[1] += jnp.where(here, nn(attention.astype(low), grad_heads), 0.0)

        for done in range(8):
            if PLAN[9 + 2 * done]:

                @pl.when(s == done)
                def _():
                    rs.run(PLAN[9 + 2 * done])

        grad_q = (query_part[...] * 0.125).T.astype(low)
        grad_k = (parts[0] * 0.125).astype(low)
        grad_v = parts[1].astype(low)
        grad_part[:, pl.ds(0, LANES)] = grad_q
        grad_part[:, pl.ds(LANES, LANES)] = grad_k
        grad_part[:, pl.ds(2 * LANES, LANES)] = grad_v
        qv_out[pl.ds(pair, 1), :] = jnp.sum(grad_q.astype(full), 0, keepdims=True)
        qv_out[pl.ds(8 + pair, 1), :] = jnp.sum(grad_v.astype(full), 0, keepdims=True)
        for half in range(2):
            rows = pl.ds(half * SLOTS, SLOTS)
            total_acc[rows, :] += nt(
                grad_part[rows, :], wv[slot, :, :, :, pl.ds(0, 3 * LANES)].reshape(1024, 3 * LANES)
            )
        for again in (2, 3):

            @pl.when(s == 2 * again)
            def _():
                rs.sent(6 + again, (0,))

        target = jnp.where(slot == 0, 12 + lax.rem(k, 2), 8 + k)
        for zi in range(2):
            rows = pl.ds(zi * 512, 512)
            blocks = pl.ds(2 * zi, 2)
            rs.g[target, blocks, :, :, pl.ds(0, 3 * LANES)] = (
                nn(tall_t[rows, :], grad_part[...]).astype(low).reshape(2, 2, 128, 3 * LANES)
            )
            rs.g[target, blocks, :, :, pl.ds(3 * LANES, LANES)] = (
                nn(back_t[rows, :], heads_v[slot]).astype(low).reshape(2, 2, 128, LANES)
            )

        @pl.when(s < 6)
        def _():
            start(pair_loads(s + 2))

        for done in range(8):
            if PLAN[10 + 2 * done]:

                @pl.when(s == done)
                def _():
                    rs.run(PLAN[10 + 2 * done])

    sent_grad = Spread(in_low, grad_spread, grad_sems)
    for first in (True, False):
        half = 1 - x if first else x

        @pl.loop(0, SLOTS // step)
        def _(at):
            half_rows = pl.ds(pl.multiple_of(at * step, step), step)
            rows = aligned(half * SLOTS + at * step, step, step)
            ones = vectors[0:1, :]
            _, normal, inverse = norm_rows(in_low[half, half_rows, :].astype(full), ones, vectors[1:2, :])
            grad = total_acc[rows, :]
            fold(0, grad * normal)
            fold(1, grad)
            result = hidden[rows, :] + norm_back(grad, normal, inverse, ones)
            in_low[half, half_rows, :] = result.astype(low)

        if first:
            sent_grad.cross.start()
            rs.run(PLAN[25])
    sent_grad.start()
    for row in range(6):
        vec_out[pl.ds(row, 1), :] = jnp.sum(vec_acc[row], 0, keepdims=True)
    rs.run(PLAN[26] + PLAN[27])
    sent_grad.forward()
    sent_out.finish()
    sent_grad.finish()
    rs.finish()


def back_all(w, made, image, back, x_all, hidden, grad_second, counts, qkv, heads, vectors):
    dma, vmem = pltpu.SemaphoreType.DMA, pltpu.VMEM
    low, full = jnp.bfloat16, jnp.float32
    anywhere = pl.BlockSpec(memory_space=pl.ANY)
    in_vmem = pl.BlockSpec(memory_space=pltpu.VMEM)
    shape = jax.ShapeDtypeStruct
    width = hidden.shape[1]
    return pl.pallas_call(
        back_body,
        out_shape=(
            shape((8, 128, WIDE), full),
            shape((4, 128, WIDE), full),
            shape((4, SLOTS, width), low),
            shape((4, SLOTS, width), low),
            shape((8, width), full),
            shape((16, LANES), full),
        ),
        in_specs=[anywhere] * 7 + [in_vmem] + [anywhere] * 2 + [in_vmem],
        out_specs=(anywhere,) * 4 + (in_vmem,) * 2,
        scratch_shapes=[
            vmem((ROWS, width), low),
            vmem((width, ROWS), low),
            vmem((ROWS, width), low),
            vmem((width, ROWS), low),
            vmem((ROWS, width), full),
            vmem((ROWS, width), full),
            vmem((ROWS, width), full),
            vmem((2, SLOTS, width), low),
            vmem((2, SLOTS, width), low),
            vmem((2, 4, 2, 128, WIDE), low),
            vmem((ROWS, 3 * LANES), low),
            vmem((2, ROWS, LANES), full),
            vmem((LANES, ROWS), full),
            vmem((2, ROWS, 3 * LANES), low),
            vmem((2, ROWS, LANES), low),
            vmem((6, 8, width), full),
            dma((2,)), dma((2,)), dma((2,)), dma((5,)), dma((7,)), dma((7,)),
        ] + Scatter.scratch(KINDS),
        compiler_params=pltpu.CompilerParams(
            collective_id=1, has_side_effects=True, vmem_limit_bytes=62 * MIB
        ),
    )(w, made, image, back, x_all, hidden, grad_second, counts, qkv, heads, vectors)


TILES = (
    [t for t in range(16) if t % 4 < 3],
    [3, 7, 11, 15],
    [t for t in range(16, 48) if t // 4 % 2 == 0],
    [t for t in range(16, 48) if t // 4 % 2 == 1],
)
SIZES = (3072.0 * 1024.0, 1024.0 * 1024.0, 4096.0 * 1024.0, 4096.0 * 1024.0)
VECS = 12
MISC = 12
SUMS = 14


def col_of(refs, t):
    chunk, part = t // 4, t % 4
    if chunk < 4:
        if part < 3:
            return refs[0].at[pl.ds(part, 1), pl.ds(chunk * LANES, LANES)]
        return refs[1].at[pl.ds(chunk, 1), :]
    return refs[2 + chunk % 2].at[pl.ds((chunk - 4) // 2 * 4 + part, 1), :]


def factor_body(
    total_q, total_m, squares, vec_sums, qv_sums, bias_grad, vecs, moments,
    row_mix, col_out, row_up, col_down, col_mix, row_out, col_up, row_down,
    row_new, row_flat, new_mix, new_out, new_up, new_down, vec_grad, vec_moment, vec_new, scale,
    core_s, core_r, pack_s, pack_r, ctx_r, line_s, line_r, y_r, last_s, last_r,
    c_ss, c_rs, x_ss, x_rs, z_ss, z_rs, y_ss, y_rs, l_ss, l_rs,
):
    z, y, x, c = place()
    line, y_peer, x_peer, c_peer = peers_of(z, y, x, c)
    square_peers = []
    for step in range(1, 16):
        spot = lax.rem((z * 2 + y) * 2 + c + step, 16)
        square_peers.append((lax.div(spot, 2), x, lax.rem(spot, 2)))
    greet(square_peers + [x_peer])

    def tile_of(t):
        cols = pl.ds(t % 4 * LANES, LANES)
        return total_q[t // 4, :, cols] if t < 16 else total_m[t // 4 - 4, :, cols]

    def lanes(at):
        return pl.ds(at % 8 * LANES, LANES)

    lane = lax.broadcasted_iota(jnp.int32, (128, 128), 1)
    core_s[pl.ds(0, 2), :] = vec_sums[pl.ds(0, 2), :]
    for at in range(8):
        core_s[pl.ds(2, 1), lanes(at)] = qv_sums[pl.ds(at, 1), :]
        core_s[pl.ds(3, 1), lanes(at)] = qv_sums[pl.ds(8 + at, 1), :]
        core_s[pl.ds(8 + at // 2, 1), pl.ds(at % 2 * WIDE, WIDE)] = bias_grad[pl.ds(at, 1), :]
    core_s[pl.ds(4, 4), :] = vec_sums[pl.ds(2, 4), :]
    packed = jnp.zeros((128, 128), jnp.float32)
    sums, olds = [], []
    old_cols = (col_mix, row_out, col_up, row_down)
    for m in range(4):
        block = jnp.zeros((128, 128), jnp.float32)
        old = jnp.zeros((1, LANES), jnp.float32)
        for t in TILES[m]:
            tile = tile_of(t)
            tile = tile * tile
            line_s[pl.ds(SUMS + t // 8, 1), lanes(t)] = jnp.sum(tile, 0, keepdims=True)
            block += tile
            old += col_of(old_cols, t)[...]
        per_row = jnp.sum(block, 1, keepdims=True)
        packed = jnp.where((lane >= 32 * m) & (lane < 32 * m + 32), per_row, packed)
        sums.append(jnp.sum(per_row, 0, keepdims=True))
        if m % 2 == 0:
            olds.append(jnp.sum((row_mix, None, row_up)[m][...], 1, keepdims=True) * 0.5)
        else:
            olds.append(jnp.sum(old, 1, keepdims=True) * 0.125)
    pack_s[...] = packed
    misc = sums + [squares[pl.ds(m, 1), 0:1] for m in range(4)] + olds + [jnp.zeros((1, 1), jnp.float32)] * 4
    for at, value in enumerate(misc):
        core_s[pl.ds(MISC + at // 8, 1), lanes(at)] = jnp.broadcast_to(value, (1, LANES))
    core_s[pl.ds(14, 2), :] = jnp.zeros((2, 1024), jnp.float32)
    hops = [
        remote(core_s, core_r, c_ss.at[0], c_rs.at[0], c_peer),
        remote(pack_s, pack_r, c_ss.at[1], c_rs.at[1], c_peer),
    ]
    for hop in hops:
        hop.start()
    for hop in hops:
        hop.wait()
    core_r[...] = core_r[...] + core_s[...]
    hop = remote(core_r, ctx_r, x_ss.at[0], x_rs.at[0], x_peer)
    hop.start()
    hop.wait()
    line_s[pl.ds(0, VECS), :] = core_r[pl.ds(0, VECS), :] + ctx_r[pl.ds(0, VECS), :]
    line_s[pl.ds(VECS, 2), :] = core_r[pl.ds(VECS, 2), :]
    line_s[pl.ds(20, 4), :] = jnp.zeros((4, 1024), jnp.float32)
    hops = [
        remote(line_s, line_r.at[z], z_ss.at[at], z_rs.at[at], peer) for at, peer in enumerate(line)
    ]
    for hop in hops:
        hop.start()
    line_r[pl.ds(z, 1)] = line_s[...][None]
    for hop in hops:
        hop.wait()
    line_s[...] = (line_r[0] + line_r[1]) + (line_r[2] + line_r[3])
    hop = remote(line_s, y_r, y_ss.at[0], y_rs.at[0], y_peer)
    hop.start()
    hop.wait()
    line_s[...] = line_s[...] + y_r[...]
    grads = line_s[pl.ds(0, VECS), :]
    vec_grad[...] = grads
    moment = decay_rate * moments[...] + (1.0 - decay_rate) * grads * grads
    vec_moment[...] = moment
    vec_step = grads * lax.rsqrt(moment)
    new_cols = (new_mix, new_out, new_up, new_down)
    for t in range(48):
        col_of(new_cols, t)[...] = decay_rate * col_of(old_cols, t)[...] + (1.0 - decay_rate) * (
            line_s[pl.ds(SUMS + t // 8, 1), lanes(t)] * (1.0 / 1024.0)
        )
    row_sum = pack_r[...] + pack_s[...]
    row_count = jnp.where(lane < 32, 1.0 / 3072.0, jnp.where(lane < 64, 1.0 / 1024.0, 1.0 / 4096.0))
    row_old = jnp.concatenate(
        [jnp.broadcast_to(one[...], (32, LANES)) for one in (row_mix, col_out, row_up, col_down)], 0
    ).T
    row_all = decay_rate * row_old + (1.0 - decay_rate) * row_sum * row_count
    row_new[...] = row_all
    row_flat[...] = row_all.T
    row_inverse = lax.rsqrt(row_all)
    row_lengths = (1024.0, 1024.0, 1024.0, 4096.0)
    square = jnp.zeros((1, 1), jnp.float32)
    factors = []
    for m in range(4):
        all_square, all_weight, all_old = (
            line_s[pl.ds(MISC + at // 8, 1), pl.ds(at % 8 * LANES, 1)] for at in (m, 4 + m, 8 + m)
        )
        average = decay_rate * all_old / row_lengths[m] + (1.0 - decay_rate) * all_square / SIZES[m]
        block = jnp.zeros((128, 128), jnp.float32)
        for t in TILES[m]:
            update = tile_of(t) * lax.rsqrt(col_of(new_cols, t)[...])
            block += update * update
        by_row = row_inverse[:, 32 * m : 32 * m + 1]
        per_row = jnp.sum(block, 1, keepdims=True) * by_row * by_row
        square += jnp.sum(per_row, 0, keepdims=True) * average
        factors.append((jnp.sqrt(average), jnp.sqrt(all_weight / SIZES[m])))
    spot = (z * 2 + y) * 2 + c
    last_s[...] = jnp.broadcast_to(square, (8, LANES))
    last_r[pl.ds(spot, 1)] = last_s[...][None]
    hops = [
        remote(last_s, last_r.at[spot], l_ss.at[at], l_rs.at[at], peer)
        for at, peer in enumerate(square_peers)
    ]
    for hop in hops:
        hop.start()
    for hop in hops:
        hop.wait()
    square = jnp.zeros((1, 1), jnp.float32)
    for at in range(16):
        square += last_r[at, 0:1, 0:1]
    vec_square = jnp.sum(jnp.sum(vec_step * vec_step, 1, keepdims=True), 0, keepdims=True)
    old_vecs = vecs[...]
    vec_size = VECS * 1024.0
    vec_mean = jnp.sum(jnp.sum(old_vecs * old_vecs, 1, keepdims=True), 0, keepdims=True) / vec_size
    count = sum(SIZES) + vec_size
    shrink = 1.0 / jnp.maximum(1.0, jnp.sqrt((square + vec_square) / count) / clip_level)
    vec_new[...] = old_vecs - step_rate * jnp.sqrt(vec_mean) * vec_step * shrink
    for m in range(4):
        scale[pl.ds(m, 1), :] = jnp.broadcast_to(
            step_rate * factors[m][0] * factors[m][1] * shrink, (1, LANES)
        )
    scale[pl.ds(4, 4), :] = jnp.zeros((4, LANES), jnp.float32)


def factor_all(*arrays):
    dma = pltpu.SemaphoreType.DMA
    full = jnp.float32
    in_vmem = pl.BlockSpec(memory_space=pltpu.VMEM)
    shape = jax.ShapeDtypeStruct
    shapes = [(128, 128), (128, 128), (3, WIDE), (4, LANES), (16, LANES), (16, LANES)]
    shapes += [(VECS, 1024)] * 3 + [(8, LANES)]
    return pl.pallas_call(
        factor_body,
        out_shape=tuple(shape(one, full) for one in shapes),
        in_specs=[in_vmem] * len(arrays),
        out_specs=(in_vmem,) * len(shapes),
        scratch_shapes=[
            pltpu.VMEM((16, 1024), full),
            pltpu.VMEM((16, 1024), full),
            pltpu.VMEM((128, 128), full),
            pltpu.VMEM((128, 128), full),
            pltpu.VMEM((16, 1024), full),
            pltpu.VMEM((24, 1024), full),
            pltpu.VMEM((4, 24, 1024), full),
            pltpu.VMEM((24, 1024), full),
            pltpu.VMEM((8, LANES), full),
            pltpu.VMEM((16, 8, LANES), full),
            dma((2,)), dma((2,)), dma((1,)), dma((1,)), dma((3,)), dma((3,)), dma((1,)), dma((1,)),
            dma((15,)), dma((15,)),
        ],
        compiler_params=pltpu.CompilerParams(
            collective_id=3, has_side_effects=True, vmem_limit_bytes=40 * MIB
        ),
    )(*arrays)


def finish_body(
    total_q, total_m, mix_w, out_w, up_w, down_w, row_new, row_flat, new_mix, new_out, new_up, new_down,
    vec_grad, vec_moment, vec_new, scale, *outs,
):
    grads, news, copies, smalls = outs[:4], outs[4:8], outs[8:12], outs[12:]
    at = pl.program_id(0)

    def by_row(m):
        return lax.rsqrt(row_new[:, 32 * m : 32 * m + 1])

    def by_col(row, m):
        return lax.rsqrt(row) * scale[pl.ds(m, 1), :]

    def put(m, index, grad, old, update):
        new = old - grad * update
        grads[m][index] = grad
        news[m][index] = new
        copies[m][index] = new.astype(jnp.bfloat16)

    everything = slice(None)
    for part in range(3):
        cols = new_mix[pl.ds(part, 1), columns(at * LANES, LANES)]
        grad = total_q[0, :, pl.ds(part * LANES, LANES)]
        put(0, (part, everything, everything), grad, mix_w[part], by_row(0) * by_col(cols, 0))
    turned_out = lax.rsqrt(row_flat[pl.ds(32, 1), :])
    turned_down = lax.rsqrt(row_flat[pl.ds(96, 1), :])
    cols = jnp.broadcast_to(by_col(new_out[pl.ds(at, 1), :], 1), (LANES, LANES)).T
    grad = total_q[0, :, pl.ds(3 * LANES, LANES)].T
    put(1, (everything, everything), grad, out_w[...], cols * turned_out)
    for part in range(4):
        here = pl.ds(part * LANES, LANES)
        row = pl.ds(at * 4 + part, 1)
        put(
            2, (everything, here), total_m[0, :, here], up_w[:, here],
            by_row(2) * by_col(new_up[row, :], 2),
        )
        cols = jnp.broadcast_to(by_col(new_down[row, :], 3), (LANES, LANES)).T
        put(3, (here, everything), total_m[1, :, here].T, down_w[here, :], cols * turned_down)
    for target, source in zip(smalls[:7], (vec_grad, vec_moment, vec_new, new_mix, new_out, new_up, new_down)):
        target[...] = source[...]
    for m, target in enumerate(smalls[7:]):
        target[...] = row_flat[pl.ds(32 * m, 1), :]


def finish_all(total_q, total_m, weights, factors):
    low, full = jnp.bfloat16, jnp.float32
    shape = jax.ShapeDtypeStruct
    blocks = [
        pl.BlockSpec((3, 128, LANES), lambda at: (0, 0, at)),
        pl.BlockSpec((LANES, 128), lambda at: (at, 0)),
        pl.BlockSpec((128, WIDE), lambda at: (0, at)),
        pl.BlockSpec((WIDE, 128), lambda at: (at, 0)),
    ]

    def whole(array_shape):
        return pl.BlockSpec(array_shape, lambda at: (0,) * len(array_shape))

    smalls = [(VECS, 1024)] * 3 + [(3, WIDE), (4, LANES), (16, LANES), (16, LANES)] + [(1, LANES)] * 4
    shapes = [shape(one.shape, kind) for kind in (full, full, low) for one in weights]
    shapes += [shape(one, full) for one in smalls]
    return pl.pallas_call(
        finish_body,
        grid=(4,),
        out_shape=tuple(shapes),
        in_specs=[
            pl.BlockSpec((1, 128, WIDE), lambda at: (at, 0, 0)),
            pl.BlockSpec((2, 128, WIDE), lambda at: (at, 0, 0)),
        ] + blocks + [whole(one.shape) for one in factors],
        out_specs=tuple(blocks * 3 + [whole(one) for one in smalls]),
        compiler_params=pltpu.CompilerParams(vmem_limit_bytes=40 * MIB),
    )(total_q, total_m, *weights, *factors)


def fast_body(
    inputs, cotangent, key_mask, image_mask, qkv_weight, out_weight, up_weight, down_weight,
    vectors, row_qkv, col_qkv, row_out, col_out, row_up, col_up, row_down, col_down, vector_moments,
):
    images, tokens, width = inputs.shape
    pad = ((0, 0), (0, SLOTS - tokens), (0, 0))
    weight_rows = (key_mask * image_mask[:, None]).astype(jnp.bfloat16)
    x_in = jnp.pad(inputs, pad)
    b_in = jnp.pad(cotangent * weight_rows[:, :, None], pad)
    counts = jnp.sum(key_mask, 1).astype(jnp.float32)
    n_in = jnp.broadcast_to(counts[:, None, None], (images, 8, LANES))
    weights = (qkv_weight.transpose(1, 0, 2), out_weight, up_weight, down_weight)
    w, made, b_all, x_all, n_all, qkv, heads, hidden, squares, grad_second, image, bias_grad = front_all(
        x_in, b_in, n_in, weights, vectors
    )
    total_m, total_q, out_spread, grad_spread, vec_sums, qv_sums = back_all(
        w, made, image, b_all.reshape(ROWS, width), x_all, hidden, grad_second, n_all, qkv, heads, vectors
    )
    factors = factor_all(
        total_q, total_m, squares, vec_sums, qv_sums, bias_grad, vectors, vector_moments,
        row_qkv.reshape(1, LANES), col_out.reshape(1, LANES), row_up.reshape(1, LANES),
        col_down.reshape(1, LANES), col_qkv, row_out.reshape(4, LANES), col_up.reshape(16, LANES),
        row_down.reshape(16, LANES),
    )
    done = finish_all(total_q, total_m, weights, factors)

    def natural(four):
        return (four[0].transpose(1, 0, 2),) + tuple(four[1:])

    vector_grad, vector_moment, vector_new, new_mix, new_out, new_up, new_down = done[12:19]
    rows = [one.reshape(-1) for one in done[19:]]
    return (
        (out_spread[:, :tokens], grad_spread[:, :tokens])
        + natural(done[:4])
        + (vector_grad,)
        + natural(done[4:8])
        + (vector_new,)
        + natural(done[8:12])
        + (
            rows[0], new_mix, new_out.reshape(-1), rows[1], rows[2], new_up.reshape(-1),
            new_down.reshape(-1), rows[3], vector_moment,
        )
    )


def pick_body(*arrays):
    sizes = tuple(lax.axis_size(name) for name in ("fsdp", "ctx", "tp"))
    if sizes == (8, 2, 2) and arrays[0].shape == (4, 290, 1024) and arrays[6].shape == (128, 2048):
        return fast_body(*arrays)
    return body(*arrays)


def solution(mesh):
    placed = (
        P("fsdp", "ctx", None),
        P("fsdp", "ctx", None),
        P("fsdp", "ctx"),
        P("fsdp"),
        P("fsdp", None, "tp"),
        P("tp", "fsdp"),
        P("fsdp", "tp"),
        P("tp", "fsdp"),
        P(),
        P("fsdp"),
        P(None, "tp"),
        P("tp"),
        P("fsdp"),
        P("fsdp"),
        P("tp"),
        P("tp"),
        P("fsdp"),
        P(),
    )
    return jax.shard_map(
        pick_body,
        mesh=mesh,
        in_specs=placed,
        out_specs=(
            P("fsdp", "ctx", None),
            P("fsdp", "ctx", None),
            P("fsdp", None, "tp"),
            P("tp", "fsdp"),
            P("fsdp", "tp"),
            P("tp", "fsdp"),
            P(),
            P("fsdp", None, "tp"),
            P("tp", "fsdp"),
            P("fsdp", "tp"),
            P("tp", "fsdp"),
            P(),
            P("fsdp", None, "tp"),
            P("tp", "fsdp"),
            P("fsdp", "tp"),
            P("tp", "fsdp"),
            P("fsdp"),
            P(None, "tp"),
            P("tp"),
            P("fsdp"),
            P("fsdp"),
            P("tp"),
            P("tp"),
            P("fsdp"),
            P(),
        ),
        check_vma=False,
    )
```

```python
import jax
import jax.numpy as jnp
from jax import lax
from jax.experimental import pallas as pl
from jax.experimental.pallas import tpu as pltpu
from jax.sharding import PartitionSpec as P

HD = 64
FF = 4096


eps_norm = 1e-06
decay_rate = 0.5
clip_level = 0.1
step_rate = 5.0


def norm_rows(rows, scale_row, offset):
    row_mean = jnp.mean(rows, -1, keepdims=True)
    centered = rows - row_mean
    inverse = lax.rsqrt(jnp.mean(centered * centered, -1, keepdims=True) + eps_norm)
    normal = centered * inverse
    return (normal * scale_row + offset, normal, inverse)


def norm_back(grad_rows, normal, inverse, scale_row):
    scaled = grad_rows * scale_row
    first_term = jnp.mean(scaled, -1, keepdims=True)
    second_term = jnp.mean(scaled * normal, -1, keepdims=True)
    return inverse * (scaled - first_term - normal * second_term)


def gelu_erf(argument):
    return 0.5 * argument * (1.0 + lax.erf(argument * 0.7071067811865476))


def gelu_slope(argument):
    return (
        0.5 * (1.0 + lax.erf(argument * 0.7071067811865476))
        + argument * jnp.exp(-0.5 * argument * argument) * 0.3989422804014327
    )


def masked_scores(queries, key_rows, valid_keys):
    scale_qk = queries.shape[-1] ** (-0.5)
    scores = (
        jnp.einsum("gqhe,gkhe->ghqk", queries, key_rows, preferred_element_type=jnp.float32)
        * scale_qk
    )
    return jnp.where(valid_keys[:, None, None, :] > 0, scores, -1000000000.0)


def attend_forward(pieces):
    queries, key_rows, value_rows, valid_keys = pieces
    scores = masked_scores(queries, key_rows, valid_keys)
    row_max = jnp.max(scores, -1, keepdims=True)
    exponent = jnp.exp(scores - row_max)
    totals = jnp.sum(exponent, -1, keepdims=True)
    attention = (exponent / totals).astype(jnp.bfloat16)
    attended = jnp.einsum(
        "ghqk,gkhe->gqhe", attention, value_rows, preferred_element_type=jnp.float32
    )
    return (attended.astype(jnp.bfloat16), (row_max + jnp.log(totals))[..., 0])


def attend_back(pieces):
    queries, key_rows, value_rows, valid_keys, logsum, grad_heads = pieces
    scale_qk = queries.shape[-1] ** (-0.5)
    scores = masked_scores(queries, key_rows, valid_keys)
    attention = jnp.exp(scores - logsum[..., None])
    grad_attention = jnp.einsum(
        "gqhe,gkhe->ghqk", grad_heads, value_rows, preferred_element_type=jnp.float32
    )
    inner = jnp.sum(attention * grad_attention, -1, keepdims=True)
    grad_scores = (attention * (grad_attention - inner)).astype(jnp.bfloat16)
    grad_queries = (
        jnp.einsum("ghqk,gkhe->gqhe", grad_scores, key_rows, preferred_element_type=jnp.float32)
        * scale_qk
    ).astype(jnp.bfloat16)
    grad_keys = (
        jnp.einsum("ghqk,gqhe->gkhe", grad_scores, queries, preferred_element_type=jnp.float32)
        * scale_qk
    )
    grad_values = jnp.einsum(
        "ghqk,gqhe->gkhe",
        attention.astype(jnp.bfloat16),
        grad_heads,
        preferred_element_type=jnp.float32,
    )
    return (grad_queries, grad_keys, grad_values)


def place_at(piece, full_shape, start, axis):
    return lax.dynamic_update_slice_in_dim(jnp.zeros(full_shape, jnp.float32), piece, start, axis)


def factor_local(
    grad_local, rows_old, cols_old, rows_full, rows_here, cols_here, row_total, col_total, old_total
):
    rows_new = decay_rate * rows_old + (1.0 - decay_rate) * rows_here / col_total
    cols_new = decay_rate * cols_old + (1.0 - decay_rate) * cols_here / row_total
    rows_avg = decay_rate * old_total / row_total + (1.0 - decay_rate) * jnp.sum(rows_full) / (
        row_total * col_total
    )
    update = grad_local * lax.rsqrt(rows_new[:, None] * cols_new[None, :] / rows_avg)
    return (rows_new, cols_new, update)


def body(
    inputs,
    cotangent,
    key_mask,
    image_mask,
    qkv_weight,
    out_weight,
    up_weight,
    down_weight,
    vectors,
    row_qkv,
    col_qkv,
    row_out,
    col_out,
    row_up,
    col_up,
    row_down,
    col_down,
    vector_moments,
):
    images, local_tokens, model_width = inputs.shape
    rows_here = images * local_tokens
    width_piece = qkv_weight.shape[0]
    half_width = qkv_weight.shape[2]
    half_hidden = up_weight.shape[1]
    head_size = HD
    heads_here = half_width // head_size
    tp_index = lax.axis_index("tp")
    fsdp_index = lax.axis_index("fsdp")
    tp_first = (tp_index == 0).astype(jnp.float32)
    ctx_first = (lax.axis_index("ctx") == 0).astype(jnp.float32)
    fsdp_first = (fsdp_index == 0).astype(jnp.float32)
    mix_w, out_w, up_w, down_w = (
        lax.all_gather(qkv_weight.astype(jnp.bfloat16), "fsdp", axis=0, tiled=True),
        lax.all_gather(out_weight.astype(jnp.bfloat16), "fsdp", axis=1, tiled=True),
        lax.all_gather(up_weight.astype(jnp.bfloat16), "fsdp", axis=0, tiled=True),
        lax.all_gather(down_weight.astype(jnp.bfloat16), "fsdp", axis=1, tiled=True),
    )
    query_bias = lax.dynamic_slice_in_dim(vectors[2], tp_index * half_width, half_width)
    value_bias = lax.dynamic_slice_in_dim(vectors[3], tp_index * half_width, half_width)
    up_bias = lax.dynamic_slice_in_dim(vectors[8:].reshape(-1), tp_index * half_hidden, half_hidden)
    flat_rows = inputs.astype(jnp.float32).reshape(rows_here, model_width)
    normed, normal_one, inverse_one = norm_rows(flat_rows, vectors[0], vectors[1])
    normed_low = normed.astype(jnp.bfloat16)
    projected = jnp.einsum("td,dcn->tcn", normed_low, mix_w, preferred_element_type=jnp.float32)
    queries = (projected[:, 0] + query_bias).astype(jnp.bfloat16)
    key_low = projected[:, 1].astype(jnp.bfloat16).reshape(images, local_tokens, half_width)
    value_low = (
        (projected[:, 2] + value_bias)
        .astype(jnp.bfloat16)
        .reshape(images, local_tokens, half_width)
    )
    all_keys, all_values, all_valid = (
        lax.all_gather(key_low, "ctx", axis=1, tiled=True),
        lax.all_gather(value_low, "ctx", axis=1, tiled=True),
        lax.all_gather(key_mask.astype(jnp.bfloat16), "ctx", axis=1, tiled=True),
    )
    seq_all = all_keys.shape[1]
    group_size = min(2, images)
    groups = images // group_size

    def grouped(array):
        return array.reshape((groups, group_size) + array.shape[1:])

    query_heads = grouped(queries.reshape(images, local_tokens, heads_here, head_size))
    key_heads = grouped(all_keys.reshape(images, seq_all, heads_here, head_size))
    value_heads = grouped(all_values.reshape(images, seq_all, heads_here, head_size))
    valid_groups = grouped(all_valid)
    attended, logsum = lax.map(attend_forward, (query_heads, key_heads, value_heads, valid_groups))
    heads_low = attended.reshape(rows_here, half_width)
    branch = (
        lax.psum(
            jnp.dot(heads_low, out_w, preferred_element_type=jnp.float32).astype(jnp.bfloat16), "tp"
        ).astype(jnp.float32)
        + vectors[4]
    )
    hidden = flat_rows + branch
    second, normal_two, inverse_two = norm_rows(hidden, vectors[5], vectors[6])
    second_low = second.astype(jnp.bfloat16)
    pre_active = jnp.dot(second_low, up_w, preferred_element_type=jnp.float32) + up_bias
    active_low = gelu_erf(pre_active).astype(jnp.bfloat16)
    mlp_sum = lax.psum(
        jnp.dot(active_low, down_w, preferred_element_type=jnp.float32).astype(jnp.bfloat16), "tp"
    ).astype(jnp.float32)
    output = (
        (hidden + mlp_sum + vectors[7])
        .astype(jnp.bfloat16)
        .reshape(images, local_tokens, model_width)
    )
    weight_rows = key_mask.astype(jnp.float32) * image_mask.astype(jnp.float32)[:, None]
    back = (cotangent.astype(jnp.float32) * weight_rows[:, :, None]).reshape(rows_here, model_width)
    back_low = back.astype(jnp.bfloat16)
    grad_active = jnp.einsum("td,fd->tf", back_low, down_w, preferred_element_type=jnp.float32)
    grad_pre = (grad_active * gelu_slope(pre_active)).astype(jnp.bfloat16)
    grad_down = jnp.einsum("tf,td->fd", active_low, back_low, preferred_element_type=jnp.float32)
    grad_up = jnp.einsum("td,tf->df", second_low, grad_pre, preferred_element_type=jnp.float32)
    grad_up_bias = jnp.sum(grad_pre.astype(jnp.float32), 0)
    grad_second = lax.psum(
        jnp.einsum("tf,df->td", grad_pre, up_w, preferred_element_type=jnp.float32).astype(
            jnp.bfloat16
        ),
        "tp",
    ).astype(jnp.float32)
    grad_hidden = back + norm_back(grad_second, normal_two, inverse_two, vectors[5])
    grad_branch = grad_hidden.astype(jnp.bfloat16)
    grad_out = jnp.einsum("tn,td->nd", heads_low, grad_branch, preferred_element_type=jnp.float32)
    grad_heads = jnp.einsum(
        "td,nd->tn", grad_branch, out_w, preferred_element_type=jnp.float32
    ).astype(jnp.bfloat16)
    grad_head_groups = grouped(grad_heads.reshape(images, local_tokens, heads_here, head_size))
    grad_queries, grad_keys, grad_values = lax.map(
        attend_back, (query_heads, key_heads, value_heads, valid_groups, logsum, grad_head_groups)
    )
    key_grads, value_grads = (
        lax.psum_scatter(
            grad_keys.reshape(images, seq_all, half_width).astype(jnp.bfloat16),
            "ctx",
            scatter_dimension=1,
            tiled=True,
        ).astype(jnp.float32),
        lax.psum_scatter(
            grad_values.reshape(images, seq_all, half_width).astype(jnp.bfloat16),
            "ctx",
            scatter_dimension=1,
            tiled=True,
        ).astype(jnp.float32),
    )
    grad_projected = jnp.stack(
        [
            grad_queries.reshape(rows_here, half_width),
            key_grads.reshape(rows_here, half_width).astype(jnp.bfloat16),
            value_grads.reshape(rows_here, half_width).astype(jnp.bfloat16),
        ],
        1,
    )
    grad_mix = jnp.einsum(
        "td,tcn->dcn", normed_low, grad_projected, preferred_element_type=jnp.float32
    )
    grad_normed = lax.psum(
        jnp.einsum("tcn,dcn->td", grad_projected, mix_w, preferred_element_type=jnp.float32).astype(
            jnp.bfloat16
        ),
        "tp",
    ).astype(jnp.float32)
    input_grad = (
        (grad_hidden + norm_back(grad_normed, normal_one, inverse_one, vectors[0]))
        .astype(jnp.bfloat16)
        .reshape(images, local_tokens, model_width)
    )
    projected_sums = jnp.sum(grad_projected.astype(jnp.float32), 0)
    vector_part = jnp.concatenate(
        [
            jnp.stack(
                [
                    jnp.sum(grad_normed * normal_one, 0) * tp_first,
                    jnp.sum(grad_normed, 0) * tp_first,
                    place_at(projected_sums[0], (model_width,), tp_index * half_width, 0),
                    place_at(projected_sums[2], (model_width,), tp_index * half_width, 0),
                    jnp.sum(grad_branch.astype(jnp.float32), 0) * tp_first,
                    jnp.sum(grad_second * normal_two, 0) * tp_first,
                    jnp.sum(grad_second, 0) * tp_first,
                    jnp.sum(back, 0) * tp_first,
                ]
            ),
            place_at(grad_up_bias, (FF,), tp_index * half_hidden, 0).reshape(-1, model_width),
        ],
        0,
    )
    shards = (
        lax.psum_scatter(grad_mix, "fsdp", scatter_dimension=0, tiled=True),
        lax.psum_scatter(grad_out, "fsdp", scatter_dimension=1, tiled=True),
        lax.psum_scatter(grad_up, "fsdp", scatter_dimension=0, tiled=True),
        lax.psum_scatter(grad_down, "fsdp", scatter_dimension=1, tiled=True),
    )
    sum_mix, sum_out, sum_up, sum_down = (
        lax.psum(shards[0].astype(jnp.bfloat16), "ctx").astype(jnp.float32),
        lax.psum(shards[1].astype(jnp.bfloat16), "ctx").astype(jnp.float32),
        lax.psum(shards[2].astype(jnp.bfloat16), "ctx").astype(jnp.float32),
        lax.psum(shards[3].astype(jnp.bfloat16), "ctx").astype(jnp.float32),
    )
    fsdp_start = fsdp_index * width_piece
    tp_width = tp_index * half_width
    tp_hidden = tp_index * half_hidden
    mix_square = sum_mix * sum_mix
    out_square = sum_out * sum_out
    up_square = sum_up * sum_up
    down_square = sum_down * sum_down
    scalar_part = (
        jnp.stack(
            [
                jnp.sum(qkv_weight * qkv_weight),
                jnp.sum(out_weight * out_weight),
                jnp.sum(up_weight * up_weight),
                jnp.sum(down_weight * down_weight),
                jnp.sum(row_qkv) * tp_first,
                jnp.sum(row_out) * fsdp_first,
                jnp.sum(row_up) * tp_first,
                jnp.sum(row_down) * fsdp_first,
            ]
        )
        * ctx_first
    )
    (
        vector_grad,
        rows_mix,
        cols_mix,
        rows_out,
        cols_out,
        rows_up,
        cols_up,
        rows_down,
        cols_down,
        scalar_sums,
    ) = lax.psum(
        (
            vector_part,
            place_at(jnp.sum(mix_square, (1, 2)), (model_width,), fsdp_start, 0) * ctx_first,
            place_at(jnp.sum(mix_square, 0), (3, model_width), tp_width, 1) * ctx_first,
            place_at(jnp.sum(out_square, 1), (model_width,), tp_width, 0) * ctx_first,
            place_at(jnp.sum(out_square, 0), (model_width,), fsdp_start, 0) * ctx_first,
            place_at(jnp.sum(up_square, 1), (model_width,), fsdp_start, 0) * ctx_first,
            place_at(jnp.sum(up_square, 0), (FF,), tp_hidden, 0) * ctx_first,
            place_at(jnp.sum(down_square, 1), (FF,), tp_hidden, 0) * ctx_first,
            place_at(jnp.sum(down_square, 0), (model_width,), fsdp_start, 0) * ctx_first,
            scalar_part,
        ),
        ("fsdp", "ctx", "tp"),
    )
    qkv_rows, qkv_cols_flat, mix_update = factor_local(
        sum_mix.reshape(width_piece, -1),
        row_qkv,
        col_qkv.reshape(-1),
        rows_mix,
        lax.dynamic_slice_in_dim(rows_mix, fsdp_start, width_piece),
        lax.dynamic_slice_in_dim(cols_mix, tp_width, half_width, 1).reshape(-1),
        model_width,
        3 * model_width,
        scalar_sums[4],
    )
    out_rows, out_cols, out_update = factor_local(
        sum_out,
        row_out,
        col_out,
        rows_out,
        lax.dynamic_slice_in_dim(rows_out, tp_width, half_width),
        lax.dynamic_slice_in_dim(cols_out, fsdp_start, width_piece),
        model_width,
        model_width,
        scalar_sums[5],
    )
    up_rows, up_cols, up_update = factor_local(
        sum_up,
        row_up,
        col_up,
        rows_up,
        lax.dynamic_slice_in_dim(rows_up, fsdp_start, width_piece),
        lax.dynamic_slice_in_dim(cols_up, tp_hidden, half_hidden),
        model_width,
        FF,
        scalar_sums[6],
    )
    down_rows, down_cols, down_update = factor_local(
        sum_down,
        row_down,
        col_down,
        rows_down,
        lax.dynamic_slice_in_dim(rows_down, tp_hidden, half_hidden),
        lax.dynamic_slice_in_dim(cols_down, fsdp_start, width_piece),
        FF,
        model_width,
        scalar_sums[7],
    )
    vector_moment = decay_rate * vector_moments + (1.0 - decay_rate) * vector_grad * vector_grad
    vector_step = vector_grad * lax.rsqrt(vector_moment)
    local_square = (
        jnp.sum(mix_update * mix_update)
        + jnp.sum(out_update * out_update)
        + jnp.sum(up_update * up_update)
        + jnp.sum(down_update * down_update)
    )
    global_square = lax.psum(local_square, ("fsdp", "tp")) + jnp.sum(vector_step * vector_step)
    param_count = 4 * model_width * model_width + 2 * model_width * FF + vectors.size
    shrink = 1.0 / jnp.maximum(1.0, jnp.sqrt(global_square / param_count) / clip_level)
    qkv_new = (
        qkv_weight
        - step_rate
        * jnp.sqrt(scalar_sums[0] / (3 * model_width * model_width))
        * mix_update.reshape(qkv_weight.shape)
        * shrink
    )
    out_new = (
        out_weight
        - step_rate * jnp.sqrt(scalar_sums[1] / (model_width * model_width)) * out_update * shrink
    )
    up_new = (
        up_weight - step_rate * jnp.sqrt(scalar_sums[2] / (model_width * FF)) * up_update * shrink
    )
    down_new = (
        down_weight
        - step_rate * jnp.sqrt(scalar_sums[3] / (model_width * FF)) * down_update * shrink
    )
    vector_new = vectors - step_rate * jnp.sqrt(jnp.mean(vectors * vectors)) * vector_step * shrink
    return (
        output,
        input_grad,
        sum_mix,
        sum_out,
        sum_up,
        sum_down,
        vector_grad,
        qkv_new,
        out_new,
        up_new,
        down_new,
        vector_new,
        qkv_new.astype(jnp.bfloat16),
        out_new.astype(jnp.bfloat16),
        up_new.astype(jnp.bfloat16),
        down_new.astype(jnp.bfloat16),
        qkv_rows,
        qkv_cols_flat.reshape(3, half_width),
        out_rows,
        out_cols,
        up_rows,
        up_cols,
        down_rows,
        down_cols,
        vector_moment,
    )


MESH = pl.DeviceIdType.MESH
LANES = 128
SLOTS = 320
ROWS = 2 * SLOTS
WIDE = 512
CHUNKS = 12
PAIRS = 8
MIB = 1024 * 1024


def place():
    shard = lax.axis_index("fsdp")
    return (lax.div(shard, 2), lax.rem(shard, 2), lax.axis_index("ctx"), lax.axis_index("tp"))


def peers_of(z, y, x, c):
    line = [(lax.rem(z + step, 4) * 2 + y, x, c) for step in (1, 2, 3)]
    return (line, (z * 2 + 1 - y, x, c), (z * 2 + y, 1 - x, c), (z * 2 + y, x, 1 - c))


def greet(peers):
    barrier = pltpu.get_barrier_semaphore()
    for peer in peers:
        pl.semaphore_signal(barrier, inc=1, device_id=peer, device_id_type=MESH)
    pl.semaphore_wait(barrier, len(peers))


def remote(src, dst, send, recv, peer):
    return pltpu.make_async_remote_copy(
        src_ref=src, dst_ref=dst, send_sem=send, recv_sem=recv, device_id=peer, device_id_type=MESH
    )


def nn(left, right):
    return lax.dot_general(left, right, (((1,), (0,)), ((), ())), preferred_element_type=jnp.float32)


def nt(left, right):
    return lax.dot_general(left, right, (((1,), (1,)), ((), ())), preferred_element_type=jnp.float32)


def aligned(start, size, unit):
    if isinstance(start, int):
        return pl.ds(start, size)
    return pl.ds(pl.multiple_of(start, unit), size)


def columns(start, size):
    return aligned(start, size, LANES)


def slots_valid(counts, axis):
    shape = (1, ROWS) if axis else (ROWS, 1)
    slot = lax.broadcasted_iota(jnp.int32, shape, axis)
    first = counts[0, 0:1, 0:1].astype(jnp.int32)
    second = counts[1, 0:1, 0:1].astype(jnp.int32)
    return ((slot < SLOTS) & (slot < first)) | ((slot >= SLOTS) & (slot - SLOTS < second))


def square_sum(ref):
    flat = ref if len(ref.shape) == 2 else ref.reshape(ref.shape[0] * ref.shape[1], ref.shape[2])
    step = flat.shape[0] // 8

    def add(at, total):
        values = flat[pl.ds(pl.multiple_of(at * step, step), step), :]
        return total + jnp.sum(values * values, 0, keepdims=True)

    total = lax.fori_loop(0, 8, add, jnp.zeros((1, flat.shape[1]), jnp.float32))
    return jnp.sum(total, 1, keepdims=True)


SERVE = (
    (),
    ((0, 0), (0, 1), (0, 2), (1, 0), (0, 3), (1, 1), (2, 0), (1, 2), (0, 4), (3, 0),),
    (),
    ((2, 1),),
    (),
    ((1, 3), (0, 5),),
    ((3, 1),),
    (),
    ((2, 2), (1, 4),),
    (),
    ((0, 6),),
    ((3, 2),),
    (),
    ((1, 5), (2, 3),),
    (),
    ((0, 7),),
    ((1, 6), (3, 3), (2, 4),),
    (),
    (),
    (),
    ((3, 4),),
    ((0, 8), (1, 7),),
    (),
    (),
    (),
    (),
    ((0, 9), (1, 8),),
    ((2, 5), (0, 10), (2, 6), (3, 5),),
    ((1, 9),),
    ((2, 7), (3, 6),),
    ((0, 11),),
    ((1, 10), (2, 8), (3, 7),),
    (),
    ((2, 9),),
    ((3, 8), (1, 11),),
    ((2, 10), (3, 9),),
    (),
    ((2, 11),),
    ((3, 10),),
    ((3, 11),),
    (),
    (),
    (),
    (),
)


def transpose_into(target, source):
    for at in range(source.shape[1] // LANES):
        target[pl.ds(at * LANES, LANES), :] = source[:, pl.ds(at * LANES, LANES)].T


def front_body(
    x_in, b_in, n_in, mix_w, out_w, up_w, down_w, vectors,
    kept, g_out, b_out, x_out, n_out, qkv, heads, hidden, squares, grad_second, image_out, bias_grad,
    normed, w, wo, normed_t, back_t, halves, total_acc, staged,
    local, in_s, in_r, zs, zr, ys, yr, xs, xr, cs, cr, ws, gs,
):
    z, y, x, c = place()
    line, y_peer, x_peer, c_peer = peers_of(z, y, x, c)
    own = []
    mine, theirs = 2 * x + c, 2 * (1 - x) + c
    pairs = ((x_in, x_out), (n_in, n_out), (b_in, b_out))
    for at, (src, dst) in enumerate(pairs):
        own.append(pltpu.make_async_copy(src.at[mine], dst.at[x], local.at[at]))
    for copy in own:
        copy.start()
    low = jnp.bfloat16
    for k in range(4):
        lanes = pl.ds(k * LANES, LANES)
        for part in range(3):
            w[k, c, z, y, :, pl.ds(part * LANES, LANES)] = mix_w[part, :, lanes].astype(low)
        w[k, c, z, y, :, pl.ds(3 * LANES, LANES)] = out_w[lanes, :].T.astype(low)
        w[4 + 2 * k, c, z, y] = up_w[:, pl.ds(k * WIDE, WIDE)].astype(low)
        for part in range(4):
            rows = pl.ds(k * WIDE + part * LANES, LANES)
            w[5 + 2 * k, c, z, y, :, pl.ds(part * LANES, LANES)] = down_w[rows, :].T.astype(low)
    greet(line + [y_peer, x_peer, c_peer])
    swaps = [
        remote(src.at[theirs], dst.at[x], in_s.at[at], in_r.at[at], x_peer)
        for at, (src, dst) in enumerate(pairs)
    ]

    def share(k):
        size = 80 if k < 6 else 96
        return aligned(x * (128 - size), size, 16), aligned(x * size, 128 - size, 16)

    def z_copies(k):
        block = w.at[k, c, z, y, share(k)[0]]
        return [remote(block, block, zs.at[k, at], zr.at[k, at], peer) for at, peer in enumerate(line)]

    def y_copies(k):
        rows = share(k)[0]
        blocks = [w.at[k, c, pl.ds(2 * at, 2), y, rows] for at in range(2)]
        return [remote(block, block, ys.at[k, at], yr.at[k, at], y_peer) for at, block in enumerate(blocks)]

    def x_copies(k):
        rows = share(k)[1]
        blocks = [w.at[k, c, at, :, rows] for at in range(4)]
        return [remote(block, block, xs.at[k, at], xr.at[k, at], x_peer) for at, block in enumerate(blocks)]

    def c_copies(k):
        blocks = [w.at[k, c, at] for at in range(4)]
        return [remote(block, block, cs.at[k, at], cr.at[k, at], c_peer) for at, block in enumerate(blocks)]

    def keep(k):
        return pltpu.make_async_copy(w.at[k], kept.at[k], ws.at[k])

    def start(copies):
        for copy in copies:
            copy.start()

    def arrive(copies):
        for copy in copies:
            copy.wait_recv()

    ahead = 3

    def serve(kind, k):
        if kind == 0:
            arrive(z_copies(k))
            start(y_copies(k))
            if k + ahead < CHUNKS:
                start(z_copies(k + ahead))
        elif kind == 1:
            arrive(y_copies(k))
            start(x_copies(k))
        elif kind == 2:
            arrive(x_copies(k))
            start(c_copies(k))
        else:
            arrive(c_copies(k))
            if k < 4:
                keep(k).start()

    def hook(at):
        for call in SERVE[at]:
            serve(*call)
        if at == 8:
            swaps[2].start()

    swaps[0].start()
    swaps[1].start()
    for t in range(ahead):
        start(z_copies(t))
    own[0].wait()
    own[1].wait()

    def norm_first(half):
        @pl.loop(0, SLOTS // 64)
        def _(at):
            rows = pl.ds(pl.multiple_of(at * 64, 64), 64)
            result, _, _ = norm_rows(
                x_out[half, rows, :].astype(jnp.float32), vectors[0:1, :], vectors[1:2, :]
            )
            normed[aligned(half * SLOTS + at * 64, 64, 64), :] = result.astype(jnp.bfloat16)

    norm_first(x)
    for m, ref in enumerate((mix_w, out_w, up_w, down_w)):
        squares[pl.ds(m, 1), :] = jnp.broadcast_to(square_sum(ref), (1, LANES))
    hook(0)
    swaps[0].wait_recv()
    swaps[1].wait_recv()
    norm_first(1 - x)
    hook(1)
    valid = slots_valid(n_out, 1)
    lane = lax.broadcasted_iota(jnp.int32, (1, LANES), 1)

    def pair_task(side, k):
        pair = side * 4 + k
        weights = w[k, side].reshape(1024, WIDE)
        wo[:, columns(pair * LANES, LANES)] = weights[:, 3 * LANES :]
        weights = weights[:, : 3 * LANES]
        q_bias = vectors[2:3, columns(pair * LANES, LANES)]
        v_bias = vectors[3:4, columns(pair * LANES, LANES)]
        bias = jnp.concatenate([q_bias, jnp.zeros_like(q_bias), v_bias], 1)
        for half in range(2):
            qkv[pair, pl.ds(half * SLOTS, SLOTS), :] = (
                nn(normed[pl.ds(half * SLOTS, SLOTS), :], weights) + bias
            ).astype(
                jnp.bfloat16
            )

        hook(3 + 5 * k + 2 * side)

        @pl.loop(0, 2)
        def _(half):
            rows = pl.ds(pl.multiple_of(half * SLOTS, SLOTS), SLOTS)
            queries = qkv[pair, rows, pl.ds(0, LANES)] * jnp.bfloat16(0.125)
            keys = qkv[pair, :, pl.ds(LANES, LANES)]
            values = qkv[pair, :, pl.ds(2 * LANES, LANES)]
            results = []
            for at in range(2):
                here = (lane < HD) if at == 0 else (lane >= HD)
                scores = nt(jnp.where(here, queries, jnp.zeros_like(queries)), keys)
                scores = jnp.where(valid, scores, -1000000000.0)
                top = jnp.max(scores, 1, keepdims=True)
                exponent = jnp.exp(scores - top)
                attention = exponent * (1.0 / jnp.sum(exponent, 1, keepdims=True))
                results.append(nn(attention.astype(jnp.bfloat16), values))
            heads[rows, columns(pair * LANES, LANES)] = jnp.where(
                lane < HD, results[0], results[1]
            ).astype(jnp.bfloat16)

    for k in range(4):
        hook(2 + 5 * k)
        pair_task(0, k)
        hook(4 + 5 * k)
        pair_task(1, k)
        hook(6 + 5 * k)

    for tile in range(4):
        for half in range(2):
            rows = pl.ds(half * SLOTS, SLOTS)
            cols = pl.ds(tile * 256, 256)
            branch = nt(heads[rows, :], wo[cols, :])
            hidden[rows, cols] = x_out[half, :, cols].astype(jnp.float32) + (branch + vectors[4:5, cols])
        hook(22 + tile)

    @pl.loop(0, ROWS // 64)
    def _(at):
        rows = pl.ds(pl.multiple_of(at * 64, 64), 64)
        result, _, _ = norm_rows(hidden[rows, :], vectors[5:6, :], vectors[6:7, :])
        normed[rows, :] = result.astype(jnp.bfloat16)
        total_acc[rows, :] = hidden[rows, :] + vectors[7:8, :]

    own[2].wait()
    swaps[2].wait_recv()
    hook(26)
    transpose_into(normed_t, normed)
    for half in range(2):
        for at in range(1024 // LANES):
            lanes = pl.ds(at * LANES, LANES)
            back_t[lanes, pl.ds(half * SLOTS, SLOTS)] = b_out[half, :, lanes].T
    grad_second[...] = jnp.zeros_like(grad_second)

    def send_tile(s):
        j, side = (s // 2, s % 2) if isinstance(s, int) else (lax.div(s, 2), lax.rem(s, 2))
        return pltpu.make_async_copy(staged, g_out.at[pl.ds(2 * j, 2), side], gs.at[0])

    hook(27)

    def hooks_at(s, first):
        for done in range(8):
            if SERVE[first + 2 * done]:

                @pl.when(s == done)
                def _():
                    hook(first + 2 * done)

    @pl.loop(0, 8)
    def _(s):
        j, side = lax.div(s, 2), lax.rem(s, 2)
        tile = side * 4 + j
        bias = vectors[pl.ds(8 + side * 2 + lax.div(j, 2), 1), columns(lax.rem(j, 2) * WIDE, WIDE)]
        up = w[4 + 2 * j, side].reshape(1024, WIDE)
        down = w[5 + 2 * j, side].reshape(1024, WIDE)
        sums = jnp.zeros((1, WIDE), jnp.float32)
        for half in range(2):
            rows = pl.ds(half * SLOTS, SLOTS)
            pre = nn(normed[rows, :], up) + bias
            grad_active = nn(b_out[half], down)
            share = 0.5 * (1.0 + lax.erf(pre * 0.7071067811865476))
            slope = share + pre * jnp.exp(-0.5 * pre * pre) * 0.3989422804014327
            act = (pre * share).astype(low)
            grad_pre = (grad_active * slope).astype(low)
            halves[0, rows, :] = act
            halves[1, rows, :] = grad_pre
            sums += jnp.sum(grad_pre.astype(jnp.float32), 0, keepdims=True)
            total_acc[rows, :] += nt(act, down)
            grad_second[rows, :] += nt(grad_pre, up)
        bias_grad[pl.ds(tile, 1), :] = sums
        hooks_at(s, 28)

        @pl.when(s > 0)
        def _():
            send_tile(s).wait()

        for zi in range(2):
            rows = pl.ds(zi * 512, 512)
            staged[0, pl.ds(2 * zi, 2)] = nn(normed_t[rows, :], halves[1]).astype(low).reshape(2, 2, 128, WIDE)
            staged[1, pl.ds(2 * zi, 2)] = nn(back_t[rows, :], halves[0]).astype(low).reshape(2, 2, 128, WIDE)
        send_tile(s).start()
        hooks_at(s, 29)

    for half in range(2):
        image_out[half] = total_acc[pl.ds(half * SLOTS, SLOTS), :].astype(low)
    send_tile(7).wait()
    for k in range(4):
        keep(k).wait()
    for swap in swaps:
        swap.wait_send()

    for k in range(CHUNKS):
        for copy in z_copies(k) + y_copies(k) + x_copies(k) + c_copies(k):
            copy.wait_send()


def front_all(x_in, b_in, n_in, weights, vectors):
    dma = pltpu.SemaphoreType.DMA
    low, full = jnp.bfloat16, jnp.float32
    anywhere = pl.BlockSpec(memory_space=pl.ANY)
    in_vmem = pl.BlockSpec(memory_space=pltpu.VMEM)
    shape = jax.ShapeDtypeStruct
    width = x_in.shape[2]
    return pl.pallas_call(
        front_body,
        out_shape=(
            shape((4, 2, 4, 2, 128, WIDE), low),
            shape((8, 2, 4, 2, 128, WIDE), low),
            shape((2, SLOTS, width), low),
            shape((2, SLOTS, width), low),
            shape((2, 8, LANES), full),
            shape((PAIRS, ROWS, 3 * LANES), low),
            shape((ROWS, width), low),
            shape((ROWS, width), full),
            shape((8, LANES), full),
            shape((ROWS, width), full),
            shape((2, SLOTS, width), low),
            shape((8, WIDE), full),
        ),
        in_specs=[anywhere] * 3 + [in_vmem] * 5,
        out_specs=(anywhere, anywhere) + (in_vmem,) * 10,
        scratch_shapes=[
            pltpu.VMEM((ROWS, width), low),
            pltpu.VMEM((CHUNKS, 2, 4, 2, 128, WIDE), low),
            pltpu.VMEM((1024, 1024), low),
            pltpu.VMEM((width, ROWS), low),
            pltpu.VMEM((width, ROWS), low),
            pltpu.VMEM((2, ROWS, WIDE), low),
            pltpu.VMEM((ROWS, width), full),
            pltpu.VMEM((2, 4, 2, 128, WIDE), low),
            dma((3,)), dma((3,)), dma((3,)), dma((CHUNKS, 3)), dma((CHUNKS, 3)),
            dma((CHUNKS, 2)), dma((CHUNKS, 2)), dma((CHUNKS, 4)), dma((CHUNKS, 4)), dma((CHUNKS, 4)), dma((CHUNKS, 4)),
            dma((4,)), dma((1,)),
        ],
        compiler_params=pltpu.CompilerParams(
            collective_id=0, has_side_effects=True, vmem_limit_bytes=62 * MIB
        ),
    )(x_in, b_in, n_in, *weights, vectors)


def add_into(held, index, arrived, from_index):
    held[index] = (
        held[index].astype(jnp.float32) + arrived[from_index].astype(jnp.float32)
    ).astype(jnp.bfloat16)


class Scatter:
    def __init__(self, crosswise, refs):
        self.crosswise = crosswise
        self.where = place()
        self.line, self.y_peer, self.x_peer, self.c_peer = peers_of(*self.where)
        x = self.where[2]
        self.near = aligned(x * 64, 64, 64)
        self.far = aligned((1 - x) * 64, 64, 64)
        self.slot = [sum(k == crosswise[at] for k in crosswise[:at]) for at in range(len(crosswise))]
        (
            self.g, self.cb, self.xa, self.ya, self.za, self.fa, self.yb, self.zb, self.xb, self.stage,
            self.cs, self.cr, self.s1s, self.s1r, self.s2s, self.s2r, self.s3s, self.s3r, self.s4s, self.s4r,
            self.out_sem, self.free, self.in_sem, self.made,
        ) = refs[:24]
        self.totals = refs[24:]
        self.waited = set()

    def hops(self, stage, q):
        z, y, x, c = self.where
        at, own = self.slot[q], self.g.at[q]
        if stage == 0:
            c = self.where[3]
            source = self.made.at[q, 1 - c] if q < 8 else self.g.at[12 + q % 2]
            return [
                remote(source, self.cb.at[q % 4], self.cs.at[q], self.cr.at[q], self.c_peer)
            ]
        first, third = (self.s1s.at[q], self.s1r.at[q]), (self.s4s.at[q], self.s4r.at[q])
        second, last = (self.s2s.at[q], self.s2r.at[q]), (self.s3s.at[q], self.s3r.at[q])
        ahead = [lax.rem(z + d + 1, 4) for d in range(3)]
        if self.crosswise[q]:
            near = self.near
            if stage == 1:
                return [remote(own.at[:, :, self.far], self.xa.at[at], *first, self.x_peer)]
            if stage == 2:
                return [
                    remote(own.at[:, 1 - y, near], self.ya.at[at], second[0].at[0], second[1].at[0], self.y_peer)
                ]
            if stage == 3:
                return [
                    remote(own.at[to, y, near], self.za.at[at, d], last[0].at[d], last[1].at[d], peer)
                    for d, (to, peer) in enumerate(zip(ahead, self.line))
                ]
            return [remote(own.at[z, y, near], self.fa.at[at], *third, self.x_peer)]
        if stage == 1:
            return [remote(own.at[:, 1 - y], self.yb.at[at], *first, self.y_peer)]
        if stage == 2:
            return [
                remote(own.at[to, y], self.zb.at[at, d], second[0].at[d], second[1].at[d], peer)
                for d, (to, peer) in enumerate(zip(ahead, self.line))
            ]
        if stage == 3:
            return [remote(own.at[z, y], self.xb.at[at], last[0].at[0], last[1].at[0], self.x_peer)]
        return []

    def start(self, stage, q):
        for copy in self.hops(stage, q):
            copy.start()

    def arrive(self, stage, q):
        for copy in self.hops(stage, q):
            copy.wait_recv()

    def sent(self, q, stages):
        for stage in stages:
            self.waited.add((stage, q))
            for copy in self.hops(stage, q):
                copy.wait_send()

    def begin(self, q):
        if q < 8:
            self.load(q).start()
        if q >= 4:
            pl.semaphore_wait(self.free.at[q % 4], 1)
        self.start(0, q)

    def load(self, q):
        return pltpu.make_async_copy(self.made.at[q, self.where[3]], self.g.at[q], self.in_sem.at[q])

    def one(self, q):
        if q < 8:
            self.load(q).wait()
        self.arrive(0, q)

        @pl.loop(0, 8)
        def _(block):
            zi, yi = lax.div(block, 2), lax.rem(block, 2)
            add_into(self.g, (q, zi, yi), self.cb, (q % 4, zi, yi))

        if q < 8:
            pl.semaphore_signal(
                self.free.at[q % 4], inc=1, device_id=self.c_peer, device_id_type=MESH
            )

        self.start(1, q)

    def two(self, q):
        y, at = self.where[1], self.slot[q]
        self.arrive(1, q)
        if self.crosswise[q]:

            @pl.loop(0, 8)
            def _(block):
                zi, yi = lax.div(block, 2), lax.rem(block, 2)
                add_into(self.g, (q, zi, yi, self.near), self.xa, (at, zi, yi))

        else:

            @pl.loop(0, 4)
            def _(zi):
                add_into(self.g, (q, zi, y), self.yb, (at, zi))

        self.start(2, q)

    def sum_line(self, q, rows, buffer):
        z, y = self.where[:2]
        value = self.g[(q, z, y) + rows].astype(jnp.float32)
        for d in range(3):
            value += buffer[self.slot[q], d].astype(jnp.float32)
        self.g[(q, z, y) + rows] = value.astype(jnp.bfloat16)

    def three(self, q):
        y, at = self.where[1], self.slot[q]
        self.arrive(2, q)
        if self.crosswise[q]:

            @pl.loop(0, 4)
            def _(zi):
                add_into(self.g, (q, zi, y, self.near), self.ya, (at, zi))

        else:
            self.sum_line(q, (), self.zb)
        self.start(3, q)

    def export(self, q):
        target = self.totals[0].at[q] if q < 8 else self.totals[1].at[q - 8]
        return pltpu.make_async_copy(self.stage.at[q % 4], target, self.out_sem.at[q])

    def four(self, q):
        z, y = self.where[:2]
        at = self.slot[q]
        self.arrive(3, q)
        if self.crosswise[q]:
            self.sum_line(q, (self.near,), self.za)
            self.start(4, q)
        else:
            if q >= 4:
                self.export(q - 4).wait()
            self.stage[q % 4] = self.g[q, z, y].astype(jnp.float32) + self.xb[at].astype(jnp.float32)
            self.export(q).start()

    def five(self, q):
        z, y = self.where[:2]
        if self.crosswise[q]:
            self.arrive(4, q)
            if q >= 4:
                self.export(q - 4).wait()
            self.stage[q % 4, self.near] = self.g[q, z, y, self.near].astype(jnp.float32)
            self.stage[q % 4, self.far] = self.fa[self.slot[q]].astype(jnp.float32)
            self.export(q).start()

    def run(self, calls):
        for name, q in calls:
            getattr(self, name)(q)

    def finish(self):
        count = len(self.crosswise)
        for q in range(count - 4, count):
            self.export(q).wait()
        for stage in range(5):
            for q in range(count):
                if (stage, q) not in self.waited:
                    self.sent(q, (stage,))

    @staticmethod
    def scratch(crosswise):
        dma, vmem, low = pltpu.SemaphoreType.DMA, pltpu.VMEM, jnp.bfloat16
        n, across = len(crosswise), sum(crosswise)
        along = n - across
        return [
            vmem((14, 4, 2, 128, WIDE), low),
            vmem((4, 4, 2, 128, WIDE), low),
            vmem((across, 4, 2, 64, WIDE), low),
            vmem((across, 4, 64, WIDE), low),
            vmem((across, 3, 64, WIDE), low),
            vmem((across, 64, WIDE), low),
            vmem((along, 4, 128, WIDE), low),
            vmem((along, 3, 128, WIDE), low),
            vmem((along, 128, WIDE), low),
            vmem((4, 128, WIDE), jnp.float32),
            dma((n,)), dma((n,)), dma((n,)), dma((n,)), dma((n, 3)), dma((n, 3)),
            dma((n, 3)), dma((n, 3)), dma((n,)), dma((n,)), dma((n,)), pltpu.SemaphoreType.REGULAR((4,)), dma((8,)),
        ]


class Spread:
    def __init__(self, src, dst, sems):
        z, y, x, c = place()
        _, _, x_peer, c_peer = peers_of(z, y, x, c)
        mine, theirs = 2 * x + c, 2 * (1 - x) + c
        self.cross = remote(src.at[1 - x], dst.at[mine], sems.at[0], sems.at[1], x_peer)
        self.near = remote(src.at[x], dst.at[mine], sems.at[2], sems.at[3], c_peer)
        self.local = pltpu.make_async_copy(src.at[x], dst.at[mine], sems.at[4])
        self.onward = remote(dst.at[theirs], dst.at[theirs], sems.at[5], sems.at[6], c_peer)

    def start(self):
        self.near.start()
        self.local.start()

    def forward(self):
        self.cross.wait_recv()
        self.onward.start()

    def finish(self):
        self.cross.wait_send()
        self.near.wait()
        self.local.wait()
        self.onward.wait()


KINDS = (False, False, False, True, True, True, True, True, False, True, False, False)
PLAN = (
    (("begin", 2), ("begin", 0), ("begin", 1), ("begin", 3),),
    (),
    (),
    (("one", 2),),
    (("begin", 6),),
    (("one", 0),),
    (("begin", 4),),
    (("one", 1),),
    (("begin", 5), ("one", 3),),
    (("two", 2), ("begin", 7), ("one", 6),),
    (("one", 4),),
    (("two", 0), ("one", 5), ("two", 3), ("one", 7), ("begin", 8),),
    (("three", 2),),
    (("two", 1), ("two", 6), ("one", 8),),
    (("begin", 9),),
    (("three", 0), ("three", 3),),
    (("one", 9), ("three", 6), ("two", 4),),
    (("three", 1),),
    (("begin", 10),),
    (("four", 3), ("two", 5), ("two", 8),),
    (("four", 6), ("one", 10), ("three", 4),),
    (("three", 5), ("two", 7),),
    (("four", 2), ("begin", 11), ("four", 0), ("three", 8),),
    (("two", 10), ("four", 4),),
    (("one", 11),),
    (("four", 5), ("two", 9), ("four", 1), ("three", 7),),
    (("five", 3), ("five", 6),),
    (("five", 4), ("four", 8), ("two", 11), ("three", 10), ("three", 9), ("four", 7), ("five", 5), ("four", 10), ("three", 11), ("five", 7), ("four", 11), ("four", 9), ("five", 9),),
)


def back_body(
    w, made, image_in, back_in, x_in, hidden_in, second_in, counts, qkv_in, heads_in, vectors,
    total_m, total_q, out_spread, grad_spread, vec_out, qv_out,
    tall, tall_t, back, back_t, hidden, total_acc, grad_second, out_low, in_low, wv,
    grad_part, parts, query_part, qkv_v, heads_v, vec_acc, *rest,
):
    ws, qs, hs, in_sems, out_sems, grad_sems = rest[:6]
    z, y, x, c = place()
    rs = Scatter(KINDS, rest[6:] + (made, total_m, total_q))
    greet(rs.line + [rs.y_peer, rs.x_peer, rs.c_peer])
    low, full = jnp.bfloat16, jnp.float32

    def turn(s):
        return (s % 2, s // 2) if isinstance(s, int) else (lax.rem(s, 2), lax.div(s, 2))

    def side_of(s):
        return lax.rem(1 - c + s, 2)

    def pair_loads(s):
        slot, k = turn(s)
        pair = side_of(s) * 4 + k
        return [
            pltpu.make_async_copy(w.at[k, side_of(s)], wv.at[slot], ws.at[slot]),
            pltpu.make_async_copy(qkv_in.at[pair], qkv_v.at[slot], qs.at[slot]),
            pltpu.make_async_copy(
                heads_in.at[:, columns(pair * LANES, LANES)], heads_v.at[slot], hs.at[slot]
            ),
        ]

    def start(copies):
        for copy in copies:
            copy.start()

    loads = [
        pltpu.make_async_copy(src, dst, in_sems.at[at])
        for at, (src, dst) in enumerate(
            ((image_in, out_low), (second_in, grad_second), (hidden_in, hidden), (back_in, back), (x_in, in_low))
        )
    ]
    rs.run(PLAN[0])
    start(loads)
    start(pair_loads(0))
    start(pair_loads(1))
    sent_out = Spread(out_low, out_spread, out_sems)
    loads[0].wait()
    sent_out.cross.start()
    sent_out.start()
    rs.run(PLAN[1])
    vec_acc[...] = jnp.zeros_like(vec_acc)

    def fold(row, value):
        vec_acc[row] += jnp.sum(value.reshape(-1, 8, value.shape[1]), 0)

    step = 64
    for load in loads[1:]:
        load.wait()

    @pl.loop(0, ROWS // step)
    def _(at):
        rows = pl.ds(pl.multiple_of(at * step, step), step)
        half_rows = pl.ds(pl.multiple_of(lax.rem(at, 5) * step, step), step)
        ones = vectors[5:6, :]
        _, normal, inverse = norm_rows(hidden[rows, :], ones, vectors[6:7, :])
        grad = grad_second[rows, :]
        behind = back[rows, :].astype(full)
        result = behind + norm_back(grad, normal, inverse, ones)
        hidden[rows, :] = result
        branch = result.astype(low)
        back[rows, :] = branch
        fold(2, branch.astype(full))
        fold(3, grad * normal)
        fold(4, grad)
        fold(5, behind)
        first, _, _ = norm_rows(
            in_low[lax.div(at, 5), half_rows, :].astype(full), vectors[0:1, :], vectors[1:2, :]
        )
        tall[rows, :] = first.astype(low)
        for turn_at in range(5):
            if PLAN[2 + turn_at]:

                @pl.when(at == 2 * turn_at + 1)
                def _():
                    rs.run(PLAN[2 + turn_at])

    transpose_into(back_t, back)
    rs.run(PLAN[7])
    transpose_into(tall_t, tall)
    total_acc[...] = jnp.zeros_like(total_acc)
    rs.run(PLAN[8])
    sent_out.forward()
    valid = slots_valid(counts, 0)
    lane = lax.broadcasted_iota(jnp.int32, (1, LANES), 1)
    line = lax.broadcasted_iota(jnp.int32, (LANES, 1), 0)

    @pl.loop(0, 8)
    def _(s):
        slot, k = turn(s)
        pair = side_of(s) * 4 + k
        for copy in pair_loads(s):
            copy.wait()
        grad_heads = nn(back[...], wv[slot, :, :, :, pl.ds(3 * LANES, LANES)].reshape(1024, LANES))
        grad_heads = grad_heads.astype(low)
        queries = qkv_v[slot, :, pl.ds(0, LANES)]
        keys = qkv_v[slot, :, pl.ds(LANES, LANES)]
        values = qkv_v[slot, :, pl.ds(2 * LANES, LANES)]
        keys_t = keys.T
        parts[...] = jnp.zeros_like(parts)
        query_part[...] = jnp.zeros_like(query_part)

        @pl.loop(0, 2)
        def _(at):
            here = (lane >= at * HD) & (lane < at * HD + HD)
            own_keys = jnp.where(here, keys * jnp.bfloat16(0.125), jnp.zeros_like(keys))
            own_values = jnp.where(here, values, jnp.zeros_like(values))
            scores = jnp.where(valid, nt(own_keys, queries), -1000000000.0)
            top = jnp.max(scores, 0, keepdims=True)
            exponent = jnp.exp(scores - top)
            attention = exponent * (1.0 / jnp.sum(exponent, 0, keepdims=True))
            grad_attention = nt(own_values, grad_heads)
            inner = jnp.sum(attention * grad_attention, 0, keepdims=True)
            grad_scores = (attention * (grad_attention - inner)).astype(low)
            own_line = (line >= at * HD) & (line < at * HD + HD)
            query_part[...] += jnp.where(own_line, nn(keys_t, grad_scores), 0.0)
            parts[0] += jnp.where(here, nn(grad_scores, queries), 0.0)
            parts[1] += jnp.where(here, nn(attention.astype(low), grad_heads), 0.0)

        for done in range(8):
            if PLAN[9 + 2 * done]:

                @pl.when(s == done)
                def _():
                    rs.run(PLAN[9 + 2 * done])

        grad_q = (query_part[...] * 0.125).T.astype(low)
        grad_k = (parts[0] * 0.125).astype(low)
        grad_v = parts[1].astype(low)
        grad_part[:, pl.ds(0, LANES)] = grad_q
        grad_part[:, pl.ds(LANES, LANES)] = grad_k
        grad_part[:, pl.ds(2 * LANES, LANES)] = grad_v
        qv_out[pl.ds(pair, 1), :] = jnp.sum(grad_q.astype(full), 0, keepdims=True)
        qv_out[pl.ds(8 + pair, 1), :] = jnp.sum(grad_v.astype(full), 0, keepdims=True)
        for half in range(2):
            rows = pl.ds(half * SLOTS, SLOTS)
            total_acc[rows, :] += nt(
                grad_part[rows, :], wv[slot, :, :, :, pl.ds(0, 3 * LANES)].reshape(1024, 3 * LANES)
            )
        for again in (2, 3):

            @pl.when(s == 2 * again)
            def _():
                rs.sent(6 + again, (0,))

        target = jnp.where(slot == 0, 12 + lax.rem(k, 2), 8 + k)
        for zi in range(2):
            rows = pl.ds(zi * 512, 512)
            blocks = pl.ds(2 * zi, 2)
            rs.g[target, blocks, :, :, pl.ds(0, 3 * LANES)] = (
                nn(tall_t[rows, :], grad_part[...]).astype(low).reshape(2, 2, 128, 3 * LANES)
            )
            rs.g[target, blocks, :, :, pl.ds(3 * LANES, LANES)] = (
                nn(back_t[rows, :], heads_v[slot]).astype(low).reshape(2, 2, 128, LANES)
            )

        @pl.when(s < 6)
        def _():
            start(pair_loads(s + 2))

        for done in range(8):
            if PLAN[10 + 2 * done]:

                @pl.when(s == done)
                def _():
                    rs.run(PLAN[10 + 2 * done])

    sent_grad = Spread(in_low, grad_spread, grad_sems)
    for first in (True, False):
        half = 1 - x if first else x

        @pl.loop(0, SLOTS // step)
        def _(at):
            half_rows = pl.ds(pl.multiple_of(at * step, step), step)
            rows = aligned(half * SLOTS + at * step, step, step)
            ones = vectors[0:1, :]
            _, normal, inverse = norm_rows(in_low[half, half_rows, :].astype(full), ones, vectors[1:2, :])
            grad = total_acc[rows, :]
            fold(0, grad * normal)
            fold(1, grad)
            result = hidden[rows, :] + norm_back(grad, normal, inverse, ones)
            in_low[half, half_rows, :] = result.astype(low)

        if first:
            sent_grad.cross.start()
            rs.run(PLAN[25])
    sent_grad.start()
    for row in range(6):
        vec_out[pl.ds(row, 1), :] = jnp.sum(vec_acc[row], 0, keepdims=True)
    rs.run(PLAN[26] + PLAN[27])
    sent_grad.forward()
    sent_out.finish()
    sent_grad.finish()
    rs.finish()


def back_all(w, made, image, back, x_all, hidden, grad_second, counts, qkv, heads, vectors):
    dma, vmem = pltpu.SemaphoreType.DMA, pltpu.VMEM
    low, full = jnp.bfloat16, jnp.float32
    anywhere = pl.BlockSpec(memory_space=pl.ANY)
    in_vmem = pl.BlockSpec(memory_space=pltpu.VMEM)
    shape = jax.ShapeDtypeStruct
    width = hidden.shape[1]
    return pl.pallas_call(
        back_body,
        out_shape=(
            shape((8, 128, WIDE), full),
            shape((4, 128, WIDE), full),
            shape((4, SLOTS, width), low),
            shape((4, SLOTS, width), low),
            shape((8, width), full),
            shape((16, LANES), full),
        ),
        in_specs=[anywhere] * 7 + [in_vmem] + [anywhere] * 2 + [in_vmem],
        out_specs=(anywhere,) * 4 + (in_vmem,) * 2,
        scratch_shapes=[
            vmem((ROWS, width), low),
            vmem((width, ROWS), low),
            vmem((ROWS, width), low),
            vmem((width, ROWS), low),
            vmem((ROWS, width), full),
            vmem((ROWS, width), full),
            vmem((ROWS, width), full),
            vmem((2, SLOTS, width), low),
            vmem((2, SLOTS, width), low),
            vmem((2, 4, 2, 128, WIDE), low),
            vmem((ROWS, 3 * LANES), low),
            vmem((2, ROWS, LANES), full),
            vmem((LANES, ROWS), full),
            vmem((2, ROWS, 3 * LANES), low),
            vmem((2, ROWS, LANES), low),
            vmem((6, 8, width), full),
            dma((2,)), dma((2,)), dma((2,)), dma((5,)), dma((7,)), dma((7,)),
        ] + Scatter.scratch(KINDS),
        compiler_params=pltpu.CompilerParams(
            collective_id=1, has_side_effects=True, vmem_limit_bytes=62 * MIB
        ),
    )(w, made, image, back, x_all, hidden, grad_second, counts, qkv, heads, vectors)


TILES = (
    [t for t in range(16) if t % 4 < 3],
    [3, 7, 11, 15],
    [t for t in range(16, 48) if t // 4 % 2 == 0],
    [t for t in range(16, 48) if t // 4 % 2 == 1],
)
SIZES = (3072.0 * 1024.0, 1024.0 * 1024.0, 4096.0 * 1024.0, 4096.0 * 1024.0)
VECS = 12
MISC = 12
SUMS = 14


def col_of(refs, t):
    chunk, part = t // 4, t % 4
    if chunk < 4:
        if part < 3:
            return refs[0].at[pl.ds(part, 1), pl.ds(chunk * LANES, LANES)]
        return refs[1].at[pl.ds(chunk, 1), :]
    return refs[2 + chunk % 2].at[pl.ds((chunk - 4) // 2 * 4 + part, 1), :]


def factor_body(
    total_q, total_m, squares, vec_sums, qv_sums, bias_grad, vecs, moments,
    row_mix, col_out, row_up, col_down, col_mix, row_out, col_up, row_down,
    row_new, row_flat, new_mix, new_out, new_up, new_down, vec_grad, vec_moment, vec_new, scale,
    core_s, core_r, pack_s, pack_r, ctx_r, line_s, line_r, y_r, last_s, last_r,
    c_ss, c_rs, x_ss, x_rs, z_ss, z_rs, y_ss, y_rs, l_ss, l_rs,
):
    z, y, x, c = place()
    line, y_peer, x_peer, c_peer = peers_of(z, y, x, c)
    square_peers = []
    for step in range(1, 16):
        spot = lax.rem((z * 2 + y) * 2 + c + step, 16)
        square_peers.append((lax.div(spot, 2), x, lax.rem(spot, 2)))
    greet(square_peers + [x_peer])

    def tile_of(t):
        cols = pl.ds(t % 4 * LANES, LANES)
        return total_q[t // 4, :, cols] if t < 16 else total_m[t // 4 - 4, :, cols]

    def lanes(at):
        return pl.ds(at % 8 * LANES, LANES)

    lane = lax.broadcasted_iota(jnp.int32, (128, 128), 1)
    core_s[pl.ds(0, 2), :] = vec_sums[pl.ds(0, 2), :]
    for at in range(8):
        core_s[pl.ds(2, 1), lanes(at)] = qv_sums[pl.ds(at, 1), :]
        core_s[pl.ds(3, 1), lanes(at)] = qv_sums[pl.ds(8 + at, 1), :]
        core_s[pl.ds(8 + at // 2, 1), pl.ds(at % 2 * WIDE, WIDE)] = bias_grad[pl.ds(at, 1), :]
    core_s[pl.ds(4, 4), :] = vec_sums[pl.ds(2, 4), :]
    packed = jnp.zeros((128, 128), jnp.float32)
    sums, olds = [], []
    old_cols = (col_mix, row_out, col_up, row_down)
    for m in range(4):
        block = jnp.zeros((128, 128), jnp.float32)
        old = jnp.zeros((1, LANES), jnp.float32)
        for t in TILES[m]:
            tile = tile_of(t)
            tile = tile * tile
            line_s[pl.ds(SUMS + t // 8, 1), lanes(t)] = jnp.sum(tile, 0, keepdims=True)
            block += tile
            old += col_of(old_cols, t)[...]
        per_row = jnp.sum(block, 1, keepdims=True)
        packed = jnp.where((lane >= 32 * m) & (lane < 32 * m + 32), per_row, packed)
        sums.append(jnp.sum(per_row, 0, keepdims=True))
        if m % 2 == 0:
            olds.append(jnp.sum((row_mix, None, row_up)[m][...], 1, keepdims=True) * 0.5)
        else:
            olds.append(jnp.sum(old, 1, keepdims=True) * 0.125)
    pack_s[...] = packed
    misc = sums + [squares[pl.ds(m, 1), 0:1] for m in range(4)] + olds + [jnp.zeros((1, 1), jnp.float32)] * 4
    for at, value in enumerate(misc):
        core_s[pl.ds(MISC + at // 8, 1), lanes(at)] = jnp.broadcast_to(value, (1, LANES))
    core_s[pl.ds(14, 2), :] = jnp.zeros((2, 1024), jnp.float32)
    hops = [
        remote(core_s, core_r, c_ss.at[0], c_rs.at[0], c_peer),
        remote(pack_s, pack_r, c_ss.at[1], c_rs.at[1], c_peer),
    ]
    for hop in hops:
        hop.start()
    for hop in hops:
        hop.wait()
    core_r[...] = core_r[...] + core_s[...]
    hop = remote(core_r, ctx_r, x_ss.at[0], x_rs.at[0], x_peer)
    hop.start()
    hop.wait()
    line_s[pl.ds(0, VECS), :] = core_r[pl.ds(0, VECS), :] + ctx_r[pl.ds(0, VECS), :]
    line_s[pl.ds(VECS, 2), :] = core_r[pl.ds(VECS, 2), :]
    line_s[pl.ds(20, 4), :] = jnp.zeros((4, 1024), jnp.float32)
    hops = [
        remote(line_s, line_r.at[z], z_ss.at[at], z_rs.at[at], peer) for at, peer in enumerate(line)
    ]
    for hop in hops:
        hop.start()
    line_r[pl.ds(z, 1)] = line_s[...][None]
    for hop in hops:
        hop.wait()
    line_s[...] = (line_r[0] + line_r[1]) + (line_r[2] + line_r[3])
    hop = remote(line_s, y_r, y_ss.at[0], y_rs.at[0], y_peer)
    hop.start()
    hop.wait()
    line_s[...] = line_s[...] + y_r[...]
    grads = line_s[pl.ds(0, VECS), :]
    vec_grad[...] = grads
    moment = decay_rate * moments[...] + (1.0 - decay_rate) * grads * grads
    vec_moment[...] = moment
    vec_step = grads * lax.rsqrt(moment)
    new_cols = (new_mix, new_out, new_up, new_down)
    for t in range(48):
        col_of(new_cols, t)[...] = decay_rate * col_of(old_cols, t)[...] + (1.0 - decay_rate) * (
            line_s[pl.ds(SUMS + t // 8, 1), lanes(t)] * (1.0 / 1024.0)
        )
    row_sum = pack_r[...] + pack_s[...]
    row_count = jnp.where(lane < 32, 1.0 / 3072.0, jnp.where(lane < 64, 1.0 / 1024.0, 1.0 / 4096.0))
    row_old = jnp.concatenate(
        [jnp.broadcast_to(one[...], (32, LANES)) for one in (row_mix, col_out, row_up, col_down)], 0
    ).T
    row_all = decay_rate * row_old + (1.0 - decay_rate) * row_sum * row_count
    row_new[...] = row_all
    row_flat[...] = row_all.T
    row_inverse = lax.rsqrt(row_all)
    row_lengths = (1024.0, 1024.0, 1024.0, 4096.0)
    square = jnp.zeros((1, 1), jnp.float32)
    factors = []
    for m in range(4):
        all_square, all_weight, all_old = (
            line_s[pl.ds(MISC + at // 8, 1), pl.ds(at % 8 * LANES, 1)] for at in (m, 4 + m, 8 + m)
        )
        average = decay_rate * all_old / row_lengths[m] + (1.0 - decay_rate) * all_square / SIZES[m]
        block = jnp.zeros((128, 128), jnp.float32)
        for t in TILES[m]:
            update = tile_of(t) * lax.rsqrt(col_of(new_cols, t)[...])
            block += update * update
        by_row = row_inverse[:, 32 * m : 32 * m + 1]
        per_row = jnp.sum(block, 1, keepdims=True) * by_row * by_row
        square += jnp.sum(per_row, 0, keepdims=True) * average
        factors.append((jnp.sqrt(average), jnp.sqrt(all_weight / SIZES[m])))
    spot = (z * 2 + y) * 2 + c
    last_s[...] = jnp.broadcast_to(square, (8, LANES))
    last_r[pl.ds(spot, 1)] = last_s[...][None]
    hops = [
        remote(last_s, last_r.at[spot], l_ss.at[at], l_rs.at[at], peer)
        for at, peer in enumerate(square_peers)
    ]
    for hop in hops:
        hop.start()
    for hop in hops:
        hop.wait()
    square = jnp.zeros((1, 1), jnp.float32)
    for at in range(16):
        square += last_r[at, 0:1, 0:1]
    vec_square = jnp.sum(jnp.sum(vec_step * vec_step, 1, keepdims=True), 0, keepdims=True)
    old_vecs = vecs[...]
    vec_size = VECS * 1024.0
    vec_mean = jnp.sum(jnp.sum(old_vecs * old_vecs, 1, keepdims=True), 0, keepdims=True) / vec_size
    count = sum(SIZES) + vec_size
    shrink = 1.0 / jnp.maximum(1.0, jnp.sqrt((square + vec_square) / count) / clip_level)
    vec_new[...] = old_vecs - step_rate * jnp.sqrt(vec_mean) * vec_step * shrink
    for m in range(4):
        scale[pl.ds(m, 1), :] = jnp.broadcast_to(
            step_rate * factors[m][0] * factors[m][1] * shrink, (1, LANES)
        )
    scale[pl.ds(4, 4), :] = jnp.zeros((4, LANES), jnp.float32)


def factor_all(*arrays):
    dma = pltpu.SemaphoreType.DMA
    full = jnp.float32
    in_vmem = pl.BlockSpec(memory_space=pltpu.VMEM)
    shape = jax.ShapeDtypeStruct
    shapes = [(128, 128), (128, 128), (3, WIDE), (4, LANES), (16, LANES), (16, LANES)]
    shapes += [(VECS, 1024)] * 3 + [(8, LANES)]
    return pl.pallas_call(
        factor_body,
        out_shape=tuple(shape(one, full) for one in shapes),
        in_specs=[in_vmem] * len(arrays),
        out_specs=(in_vmem,) * len(shapes),
        scratch_shapes=[
            pltpu.VMEM((16, 1024), full),
            pltpu.VMEM((16, 1024), full),
            pltpu.VMEM((128, 128), full),
            pltpu.VMEM((128, 128), full),
            pltpu.VMEM((16, 1024), full),
            pltpu.VMEM((24, 1024), full),
            pltpu.VMEM((4, 24, 1024), full),
            pltpu.VMEM((24, 1024), full),
            pltpu.VMEM((8, LANES), full),
            pltpu.VMEM((16, 8, LANES), full),
            dma((2,)), dma((2,)), dma((1,)), dma((1,)), dma((3,)), dma((3,)), dma((1,)), dma((1,)),
            dma((15,)), dma((15,)),
        ],
        compiler_params=pltpu.CompilerParams(
            collective_id=3, has_side_effects=True, vmem_limit_bytes=40 * MIB
        ),
    )(*arrays)


def finish_body(
    total_q, total_m, mix_w, out_w, up_w, down_w, row_new, row_flat, new_mix, new_out, new_up, new_down,
    vec_grad, vec_moment, vec_new, scale, *outs,
):
    grads, news, copies, smalls = outs[:4], outs[4:8], outs[8:12], outs[12:]
    at = pl.program_id(0)

    def by_row(m):
        return lax.rsqrt(row_new[:, 32 * m : 32 * m + 1])

    def by_col(row, m):
        return lax.rsqrt(row) * scale[pl.ds(m, 1), :]

    def put(m, index, grad, old, update):
        new = old - grad * update
        grads[m][index] = grad
        news[m][index] = new
        copies[m][index] = new.astype(jnp.bfloat16)

    everything = slice(None)
    for part in range(3):
        cols = new_mix[pl.ds(part, 1), columns(at * LANES, LANES)]
        grad = total_q[0, :, pl.ds(part * LANES, LANES)]
        put(0, (part, everything, everything), grad, mix_w[part], by_row(0) * by_col(cols, 0))
    turned_out = lax.rsqrt(row_flat[pl.ds(32, 1), :])
    turned_down = lax.rsqrt(row_flat[pl.ds(96, 1), :])
    cols = jnp.broadcast_to(by_col(new_out[pl.ds(at, 1), :], 1), (LANES, LANES)).T
    grad = total_q[0, :, pl.ds(3 * LANES, LANES)].T
    put(1, (everything, everything), grad, out_w[...], cols * turned_out)
    for part in range(4):
        here = pl.ds(part * LANES, LANES)
        row = pl.ds(at * 4 + part, 1)
        put(
            2, (everything, here), total_m[0, :, here], up_w[:, here],
            by_row(2) * by_col(new_up[row, :], 2),
        )
        cols = jnp.broadcast_to(by_col(new_down[row, :], 3), (LANES, LANES)).T
        put(3, (here, everything), total_m[1, :, here].T, down_w[here, :], cols * turned_down)
    for target, source in zip(smalls[:7], (vec_grad, vec_moment, vec_new, new_mix, new_out, new_up, new_down)):
        target[...] = source[...]
    for m, target in enumerate(smalls[7:]):
        target[...] = row_flat[pl.ds(32 * m, 1), :]


def finish_all(total_q, total_m, weights, factors):
    low, full = jnp.bfloat16, jnp.float32
    shape = jax.ShapeDtypeStruct
    blocks = [
        pl.BlockSpec((3, 128, LANES), lambda at: (0, 0, at)),
        pl.BlockSpec((LANES, 128), lambda at: (at, 0)),
        pl.BlockSpec((128, WIDE), lambda at: (0, at)),
        pl.BlockSpec((WIDE, 128), lambda at: (at, 0)),
    ]

    def whole(array_shape):
        return pl.BlockSpec(array_shape, lambda at: (0,) * len(array_shape))

    smalls = [(VECS, 1024)] * 3 + [(3, WIDE), (4, LANES), (16, LANES), (16, LANES)] + [(1, LANES)] * 4
    shapes = [shape(one.shape, kind) for kind in (full, full, low) for one in weights]
    shapes += [shape(one, full) for one in smalls]
    return pl.pallas_call(
        finish_body,
        grid=(4,),
        out_shape=tuple(shapes),
        in_specs=[
            pl.BlockSpec((1, 128, WIDE), lambda at: (at, 0, 0)),
            pl.BlockSpec((2, 128, WIDE), lambda at: (at, 0, 0)),
        ] + blocks + [whole(one.shape) for one in factors],
        out_specs=tuple(blocks * 3 + [whole(one) for one in smalls]),
        compiler_params=pltpu.CompilerParams(vmem_limit_bytes=40 * MIB),
    )(total_q, total_m, *weights, *factors)


def fast_body(
    inputs, cotangent, key_mask, image_mask, qkv_weight, out_weight, up_weight, down_weight,
    vectors, row_qkv, col_qkv, row_out, col_out, row_up, col_up, row_down, col_down, vector_moments,
):
    images, tokens, width = inputs.shape
    pad = ((0, 0), (0, SLOTS - tokens), (0, 0))
    weight_rows = (key_mask * image_mask[:, None]).astype(jnp.bfloat16)
    x_in = jnp.pad(inputs, pad)
    b_in = jnp.pad(cotangent * weight_rows[:, :, None], pad)
    counts = jnp.sum(key_mask, 1).astype(jnp.float32)
    n_in = jnp.broadcast_to(counts[:, None, None], (images, 8, LANES))
    weights = (qkv_weight.transpose(1, 0, 2), out_weight, up_weight, down_weight)
    w, made, b_all, x_all, n_all, qkv, heads, hidden, squares, grad_second, image, bias_grad = front_all(
        x_in, b_in, n_in, weights, vectors
    )
    total_m, total_q, out_spread, grad_spread, vec_sums, qv_sums = back_all(
        w, made, image, b_all.reshape(ROWS, width), x_all, hidden, grad_second, n_all, qkv, heads, vectors
    )
    factors = factor_all(
        total_q, total_m, squares, vec_sums, qv_sums, bias_grad, vectors, vector_moments,
        row_qkv.reshape(1, LANES), col_out.reshape(1, LANES), row_up.reshape(1, LANES),
        col_down.reshape(1, LANES), col_qkv, row_out.reshape(4, LANES), col_up.reshape(16, LANES),
        row_down.reshape(16, LANES),
    )
    done = finish_all(total_q, total_m, weights, factors)

    def natural(four):
        return (four[0].transpose(1, 0, 2),) + tuple(four[1:])

    vector_grad, vector_moment, vector_new, new_mix, new_out, new_up, new_down = done[12:19]
    rows = [one.reshape(-1) for one in done[19:]]
    return (
        (out_spread[:, :tokens], grad_spread[:, :tokens])
        + natural(done[:4])
        + (vector_grad,)
        + natural(done[4:8])
        + (vector_new,)
        + natural(done[8:12])
        + (
            rows[0], new_mix, new_out.reshape(-1), rows[1], rows[2], new_up.reshape(-1),
            new_down.reshape(-1), rows[3], vector_moment,
        )
    )


def pick_body(*arrays):
    sizes = tuple(lax.axis_size(name) for name in ("fsdp", "ctx", "tp"))
    if sizes == (8, 2, 2) and arrays[0].shape == (4, 290, 1024) and arrays[6].shape == (128, 2048):
        return fast_body(*arrays)
    return body(*arrays)


def solution(mesh):
    placed = (
        P("fsdp", "ctx", None),
        P("fsdp", "ctx", None),
        P("fsdp", "ctx"),
        P("fsdp"),
        P("fsdp", None, "tp"),
        P("tp", "fsdp"),
        P("fsdp", "tp"),
        P("tp", "fsdp"),
        P(),
        P("fsdp"),
        P(None, "tp"),
        P("tp"),
        P("fsdp"),
        P("fsdp"),
        P("tp"),
        P("tp"),
        P("fsdp"),
        P(),
    )
    return jax.shard_map(
        pick_body,
        mesh=mesh,
        in_specs=placed,
        out_specs=(
            P("fsdp", "ctx", None),
            P("fsdp", "ctx", None),
            P("fsdp", None, "tp"),
            P("tp", "fsdp"),
            P("fsdp", "tp"),
            P("tp", "fsdp"),
            P(),
            P("fsdp", None, "tp"),
            P("tp", "fsdp"),
            P("fsdp", "tp"),
            P("tp", "fsdp"),
            P(),
            P("fsdp", None, "tp"),
            P("tp", "fsdp"),
            P("fsdp", "tp"),
            P("tp", "fsdp"),
            P("fsdp"),
            P(None, "tp"),
            P("tp"),
            P("fsdp"),
            P("fsdp"),
            P("tp"),
            P("tp"),
            P("fsdp"),
            P(),
        ),
        check_vma=False,
    )
```
